32 devices in a mesh: dp: 8 (over z, x), ctx: 4 (over y, core).
Axes of the slice: x: 2, y: 2, z: 4, core: 2. Of those that a mesh axis runs over, the one named last changes fastest.
Arguments:
- tokens: bfloat16 [1024, 48, 512], P('ctx', 'dp'), may hold values from -9 to 9
- cotangent: bfloat16 [1024, 48, 512], P('ctx', 'dp'), may hold values from -5 to 5
- lengths: int32 [48], P('dp'), may hold values from 64 to 1024, as said below
- project_matrix: float32 [512, 1536], P(('dp', 'ctx')), may hold values from -0.25 to 0.25
- output_matrix: float32 [512, 512], P(('dp', 'ctx')), may hold values from -1.5 to 1.5
- expand_matrix: float32 [512, 2048], P(('dp', 'ctx')), may hold values from -0.25 to 0.25
- reduce_matrix: float32 [2048, 512], P(('dp', 'ctx')), may hold values from -0.125 to 0.125
- biases: float32 [2560], P(('dp', 'ctx')), may hold values from -1 to 1
- alphas: float32 [2], replicated, may hold values from 0.3 to 1
- project_first: float32 [512, 1536], P(('dp', 'ctx')), may hold values from -0.0009765625 to 0.0009765625
- project_second: float32 [512, 1536], P(('dp', 'ctx')), may hold values from 1.5881647e-10 to 2.5410636e-09
- output_first: float32 [512, 512], P(('dp', 'ctx')), may hold values from -0.0009765625 to 0.0009765625
- output_second: float32 [512, 512], P(('dp', 'ctx')), may hold values from 1.5881647e-11 to 2.5410635e-10
- expand_first: float32 [512, 2048], P(('dp', 'ctx')), may hold values from -0.0009765625 to 0.0009765625
- expand_second: float32 [512, 2048], P(('dp', 'ctx')), may hold values from 1.5881647e-10 to 2.5410636e-09
- reduce_first: float32 [2048, 512], P(('dp', 'ctx')), may hold values from -0.0009765625 to 0.0009765625
- reduce_second: float32 [2048, 512], P(('dp', 'ctx')), may hold values from 1.5881647e-10 to 2.5410636e-09
- bias_first: float32 [2560], P(('dp', 'ctx')), may hold values from -0.001953125 to 0.001953125
- bias_second: float32 [2560], P(('dp', 'ctx')), may hold values from 6.352659e-10 to 1.0164254e-08
- alpha_first: float32 [2], replicated, may hold values from -0.01953125 to 0.01953125
- alpha_second: float32 [2], replicated, may hold values from 8.1314035e-08 to 1.3010246e-06
Outputs:
- mixed: bfloat16 [1024, 48, 512], P('ctx', 'dp')
- input_grad: float32 [1024, 48, 512], P('ctx', 'dp')
- project_moment: float32 [512, 1536], P(('dp', 'ctx'))
- project_square: float32 [512, 1536], P(('dp', 'ctx'))
- project_master: float32 [512, 1536], P(('dp', 'ctx'))
- output_moment: float32 [512, 512], P(('dp', 'ctx'))
- output_square: float32 [512, 512], P(('dp', 'ctx'))
- output_master: float32 [512, 512], P(('dp', 'ctx'))
- expand_moment: float32 [512, 2048], P(('dp', 'ctx'))
- expand_square: float32 [512, 2048], P(('dp', 'ctx'))
- expand_master: float32 [512, 2048], P(('dp', 'ctx'))
- reduce_moment: float32 [2048, 512], P(('dp', 'ctx'))
- reduce_square: float32 [2048, 512], P(('dp', 'ctx'))
- reduce_master: float32 [2048, 512], P(('dp', 'ctx'))
- bias_moment: float32 [2560], P(('dp', 'ctx'))
- bias_square: float32 [2560], P(('dp', 'ctx'))
- bias_master: float32 [2560], P(('dp', 'ctx'))
- alpha_moment: float32 [2], replicated
- alpha_square: float32 [2], replicated
- alpha_master: float32 [2], replicated
- grad_norm: float32 [], replicated
The draws below stay inside these ranges and needn't reach their ends.
Inputs may be any that keep to these rules, and one draw needn't show every extreme that they name: `lengths`: of the 6 sequences of each index of dp, one has length 1024.
All inputs are finite; a program needn't handle non-finite values.
Results may differ from the reference program's by a relative error of at most 0.012.
The reference program's roundings to bfloat16 on the way count: a program that leaves them out, or rounds other values in their place, can miss the bound.
Values may be sent and summed in bfloat16 or wider, within the bound.
No kernel may reach another device: no remote copies, remote signals or barrier semaphores. Data moves between devices by JAX's collectives and lax.ppermute only.
A program may use at most 320 MiB of HBM per device.

```python
import math
import jax
import jax.numpy as jnp
from jax import lax

D = 512
HEADS = 8
HEAD = 64
FEED_UNITS = 2048
SLOTS = 1024
MIN_LEN = 64
SEQ_DEV = 6
STEP = 10
SEQS = 48
N_DP = 8
N_CTX = 4


def draw_tokens(key, part):
    key = jax.random.fold_in(key, 7)
    column = jnp.arange(D, dtype=jnp.int32)
    owner = column * (N_DP * N_CTX) // D
    inner = (owner % N_CTX).astype(jnp.float32) / max(N_CTX - 1, 1)
    outer = (owner // N_CTX).astype(jnp.float32) / max(N_DP - 1, 1)
    rise = 0.5 * inner + 0.5 * outer
    values = jnp.clip(jax.random.normal(key, (SLOTS, SEQS, D), jnp.float32), -4.0, 4.0)
    scale = 3.0 ** (rise - 0.5)
    return (values * scale[None, None, :]).astype(jnp.bfloat16)


def draw_lengths(key, part):
    key = jax.random.fold_in(key, 11)
    first_key, second_key = jax.random.split(key)
    groups = SEQS // SEQ_DEV
    owner = jnp.arange(SEQS, dtype=jnp.int32) // SEQ_DEV
    upper = SLOTS // 3 + (SLOTS - SLOTS // 3) * owner // max(groups - 1, 1)
    upper = jnp.maximum(upper, MIN_LEN)
    raw = jax.random.randint(first_key, (SEQS,), 0, 2 ** 30, dtype=jnp.int32)
    lens = MIN_LEN + raw % (upper - MIN_LEN + 1)
    chosen = jax.random.randint(second_key, (groups,), 0, SEQ_DEV, dtype=jnp.int32)
    picked = jnp.arange(SEQS, dtype=jnp.int32) % SEQ_DEV == chosen[owner]
    return jnp.where(picked, SLOTS, lens).astype(jnp.int32)


def steps_of(rng, shape, cuts, smallest, top_value):
    level, own = 1.0, jax.random.fold_in(rng, 6)
    for dim, blocks in cuts:
        draws = jnp.exp(jax.random.uniform(jax.random.fold_in(own, dim), (blocks,), jnp.float32, smallest / len(cuts), top_value / len(cuts)))
        level = level * jnp.repeat(draws, shape[dim] // blocks).reshape([-1 if axis == dim else 1 for axis in range(len(shape))])
    return level


def centred(rng, shape, spread, limit, cuts=(), kind=jnp.bfloat16):
    entries = spread * jax.random.normal(rng, shape, jnp.float32)
    if cuts:
        entries = entries * steps_of(rng, shape, cuts, -0.22, 0.18)
    return jnp.clip(entries, -limit, limit).astype(kind)


def setup_inputs(seed: int = 0) -> dict:
    key_of = jax.random.split(jax.random.key(seed), 22)
    tokens = draw_tokens(jax.random.fold_in(key_of[21], 71), 0)
    cotangent = centred(key_of[1], (SLOTS, SEQS, D), 1.0, 5.0, ((0, 4), (1, 8)))
    lengths = draw_lengths(jax.random.fold_in(key_of[21], 71), 0)
    project_matrix = centred(key_of[3], (D, 3 * D), D ** -0.5, 0.25, ((0, 32),), jnp.float32)
    output_matrix = centred(key_of[4], (D, D), (D // 32) ** -0.5, 1.5, ((0, 32),), jnp.float32)
    expand_matrix = centred(key_of[5], (D, FEED_UNITS), D ** -0.5, 0.25, ((0, 32),), jnp.float32)
    reduce_matrix = centred(key_of[6], (FEED_UNITS, D), FEED_UNITS ** -0.5, 0.125, ((0, 32),), jnp.float32)
    biases = centred(key_of[7], (FEED_UNITS + D,), 0.25, 1.0, ((0, 32),), jnp.float32)
    alphas = jnp.clip(jnp.exp(jax.random.uniform(key_of[8], (2,), jnp.float32, math.log(0.3), math.log(1.0))), 0.3, 1.0)
    project_first = centred(key_of[9], (D, 3 * D), (0.111 * (4 * D * D + 2 * D * FEED_UNITS + FEED_UNITS + D) ** -0.5), 0.0009765625, ((0, 32),), jnp.float32)
    project_second = jnp.clip(jnp.exp(math.log(2.5410635817735283e-09) - 2.7725887 * jax.random.uniform(key_of[10], (D, 3 * D), jnp.float32) ** steps_of(key_of[10], (D, 3 * D), ((0, 32),), -0.2, 0.2)), 1.5881647386084552e-10, 2.5410635817735283e-09)
    output_first = centred(key_of[11], (D, D), (0.111 * (4 * D * D + 2 * D * FEED_UNITS + FEED_UNITS + D) ** -0.5), 0.0009765625, ((0, 32),), jnp.float32)
    output_second = jnp.clip(jnp.exp(math.log(2.541063470751226e-10) - 2.7725887 * jax.random.uniform(key_of[12], (D, D), jnp.float32) ** steps_of(key_of[12], (D, D), ((0, 32),), -0.2, 0.2)), 1.588164669219516e-11, 2.541063470751226e-10)
    expand_first = centred(key_of[13], (D, FEED_UNITS), (0.111 * (4 * D * D + 2 * D * FEED_UNITS + FEED_UNITS + D) ** -0.5), 0.0009765625, ((0, 32),), jnp.float32)
    expand_second = jnp.clip(jnp.exp(math.log(2.5410635817735283e-09) - 2.7725887 * jax.random.uniform(key_of[14], (D, FEED_UNITS), jnp.float32) ** steps_of(key_of[14], (D, FEED_UNITS), ((0, 32),), -0.2, 0.2)), 1.5881647386084552e-10, 2.5410635817735283e-09)
    reduce_first = centred(key_of[15], (FEED_UNITS, D), (0.111 * (4 * D * D + 2 * D * FEED_UNITS + FEED_UNITS + D) ** -0.5), 0.0009765625, ((0, 32),), jnp.float32)
    reduce_second = jnp.clip(jnp.exp(math.log(2.5410635817735283e-09) - 2.7725887 * jax.random.uniform(key_of[16], (FEED_UNITS, D), jnp.float32) ** steps_of(key_of[16], (FEED_UNITS, D), ((0, 32),), -0.2, 0.2)), 1.5881647386084552e-10, 2.5410635817735283e-09)
    bias_first = centred(key_of[17], (FEED_UNITS + D,), (0.222 * (4 * D * D + 2 * D * FEED_UNITS + FEED_UNITS + D) ** -0.5), 0.001953125, ((0, 32),), jnp.float32)
    bias_second = jnp.clip(jnp.exp(math.log(1.0164254327094113e-08) - 2.7725887 * jax.random.uniform(key_of[18], (FEED_UNITS + D,), jnp.float32) ** steps_of(key_of[18], (FEED_UNITS + D,), ((0, 32),), -0.2, 0.2)), 6.352658954433821e-10, 1.0164254327094113e-08)
    alpha_first = centred(key_of[19], (2,), (0.111 * D ** 0.5 * (4 * D * D + 2 * D * FEED_UNITS + FEED_UNITS + D) ** -0.5), 0.01953125, (), jnp.float32)
    alpha_second = jnp.clip(jnp.exp(jax.random.uniform(key_of[20], (2,), jnp.float32, math.log(8.13140346167529e-08), math.log(1.3010245538680465e-06))), 8.13140346167529e-08, 1.3010245538680465e-06)
    return {"tokens": tokens, "cotangent": cotangent, "lengths": lengths, "project_matrix": project_matrix, "output_matrix": output_matrix, "expand_matrix": expand_matrix, "reduce_matrix": reduce_matrix, "biases": biases, "alphas": alphas, "project_first": project_first, "project_second": project_second, "output_first": output_first, "output_second": output_second, "expand_first": expand_first, "expand_second": expand_second, "reduce_first": reduce_first, "reduce_second": reduce_second, "bias_first": bias_first, "bias_second": bias_second, "alpha_first": alpha_first, "alpha_second": alpha_second}


clip_bound = 1.0
beta_one = 0.9
beta_two = 0.999
adam_eps = 1e-08
matrix_rate = 0.05
alpha_rate = 0.2
decay_rate = 0.1

@jax.custom_vjp
def narrow_copy(v):
    return lax.optimization_barrier(v.astype(jnp.bfloat16)).astype(jnp.float32)

@jax.custom_vjp
def narrow_backward(v):
    return v

def low_keep(v):
    return (narrow_copy(v), None)

def low_pass(kept, grad):
    return (grad,)

def back_keep(v):
    return (v, None)

def back_low(kept, grad):
    return (narrow_copy(grad),)
narrow_copy.defvjp(low_keep, low_pass)
narrow_backward.defvjp(back_keep, back_low)

def matrix_product(form, left, right):
    return jnp.einsum(form, left, right, precision=lax.Precision.HIGHEST)

def layer(input_grouping, lens, project_matrix, output_matrix, expand_matrix, reduce_matrix, biases, alphas):
    count = input_grouping.shape[0]
    query_key_value = narrow_backward(narrow_copy(matrix_product('nvp,pg->nvg', input_grouping, narrow_copy(project_matrix))))
    query = query_key_value[..., :D].reshape(count, SLOTS, HEADS, HEAD)
    keys = query_key_value[..., D:2 * D].reshape(count, SLOTS, HEADS, HEAD)
    values = query_key_value[..., 2 * D:].reshape(count, SLOTS, HEADS, HEAD)
    block = min(512, SLOTS)
    kpos = jnp.arange(SLOTS, dtype=jnp.int32)

    def attend(start):
        qblock = lax.dynamic_slice_in_dim(query, start, block, 1)
        scores = matrix_product('sqhe,skhe->shqk', qblock, keys) * HEAD ** (-0.5)
        scores = narrow_backward(scores)
        qpos = start + jnp.arange(block, dtype=jnp.int32)
        allowed = (kpos[None, None, :] <= qpos[None, :, None]) & (kpos[None, None, :] < lens[:, None, None])
        probs = jax.nn.softmax(jnp.where(allowed[:, None], scores, -1e+30), axis=-1)
        return matrix_product('shqk,skhe->sqhe', narrow_copy(probs), values)
    starts = jnp.arange(SLOTS // block, dtype=jnp.int32) * block
    pieces = lax.map(jax.checkpoint(attend), starts)
    attended_rows = jnp.moveaxis(pieces, 0, 1).reshape(count, SLOTS, D)
    attended_rows = narrow_backward(narrow_copy(attended_rows))
    branch_output = narrow_backward(matrix_product('nvp,pg->nvg', attended_rows, narrow_copy(output_matrix)))
    residual_stream = input_grouping + alphas[0] * branch_output
    bias_narrow = narrow_copy(biases)
    before_activation = narrow_backward(matrix_product('vth,ha->vta', narrow_copy(residual_stream), narrow_copy(expand_matrix)) + bias_narrow[:FEED_UNITS])
    hidden_rows = narrow_copy(jax.nn.gelu(before_activation, approximate=False))
    feed_output = narrow_backward(matrix_product('qjy,yn->qjn', hidden_rows, narrow_copy(reduce_matrix)) + bias_narrow[FEED_UNITS:])
    return residual_stream + alphas[1] * feed_output

def adamw(weight, first, second, grad, rate, decay):
    first = beta_one * first + (1.0 - beta_one) * grad
    second = beta_two * second + (1.0 - beta_two) * grad * grad
    mhat = first / (1.0 - beta_one ** STEP)
    vhat = second / (1.0 - beta_two ** STEP)
    weight = weight - rate * (mhat / (jnp.sqrt(vhat) + adam_eps) + decay * weight)
    return (first, second, weight)

def reference(tokens, cotangent, lengths, project_matrix, output_matrix, expand_matrix, reduce_matrix, biases, alphas, project_first, project_second, output_first, output_second, expand_first, expand_second, reduce_first, reduce_second, bias_first, bias_second, alpha_first, alpha_second):
    group = math.gcd(SEQS, max(1, 4096 // SLOTS))
    groups = SEQS // group
    valid = (jnp.arange(SLOTS, dtype=jnp.int32)[:, None] < lengths[None, :]).astype(jnp.float32)
    pull = cotangent.astype(jnp.float32) * valid[:, :, None]
    xs = jnp.transpose(tokens.astype(jnp.float32).reshape(SLOTS, groups, group, D), (1, 2, 0, 3))
    cs = jnp.transpose(pull.reshape(SLOTS, groups, group, D), (1, 2, 0, 3))
    ls = lengths.reshape(groups, group)
    params = (project_matrix, output_matrix, expand_matrix, reduce_matrix, biases, alphas)

    def step(total, item):
        input_grouping, cgroup, lgroup = item
        result, back = jax.vjp(lambda xx, *ps: layer(xx, lgroup, *ps), input_grouping, *params)
        grads = back(cgroup)
        total = jax.tree.map(lambda a, b: a + b, total, tuple(grads[1:]))
        return (total, (result, grads[0]))
    zeros = jax.tree.map(jnp.zeros_like, params)
    totals, (outs, dxs) = lax.scan(step, zeros, (xs, cs, ls))
    mixed = jnp.transpose(outs, (2, 0, 1, 3)).reshape(SLOTS, SEQS, D).astype(jnp.bfloat16)
    input_grad = jnp.transpose(dxs, (2, 0, 1, 3)).reshape(SLOTS, SEQS, D)
    squares = jnp.float32(0.0)
    for grad in totals:
        squares = squares + jnp.sum(grad * grad)
    grad_norm = jnp.sqrt(squares)
    factor = jnp.minimum(1.0, clip_bound / (grad_norm + 1e-06))
    states = ((project_first, project_second), (output_first, output_second), (expand_first, expand_second), (reduce_first, reduce_second), (bias_first, bias_second), (alpha_first, alpha_second))
    rates = (matrix_rate, matrix_rate, matrix_rate, matrix_rate, matrix_rate, alpha_rate)
    decays = (decay_rate, decay_rate, decay_rate, decay_rate, 0.0, 0.0)
    results = []
    for weight, (first, second), grad, rate, decay in zip(params, states, totals, rates, decays):
        results.extend(adamw(weight, first, second, factor * grad, rate, decay))
    return (mixed, input_grad, results[0], results[1], results[2], results[3], results[4], results[5], results[6], results[7], results[8], results[9], results[10], results[11], results[12], results[13], results[14], results[15], results[16], results[17], grad_norm)
```

```python
from functools import partial

import jax
import jax.numpy as jnp
from jax import lax
from jax.experimental import pallas as pl
from jax.experimental.pallas import tpu as pltpu
from jax.sharding import PartitionSpec as P

HEADS = 8
HEAD = 64
STEP = 10


clip_bound = 1.0
beta_one = 0.9
beta_two = 0.999
adam_eps = 1e-08
matrix_rate = 0.05
alpha_rate = 0.2
decay_rate = 0.1

BOTH = ("dp", "ctx")
F32 = jnp.float32
BF16 = jnp.bfloat16
VMEM_LIMIT = 56 * 1024 * 1024


def adamw(weight, first, second, grad, rate, decay):
    first = beta_one * first + (1.0 - beta_one) * grad
    second = beta_two * second + (1.0 - beta_two) * grad * grad
    mhat = first / (1.0 - beta_one**STEP)
    vhat = second / (1.0 - beta_two**STEP)
    weight = weight - rate * (mhat / (jnp.sqrt(vhat) + adam_eps) + decay * weight)
    return (first, second, weight)


def dot_nn(a, b):
    return lax.dot_general(a, b, (((1,), (0,)), ((), ())), preferred_element_type=F32)


def dot_nt(a, b):
    return lax.dot_general(a, b, (((1,), (1,)), ((), ())), preferred_element_type=F32)


def dot_tn(a, b):
    return lax.dot_general(a, b, (((0,), (0,)), ((), ())), preferred_element_type=F32)


CORE, CHIP_Y, CHIP_Z, CHIP_X, LENS = 0, 1, 2, 3, 4


def block_places(info, rows):
    core, y = info[CORE], info[CHIP_Y]
    return [
        pl.multiple_of(b * rows, rows)
        for b in (
            2 * y + core,
            2 * (1 - y) + core,
            2 * y + 1 - core,
            2 * (1 - y) + 1 - core,
        )
    ]


def chip_index(info, r, fx, fy):
    z = info[CHIP_Z] ^ r
    x = info[CHIP_X] ^ fx
    y = info[CHIP_Y] ^ fy
    return (z * 2 + x) * 2 + y


def gathered_pieces(nz):
    half = nz // 2
    out = [(0, r, r, 0, 0) for r in range(nz)]
    out += [(1, r, r, 1, 0) for r in range(nz)]
    out += [(2, r, r, 0, 1) for r in range(nz)]
    out += [(3, r, r, 1, 1) for r in range(half)]
    out += [(4, r, r + half, 1, 1) for r in range(nz - half)]
    return out


def attend_forward(assemble, nz, info, *refs):
    refs = list(refs)
    x_refs = [refs.pop(0) for _ in range(4)]
    if assemble:
        pieces = [refs.pop(0) for _ in range(5)]
        wq_ref, qkv_ref, ok_ref, os_ref, lse_ref, o_s, st_s = refs
        rows = pieces[0].shape[1]
        for which, at, r, fx, fy in gathered_pieces(nz):
            place = pl.multiple_of(chip_index(info, r, fx, fy) * rows, rows)
            wq_ref[pl.ds(place, rows), :] = pieces[which][at]
    else:
        wq_ref, qkv_ref, ok_ref, os_ref, lse_ref, o_s, st_s = refs
    sub = info.shape[0] - 1
    length = info[sub]
    rows = x_refs[0].shape[1]
    places = block_places(info, rows)
    w = wq_ref[...]
    for x_ref, place in zip(x_refs, places):
        qkv_ref[0, pl.ds(place, rows), :] = dot_nn(x_ref[0], w).astype(BF16)
    blocks = (length + rows - 1) // rows
    lane = lax.broadcasted_iota(jnp.int32, (rows, 128), 1)
    low_lane = lane < HEAD
    row_i = lax.broadcasted_iota(jnp.int32, (rows, rows), 0)
    col_i = lax.broadcasted_iota(jnp.int32, (rows, rows), 1)

    def one(qb, n, pair):
        at = pair * 128
        wide = 256
        q = qkv_ref[0, qb * rows : (qb + 1) * rows, pl.ds(at, 128)]
        k = qkv_ref[0, 0 : n * rows, pl.ds(wide + at, 128)]
        v = qkv_ref[0, 0 : n * rows, pl.ds(2 * wide + at, 128)]
        vx = jnp.concatenate([v, jnp.ones_like(v)], axis=1)
        base = (n - 1) * rows
        ok = (base + col_i) < length
        if n == qb + 1:
            ok = ok & (col_i <= row_i)
        res = []
        stats = st_s[qb * rows : (qb + 1) * rows, :]
        for h in range(2):
            mine = low_lane if h == 0 else jnp.logical_not(low_lane)
            qm = jnp.where(mine, q * jnp.asarray(HEAD**-0.5, BF16), jnp.zeros_like(q))
            s = dot_nt(qm, k)
            last = jnp.where(ok, s[:, base:], -1e30)
            if n > 1:
                s = jnp.concatenate([s[:, :base], last], axis=1)
            else:
                s = last
            top = jnp.max(s, axis=1, keepdims=True)
            e = jnp.exp(s - top)
            ob = dot_nn(e.astype(BF16), vx)
            den = ob[:, 128:]
            res.append(ob[:, :128] / den)
            stats = jnp.where(lane == 2 * pair + h, top + jnp.log(den), stats)
        st_s[qb * rows : (qb + 1) * rows, :] = stats
        o_s[qb * rows : (qb + 1) * rows, pl.ds(at, 128)] = jnp.where(
            low_lane, res[0], res[1]
        ).astype(BF16)

    total = qkv_ref.shape[1] // rows
    st_s[...] = jnp.zeros_like(st_s)
    for qb in range(total):
        for n in range(1, qb + 2):
            cond = (blocks == n) if n < qb + 1 else (blocks >= n)

            @pl.when(cond)
            def _(qb=qb, n=n):
                for pair in range(2):
                    one(qb, n, pair)

    for b in range(2):
        ok_ref[0, b] = o_s[pl.ds(places[b], rows), :]
        os_ref[0, b] = o_s[pl.ds(places[2 + b], rows), :]
    lse_ref[0] = jnp.transpose(st_s[...])[:8]


def attend_backward(first, info, *refs):
    refs = list(refs)
    x_refs = [refs.pop(0) for _ in range(4)]
    if first:
        (wq_ref, qkv_ref, lse_ref, ok_ref, os_ref, dk_ref, dr_ref, dy_ref,
         g_ref, keep_ref, send_ref, do_s, r_s, dq_s, dk_s, dv_s) = refs
        g_in = None
    else:
        (wq_ref, qkv_ref, lse_ref, ok_ref, os_ref, dk_ref, dr_ref, dy_ref, g_in,
         g_ref, keep_ref, send_ref, do_s, r_s, dq_s, dk_s, dv_s) = refs
    sub = info.shape[0] - 1
    length = info[sub]
    rows = x_refs[0].shape[1]
    places = block_places(info, rows)
    lane = lax.broadcasted_iota(jnp.int32, (rows, 128), 1)
    low_lane = lane < HEAD
    head_of = lax.broadcasted_iota(jnp.int32, (8, 256), 1) // HEAD
    pick = (head_of == lax.broadcasted_iota(jnp.int32, (8, 256), 0)).astype(F32)
    for b in range(4):
        do = (dk_ref if b < 2 else dr_ref)[0, b % 2]
        o = (ok_ref if b < 2 else os_ref)[0, b % 2]
        do_s[pl.ds(places[b], rows), :] = do
        prod = do.astype(F32) * o.astype(F32)
        r_s[:, pl.ds(places[b], rows)] = lax.dot_general(
            pick, prod, (((1,), (1,)), ((), ())),
            preferred_element_type=F32, precision=lax.Precision.HIGHEST)
    dk_s[...] = jnp.zeros_like(dk_s)
    dv_s[...] = jnp.zeros_like(dv_s)
    if first:
        g_ref[...] = jnp.zeros_like(g_ref)
    else:
        g_ref[...] = g_in[...]
    key_i = lax.broadcasted_iota(jnp.int32, (rows, rows), 0)
    qry_i = lax.broadcasted_iota(jnp.int32, (rows, rows), 1)
    scale = HEAD**-0.5

    def one(qb, pair):
        n = qb + 1
        at = pair * 128
        wide = 256
        span = slice(qb * rows, (qb + 1) * rows)
        q = qkv_ref[0, span, pl.ds(at, 128)]
        k = qkv_ref[0, 0 : n * rows, pl.ds(wide + at, 128)]
        v = qkv_ref[0, 0 : n * rows, pl.ds(2 * wide + at, 128)]
        do = do_s[span, pl.ds(at, 128)]
        base = qb * rows
        ok = (key_i <= qry_i) & ((base + key_i) < length)
        dqs = []
        dv = dk = None
        for h in range(2):
            head = 2 * pair + h
            mine = low_lane if h == 0 else jnp.logical_not(low_lane)
            qm = jnp.where(mine, q * jnp.asarray(scale, BF16), jnp.zeros_like(q))
            dom = jnp.where(mine, do, jnp.zeros_like(do))
            s = dot_nt(k, qm)
            p = jnp.exp(s - lse_ref[0, head : head + 1, span])
            last = jnp.where(ok, p[base:], 0.0)
            p = jnp.concatenate([p[:base], last], axis=0) if n > 1 else last
            dp = dot_nt(v, dom)
            ds = (p * (dp - r_s[head : head + 1, span])).astype(BF16)
            dvh = dot_nn(p.astype(BF16), dom)
            dkh = dot_nn(ds, qm)
            dv = dvh if dv is None else dv + dvh
            dk = dkh if dk is None else dk + dkh
            dqs.append(dot_tn(ds, k))
        dv_s[0 : n * rows, pl.ds(at, 128)] += dv
        dk_s[0 : n * rows, pl.ds(at, 128)] += dk
        dq_s[span, pl.ds(at, 128)] = (jnp.where(low_lane, dqs[0], dqs[1]) * scale).astype(BF16)

    total = qkv_ref.shape[1] // rows
    for qb in range(total):

        @pl.when(qb * rows < length)
        def _(qb=qb):
            for pair in range(2):
                one(qb, pair)

    w = wq_ref[...]
    for b in range(4):
        place = places[b]
        here = pl.ds(place, rows)

        @pl.when(place < length)
        def _(b=b, here=here):
            d = jnp.concatenate(
                [dq_s[here, :], dk_s[here, :].astype(BF16), dv_s[here, :].astype(BF16)], axis=1
            )
            g_ref[...] += dot_tn(x_refs[b][0], d)
            dx = dot_nt(d, w)
            if b < 2:
                keep_ref[0, b] = dy_ref[0, b] + dx
            else:
                send_ref[0, b - 2] = dx.astype(BF16)

        @pl.when(place >= length)
        def _(b=b):
            if b < 2:
                keep_ref[0, b] = jnp.zeros_like(keep_ref[0, b])
            else:
                send_ref[0, b - 2] = jnp.zeros_like(send_ref[0, b - 2])


def feed(nz, info, alphas, *refs):
    refs = list(refs)
    xm, xg, cm, cg = (refs.pop(0) for _ in range(4))
    seqs = xm.shape[0] if False else 3
    own_o = [refs.pop(0) for _ in range(seqs)]
    oth_o = [refs.pop(0) for _ in range(seqs)]
    rails = [[refs.pop(0) for _ in range(5)] for _ in range(2)]
    (mixm, mixg, dy_ref, dkeep, dsend, gsend, gkeep, ga_ref,
     wo_s, w1_s, w2_s, b_s, go_s, g1_s, g2_s, gb1_s, gb2_s, ga_s,
     h_s, gp_s, dpre_s) = refs
    step = pl.program_id(0)
    s, b = step // 2, step % 2
    core = info[CORE]
    chips = nz * 4
    width = wo_s.shape[1]
    groups = w1_s.shape[1] // width
    r1 = wo_s.shape[0] // (2 * chips)
    r2 = w2_s.shape[0] // (2 * chips)

    @pl.when(step == 0)
    def _():
        bias = None
        for rail in range(2):
            for which, at, r, fx, fy in gathered_pieces(nz):
                d = chip_index(info, r, fx, fy) * 2 + (core ^ rail)
                piece = rails[rail][which]
                small = pl.ds(pl.multiple_of(d * r1, r1), r1)
                wo_s[small, :] = piece[at, 0:r1]
                for j in range(groups):
                    w1_s[small, j * width : (j + 1) * width] = piece[at, (1 + j) * r1 : (2 + j) * r1]
                first = (1 + groups) * r1
                w2_s[pl.ds(pl.multiple_of(d * r2, r2), r2), :] = piece[at, first : first + r2]
                part = piece[at, first + r2 : first + r2 + 16].astype(F32)
                bias = part if bias is None else bias + part
        b_s[...] = bias
        for ref in (go_s, g1_s, g2_s, gb1_s, gb2_s, ga_s):
            ref[...] = jnp.zeros_like(ref)

    rows = xm.shape[1]
    block = jnp.where(b == 0, 2 * info[CHIP_Y] + core, 2 * (1 - info[CHIP_Y]) + core)
    length = info[LENS + s]
    begin = block * rows

    def pick3(three):
        return jnp.where(s == 0, three[0][0, b], jnp.where(s == 1, three[1][0, b], three[2][0, b]))

    o_own = pick3(own_o)
    o_oth = pick3(oth_o)
    here = pl.ds(pl.multiple_of(core * 256, 256), 256)
    there = pl.ds(pl.multiple_of((1 - core) * 256, 256), 256)
    a0, a1 = alphas[0], alphas[1]
    x = jnp.where(b == 0, xm[0], xg[0]).astype(F32)
    branch = dot_nn(o_own, wo_s[here, :]) + dot_nn(o_oth, wo_s[there, :])
    y = x + a0 * branch
    yb = y.astype(BF16)
    f = None
    for j in range(groups):
        cols = slice(j * width, (j + 1) * width)
        pre = dot_nn(yb, w1_s[:, cols]) + b_s[j : j + 1, :]
        cdf = 0.5 + 0.5 * lax.erf(pre * (0.5**0.5))
        h = (pre * cdf).astype(BF16)
        h_s[:, cols] = h
        gp_s[:, cols] = cdf + pre * (jnp.exp(-0.5 * pre * pre) * 0.3989422804014327)
        part = dot_nn(h, w2_s[cols, :])
        f = part if f is None else f + part
    f = f + b_s[groups : groups + 1, :]
    mixed = (y + a1 * f).astype(BF16)

    @pl.when(b == 0)
    def _():
        mixm[0] = mixed

    @pl.when(b == 1)
    def _():
        mixg[0] = mixed

    @pl.when(begin < length)
    def _():
        row = lax.broadcasted_iota(jnp.int32, (rows, width), 0)
        cot = jnp.where(b == 0, cm[0], cg[0]).astype(F32)
        g = jnp.where(begin + row < length, cot, 0.0)
        df = (a1 * g).astype(BF16)
        gb2_s[...] += jnp.sum(df.astype(F32).reshape(rows // 8, 8, width), axis=0)
        dy = g
        for j in range(groups):
            cols = slice(j * width, (j + 1) * width)
            dh = dot_nt(df, w2_s[cols, :])
            dpre_f = dh * gp_s[:, cols]
            dpre = dpre_f.astype(BF16)
            gb1_s[:, cols] += jnp.sum(dpre.astype(F32).reshape(rows // 8, 8, width), axis=0)
            g2_s[cols, :] += dot_tn(h_s[:, cols], df)
            g1_s[:, cols] += dot_tn(yb, dpre)
            dy = dy + dot_nt(dpre, w1_s[:, cols])
        ga_s[0:8, :] += jnp.sum((branch * dy).reshape(rows // 8, 8, width), axis=0)
        ga_s[8:16, :] += jnp.sum((f * g).reshape(rows // 8, 8, width), axis=0)
        db = (a0 * dy).astype(BF16)
        go_s[here, :] += dot_tn(o_own, db)
        go_s[there, :] += dot_tn(o_oth, db)
        dkeep[0, 0] = dot_nt(db, wo_s[here, :]).astype(BF16)
        dsend[0, 0] = dot_nt(db, wo_s[there, :]).astype(BF16)
        dy_ref[0, 0] = dy

    @pl.when(begin >= length)
    def _():
        dkeep[...] = jnp.zeros_like(dkeep)
        dsend[...] = jnp.zeros_like(dsend)
        dy_ref[...] = jnp.zeros_like(dy_ref)

    @pl.when(step == pl.num_programs(0) - 1)
    def _():
        first = (1 + groups) * r1
        gb = jnp.concatenate(
            [jnp.sum(gb1_s[:, j * width : (j + 1) * width], axis=0, keepdims=True) for j in range(groups)]
            + [jnp.sum(gb2_s[...], axis=0, keepdims=True), jnp.zeros((16 - groups - 1, width), F32)],
            axis=0,
        ).astype(BF16)
        for out, whose in ((gkeep, core), (gsend, 1 - core)):
            for chip in range(chips):
                d = chip * 2 + whose
                small = pl.ds(pl.multiple_of(d * r1, r1), r1)
                out[chip, 0:r1] = go_s[small, :].astype(BF16)
                for j in range(groups):
                    out[chip, (1 + j) * r1 : (2 + j) * r1] = g1_s[
                        small, j * width : (j + 1) * width
                    ].astype(BF16)
                out[chip, first : first + r2] = g2_s[
                    pl.ds(pl.multiple_of(d * r2, r2), r2), :
                ].astype(BF16)
                out[chip, first + r2 : first + r2 + 16] = gb
        ga_ref[0:1, :] = jnp.sum(ga_s[0:8, :], axis=0, keepdims=True)
        ga_ref[1:2, :] = jnp.sum(ga_s[8:16, :], axis=0, keepdims=True)


def whole(shape):
    return pl.BlockSpec(shape, lambda *_: (0,) * len(shape))


SMEM = pl.BlockSpec(memory_space=pltpu.SMEM)


def routes(nz):
    def perm(to):
        out = []
        for z in range(nz):
            for x in range(2):
                for y in range(2):
                    for c in range(2):
                        z2, x2, y2, c2 = to(z, x, y, c)
                        out.append((((z * 2 + x) * 4 + y * 2 + c), ((z2 * 2 + x2) * 4 + y2 * 2 + c2)))
        return out

    table = {
        "core": perm(lambda z, x, y, c: (z, x, y, 1 - c)),
        "y": perm(lambda z, x, y, c: (z, x, 1 - y, c)),
        "x": perm(lambda z, x, y, c: (z, 1 - x, y, c)),
    }
    for r in range(1, nz):
        table[r] = perm(lambda z, x, y, c, r=r: (z ^ r, x, y, c))
    return table


def generic_body(
    tokens,
    cotangent,
    lengths,
    project_matrix,
    output_matrix,
    expand_matrix,
    reduce_matrix,
    biases,
    alphas,
    project_first,
    project_second,
    output_first,
    output_second,
    expand_first,
    expand_second,
    reduce_first,
    reduce_second,
    bias_first,
    bias_second,
    alpha_first,
    alpha_second,
):
    slot_dev, seq_dev, width = tokens.shape
    ctx_index = lax.axis_index("ctx")
    qpos = ctx_index * slot_dev + jnp.arange(slot_dev, dtype=jnp.int32)
    gathered = (
        lax.all_gather(project_matrix.astype(jnp.bfloat16), ("dp", "ctx"), axis=0, tiled=True),
        lax.all_gather(output_matrix.astype(jnp.bfloat16), ("dp", "ctx"), axis=0, tiled=True),
        lax.all_gather(expand_matrix.astype(jnp.bfloat16), ("dp", "ctx"), axis=0, tiled=True),
        lax.all_gather(reduce_matrix.astype(jnp.bfloat16), ("dp", "ctx"), axis=0, tiled=True),
        lax.all_gather(biases.astype(jnp.bfloat16), ("dp", "ctx"), axis=0, tiled=True),
    )
    w_project, w_output, w_expand, w_reduce, bias_all = gathered
    hidden_width = w_expand.shape[1]
    scale = HEAD ** (-0.5)
    flat = tokens.reshape(-1, width)
    query_key_value = jnp.dot(flat, w_project, preferred_element_type=jnp.float32).astype(
        jnp.bfloat16
    )
    query_key_value = query_key_value.reshape(slot_dev, seq_dev, 3 * width)
    query = query_key_value[..., :width].reshape(slot_dev, seq_dev, HEADS, HEAD)
    kv_all = lax.all_gather(query_key_value[..., width:], "ctx", axis=0, tiled=True)
    length = kv_all.shape[0]
    keys = kv_all[..., :width].reshape(length, seq_dev, HEADS, HEAD)
    values = kv_all[..., width:].reshape(length, seq_dev, HEADS, HEAD)
    scores = jnp.einsum("qshe,kshe->shqk", query, keys, preferred_element_type=jnp.float32) * scale
    kpos = jnp.arange(length, dtype=jnp.int32)
    allowed = (kpos[None, None, :] <= qpos[None, :, None]) & (
        kpos[None, None, :] < lengths[:, None, None]
    )
    masked = jnp.where(allowed[:, None], scores, -1e30)
    top = jnp.max(masked, axis=-1, keepdims=True)
    expo = jnp.exp(masked - top)
    prob = expo / jnp.sum(expo, axis=-1, keepdims=True)
    prob_low = prob.astype(jnp.bfloat16)
    attended_rows = jnp.einsum(
        "shqk,kshe->qshe", prob_low, values, preferred_element_type=jnp.float32
    )
    attended_rows = attended_rows.astype(jnp.bfloat16).reshape(slot_dev * seq_dev, width)
    branch_output = jnp.dot(attended_rows, w_output, preferred_element_type=jnp.float32)
    residual_stream = flat.astype(jnp.float32) + alphas[0] * branch_output
    resid_low = residual_stream.astype(jnp.bfloat16)
    bias_float = bias_all.astype(jnp.float32)
    before_activation = (
        jnp.dot(resid_low, w_expand, preferred_element_type=jnp.float32) + bias_float[:hidden_width]
    )
    activate = partial(jax.nn.gelu, approximate=False)
    hidden_rows = activate(before_activation).astype(jnp.bfloat16)
    feed_output = (
        jnp.dot(hidden_rows, w_reduce, preferred_element_type=jnp.float32)
        + bias_float[hidden_width:]
    )
    mixed = (residual_stream + alphas[1] * feed_output).astype(jnp.bfloat16).reshape(tokens.shape)
    valid = (qpos[:, None] < lengths[None, :]).astype(jnp.float32).reshape(-1, 1)
    pull = cotangent.reshape(-1, width).astype(jnp.float32) * valid
    d_ffout = (alphas[1] * pull).astype(jnp.bfloat16)
    g_reduce = jnp.dot(hidden_rows.T, d_ffout, preferred_element_type=jnp.float32)
    g_second_bias = jnp.sum(d_ffout.astype(jnp.float32), axis=0)
    d_hidden = jnp.dot(d_ffout, w_reduce.T, preferred_element_type=jnp.float32)
    d_pre = jax.vjp(activate, before_activation)[1](d_hidden)[0].astype(jnp.bfloat16)
    g_expand = jnp.dot(resid_low.T, d_pre, preferred_element_type=jnp.float32)
    g_first_bias = jnp.sum(d_pre.astype(jnp.float32), axis=0)
    d_resid = pull + jnp.dot(d_pre, w_expand.T, preferred_element_type=jnp.float32)
    g_alpha = jnp.stack([jnp.sum(branch_output * d_resid), jnp.sum(feed_output * pull)])
    d_branch = (alphas[0] * d_resid).astype(jnp.bfloat16)
    g_output = jnp.dot(attended_rows.T, d_branch, preferred_element_type=jnp.float32)
    d_att = jnp.dot(d_branch, w_output.T, preferred_element_type=jnp.float32).astype(jnp.bfloat16)
    d_att = d_att.reshape(slot_dev, seq_dev, HEADS, HEAD)
    d_prob = jnp.einsum("qshe,kshe->shqk", d_att, values, preferred_element_type=jnp.float32)
    d_scores = (prob * (d_prob - jnp.sum(prob * d_prob, axis=-1, keepdims=True))).astype(
        jnp.bfloat16
    )
    d_query = (
        jnp.einsum("shqk,kshe->qshe", d_scores, keys, preferred_element_type=jnp.float32) * scale
    )
    count = lax.axis_size("ctx") * slot_dev
    g_keys = (
        jnp.einsum("shqk,qshe->kshe", d_scores, query, preferred_element_type=jnp.float32) * scale
    )
    g_values = jnp.einsum("shqk,qshe->kshe", prob_low, d_att, preferred_element_type=jnp.float32)
    d_kv = lax.psum_scatter(
        jnp.concatenate(
            [g_keys.reshape(count, seq_dev, width), g_values.reshape(count, seq_dev, width)],
            axis=-1,
        ).astype(jnp.bfloat16),
        "ctx",
        scatter_dimension=0,
        tiled=True,
    ).astype(jnp.float32)
    d_qkv = jnp.concatenate([d_query.reshape(slot_dev, seq_dev, width), d_kv], axis=-1)
    d_qkv = d_qkv.astype(jnp.bfloat16).reshape(-1, 3 * width)
    g_project = jnp.dot(flat.T, d_qkv, preferred_element_type=jnp.float32)
    input_grad = (
        d_resid + jnp.dot(d_qkv, w_project.T, preferred_element_type=jnp.float32)
    ).reshape(tokens.shape)
    g_bias = jnp.concatenate([g_first_bias, g_second_bias])
    devices = lax.axis_size(("dp", "ctx"))
    device_index = lax.axis_index(("dp", "ctx"))
    summed = lax.psum((g_project, g_output, g_expand, g_reduce, g_bias, g_alpha), ("dp", "ctx"))
    squares = jnp.float32(0.0)
    for grad in summed:
        squares = squares + jnp.sum(grad * grad)
    owned = []
    for grad in summed[:5]:
        rows = grad.shape[0] // devices
        owned.append(lax.dynamic_slice_in_dim(grad, device_index * rows, rows, 0))
    alpha_sum = summed[5]
    grad_norm = jnp.sqrt(squares)
    factor = jnp.minimum(1.0, clip_bound / (grad_norm + 1e-06))
    weights = (project_matrix, output_matrix, expand_matrix, reduce_matrix, biases, alphas)
    states = (
        (project_first, project_second),
        (output_first, output_second),
        (expand_first, expand_second),
        (reduce_first, reduce_second),
        (bias_first, bias_second),
        (alpha_first, alpha_second),
    )
    grads = (owned[0], owned[1], owned[2], owned[3], owned[4], alpha_sum)
    rates = (matrix_rate, matrix_rate, matrix_rate, matrix_rate, matrix_rate, alpha_rate)
    decays = (decay_rate, decay_rate, decay_rate, decay_rate, 0.0, 0.0)
    results = []
    for weight, (first, second), grad, rate, decay in zip(weights, states, grads, rates, decays):
        results.extend(adamw(weight, first, second, factor * grad, rate, decay))
    return (
        mixed,
        input_grad,
        results[0],
        results[1],
        results[2],
        results[3],
        results[4],
        results[5],
        results[6],
        results[7],
        results[8],
        results[9],
        results[10],
        results[11],
        results[12],
        results[13],
        results[14],
        results[15],
        results[16],
        results[17],
        grad_norm,
    )


def fast_body(
    tokens,
    cotangent,
    lengths,
    project_matrix,
    output_matrix,
    expand_matrix,
    reduce_matrix,
    biases,
    alphas,
    project_first,
    project_second,
    output_first,
    output_second,
    expand_first,
    expand_second,
    reduce_first,
    reduce_second,
    bias_first,
    bias_second,
    alpha_first,
    alpha_second,
):
    rows, seq_dev, width = tokens.shape
    hidden = expand_matrix.shape[1]
    devices = lax.axis_size(BOTH)
    nz = devices // 8
    chips = devices // 2
    seqs = seq_dev // 2
    slots = 4 * rows
    wide = width // 2
    table = routes(nz)

    def move(v, way):
        return lax.ppermute(v, BOTH, table[way])

    ctx, dp = lax.axis_index("ctx"), lax.axis_index("dp")
    y, c, z, x = ctx // 2, ctx % 2, dp // 2, dp % 2
    me = dp * 4 + ctx

    def gather_start(piece):
        return jnp.stack([piece] + [move(piece, r) for r in range(1, nz)])

    def gather_xy(a):
        return move(a, "x"), move(a, "y")

    def gather_diag(ax, ay):
        return move(ay[: nz // 2], "x"), move(ax[nz // 2 :], "y")

    wq = project_matrix.astype(BF16)
    wq4 = wq.reshape(wq.shape[0], 3, 2, wide)
    wq_own = lax.dynamic_index_in_dim(wq4, c, 2, False).reshape(-1, 3 * wide)
    wq_give = lax.dynamic_index_in_dim(wq4, 1 - c, 2, False).reshape(-1, 3 * wide)
    wq_got = move(wq_give, "core")
    wq_chip = jnp.where(
        c == 0, jnp.concatenate([wq_own, wq_got], 0), jnp.concatenate([wq_got, wq_own], 0)
    )
    x6 = jnp.transpose(tokens, (1, 0, 2))
    c6 = jnp.transpose(cotangent, (1, 0, 2))

    def half(v, which):
        return lax.dynamic_slice_in_dim(v, which * seqs, seqs, 0)

    x_mine = half(x6, y)
    x_got = move(half(x6, 1 - y), "y")
    x_mine_o = move(x_mine, "core")
    x_got_o = move(x_got, "core")
    wa = gather_start(wq_chip)
    wax, way = gather_xy(wa)
    wad, wae = gather_diag(wax, way)

    r1, r2 = output_matrix.shape[0], reduce_matrix.shape[0]
    groups = hidden // width
    bias_rows = jnp.zeros((16 * width,), BF16)
    bias_rows = lax.dynamic_update_slice_in_dim(
        bias_rows, biases.astype(BF16), me * biases.shape[0], 0
    ).reshape(16, width)
    blob = jnp.concatenate(
        [output_matrix.astype(BF16)]
        + [expand_matrix[:, j * width : (j + 1) * width].astype(BF16) for j in range(groups)]
        + [reduce_matrix.astype(BF16), bias_rows],
        0,
    )
    blob_rows = blob.shape[0]
    ba = gather_start(blob)
    bax, bay = gather_xy(ba)
    bad, bae = gather_diag(bax, bay)
    rail = (ba, bax, bay, bad, bae)
    rail_o = tuple(move(v, "core") for v in rail)

    c_mine = half(c6, y)
    c_got = move(half(c6, 1 - y), "y")

    lens = half(lengths, y)
    place = jnp.stack([c, y, z, x]).astype(jnp.int32)

    def info_for(s):
        return jnp.concatenate([place, lens, lens[s : s + 1]])

    def seq_block(s):
        return pl.BlockSpec((1, rows, width), lambda *_: (s, 0, 0))

    o_shape = (1, 2, rows, wide)
    params = pltpu.CompilerParams(vmem_limit_bytes=VMEM_LIMIT)
    xs4 = (x_mine, x_got, x_mine_o, x_got_o)
    kept = []
    wq_full = None
    fwd_out = [
        jax.ShapeDtypeStruct((1, slots, 3 * wide), BF16),
        jax.ShapeDtypeStruct(o_shape, BF16),
        jax.ShapeDtypeStruct(o_shape, BF16),
        jax.ShapeDtypeStruct((1, 8, slots), F32),
    ]
    wq_shape = jax.ShapeDtypeStruct((width, 3 * wide), BF16)
    fwd_cost = pl.CostEstimate(
        flops=2 * slots * width * 3 * wide + 8 * slots * slots * 256, transcendentals=4 * slots * slots,
        bytes_accessed=6 * slots * width)
    for s in range(seqs):
        first = s == 0
        weight_in = (wa, wax, way, wad, wae) if first else (wq_full,)
        outs = ([wq_shape] if first else []) + fwd_out
        res = pl.pallas_call(
            partial(attend_forward, first, nz),
            grid=(1,),
            in_specs=[SMEM] + [seq_block(s)] * 4 + [whole(v.shape) for v in weight_in],
            out_specs=[whole(v.shape) for v in outs],
            out_shape=outs,
            scratch_shapes=[pltpu.VMEM((slots, wide), BF16), pltpu.VMEM((slots, 128), F32)],
            compiler_params=params,
            cost_estimate=fwd_cost,
            name="attend_forward",
        )(info_for(s), *xs4, *weight_in)
        if first:
            wq_full = res[0]
            res = res[1:]
        kept.append(tuple(res) + (move(res[2], "core"),))

    def seq_step(t):
        return (t // 2, 0, 0)

    def seq_half(t):
        return (t // 2, t % 2, 0, 0)

    own_o = [k[1] for k in kept]
    oth_o = [k[4] for k in kept]
    tok = pl.BlockSpec((1, rows, width), seq_step)
    act = pl.BlockSpec((1, 1, rows, wide), seq_half)
    feed_in = (x_mine, x_got, c_mine, c_got, *own_o, *oth_o, *rail, *rail_o)
    feed_out = [
        jax.ShapeDtypeStruct((seqs, rows, width), BF16),
        jax.ShapeDtypeStruct((seqs, rows, width), BF16),
        jax.ShapeDtypeStruct((seqs, 2, rows, width), F32),
        jax.ShapeDtypeStruct((seqs, 2, rows, wide), BF16),
        jax.ShapeDtypeStruct((seqs, 2, rows, wide), BF16),
        jax.ShapeDtypeStruct((chips, blob_rows, width), BF16),
        jax.ShapeDtypeStruct((chips, blob_rows, width), BF16),
        jax.ShapeDtypeStruct((8, width), F32),
    ]
    weights_n = width * width + 2 * width * hidden
    mixed_m, mixed_g, dy, do_keep, do_send, g_send, g_keep, ga = pl.pallas_call(
        partial(feed, nz),
        grid=(2 * seqs,),
        in_specs=[SMEM, SMEM] + [tok] * 4 + [whole(v.shape) for v in feed_in[4:]],
        out_specs=[tok, tok, pl.BlockSpec((1, 1, rows, width), seq_half), act, act]
        + [whole(v.shape) for v in feed_out[5:]],
        out_shape=feed_out,
        scratch_shapes=[
            pltpu.VMEM((width, width), BF16),
            pltpu.VMEM((width, hidden), BF16),
            pltpu.VMEM((hidden, width), BF16),
            pltpu.VMEM((16, width), F32),
            pltpu.VMEM((width, width), F32),
            pltpu.VMEM((width, hidden), F32),
            pltpu.VMEM((hidden, width), F32),
            pltpu.VMEM((8, hidden), F32),
            pltpu.VMEM((8, width), F32),
            pltpu.VMEM((16, width), F32),
            pltpu.VMEM((rows, hidden), BF16),
            pltpu.VMEM((rows, hidden), F32),
            pltpu.VMEM((rows, hidden), BF16),
        ],
        compiler_params=params,
        cost_estimate=pl.CostEstimate(
            flops=6 * 2 * seqs * rows * weights_n,
            transcendentals=2 * seqs * rows * hidden,
            bytes_accessed=4 * weights_n,
        ),
        name="feed",
    )(jnp.concatenate([place, lens]), alphas, *feed_in)

    mixed_r = move(mixed_g, "y")
    mixed6 = jnp.where(
        y == 0, jnp.concatenate([mixed_m, mixed_r], 0), jnp.concatenate([mixed_r, mixed_m], 0)
    )
    do_recv = move(do_send, "core")

    def fold(v):
        return v.reshape((nz, 2, 2) + v.shape[1:])

    def at(v, axis, index):
        return lax.dynamic_index_in_dim(v, index, axis, False)

    def add(a, b):
        return a.astype(F32) + b.astype(F32)

    def reduce_xy_start(a, b):
        return move(at(a, 1, 1 - x), "x"), move(at(b, 2, 1 - y), "y")

    def reduce_xy_next(a, b, ra, rb):
        a = add(at(a, 1, x), ra).astype(BF16)
        b = add(at(b, 2, y), rb).astype(BF16)
        return a, b, move(at(a, 1, 1 - y), "y"), move(at(b, 1, 1 - x), "x")

    def reduce_z_start(a, b, ra, rb, axis):
        a = add(at(a, 1, y), ra)
        b = add(at(b, 1, x), rb)
        v = jnp.concatenate([a, b], axis).astype(BF16)
        got = [move(at(v, 0, z ^ r), r) for r in range(1, nz)]
        return v, got

    def reduce_z_end(v, got):
        total = at(v, 0, z).astype(F32)
        for g in got:
            total = total + g.astype(F32)
        return total

    g_recv = move(g_send, "core")
    cut = blob_rows // 2

    def backward(s, grad):
        qkv, ok, osend, lse, _ = kept[s]
        first = grad is None
        ins = (wq_full, qkv, lse, ok, osend, do_keep, do_recv, dy) + (() if first else (grad,))
        own = pl.BlockSpec((1, 2, rows, wide), lambda *_: (s, 0, 0, 0))
        specs = [whole(v.shape) for v in ins[:5]]
        specs += [own, own, pl.BlockSpec((1, 2, rows, width), lambda *_: (s, 0, 0, 0))]
        specs += [] if first else [whole(grad.shape)]
        return pl.pallas_call(
            partial(attend_backward, first),
            grid=(1,),
            in_specs=[SMEM] + [seq_block(s)] * 4 + specs,
            out_specs=[whole((width, 3 * wide)), whole((1, 2, rows, width)), whole((1, 2, rows, width))],
            out_shape=[
                jax.ShapeDtypeStruct((width, 3 * wide), F32),
                jax.ShapeDtypeStruct((1, 2, rows, width), F32),
                jax.ShapeDtypeStruct((1, 2, rows, width), BF16),
            ],
            scratch_shapes=[
                pltpu.VMEM((slots, wide), BF16),
                pltpu.VMEM((8, slots), F32),
                pltpu.VMEM((slots, wide), BF16),
                pltpu.VMEM((slots, wide), F32),
                pltpu.VMEM((slots, wide), F32),
            ],
            compiler_params=params,
            cost_estimate=pl.CostEstimate(
                flops=4 * slots * width * 3 * wide + 20 * slots * slots * 256,
                transcendentals=4 * slots * slots,
                bytes_accessed=12 * slots * width,
            ),
            name="attend_backward",
        )(info_for(s), *xs4, *ins)

    grad = None
    keep, recv = [], []
    stage = None
    for s in range(seqs):
        grad, dkeep, dsend = backward(s, grad)
        keep.append(dkeep)
        recv.append(move(dsend, "core"))
    both = fold(add(g_keep, g_recv).astype(BF16))
    fa, fb = both[:, :, :, :cut], both[:, :, :, cut:]
    ra, rb = reduce_xy_start(fa, fb)
    fa, fb, ra, rb = reduce_xy_next(fa, fb, ra, rb)
    fv, fgot = reduce_z_start(fa, fb, ra, rb, 1)
    blob_sum = reduce_z_end(fv, fgot)

    total = [k + r.astype(F32) for k, r in zip(keep, recv)]
    in_mine = jnp.concatenate([t[:, 0] for t in total], 0)
    in_got = jnp.concatenate([t[:, 1] for t in total], 0).astype(BF16)
    in_recv = move(in_got, "y").astype(F32)
    input6 = jnp.where(
        y == 0, jnp.concatenate([in_mine, in_recv], 0), jnp.concatenate([in_recv, in_mine], 0)
    )

    gq = grad.astype(BF16).reshape(nz, 2, 2, 2 * r1, 3 * wide)
    cutq = 3 * wide // 2
    qa, qb = gq[..., :cutq], gq[..., cutq:]
    ra, rb = reduce_xy_start(qa, qb)
    qa, qb, ra, rb = reduce_xy_next(qa, qb, ra, rb)
    qv, qgot = reduce_z_start(qa, qb, ra, rb, 2)
    q_sum = reduce_z_end(qv, qgot)
    q_own = lax.dynamic_slice_in_dim(q_sum, c * r1, r1, 0)
    q_give = lax.dynamic_slice_in_dim(q_sum, (1 - c) * r1, r1, 0)
    q_got = move(q_give, "core")
    cols = (r1, 3, 1, wide)
    q_own, q_got = q_own.reshape(cols), q_got.reshape(cols)
    g_project = jnp.where(
        c == 0, jnp.concatenate([q_own, q_got], 2), jnp.concatenate([q_got, q_own], 2)
    ).reshape(r1, 6 * wide)

    g_output = blob_sum[:r1]
    g_expand = jnp.concatenate([blob_sum[(1 + j) * r1 : (2 + j) * r1] for j in range(groups)], 1)
    g_reduce = blob_sum[(1 + groups) * r1 : (1 + groups) * r1 + r2]
    g_bias = lax.dynamic_slice_in_dim(
        blob_sum[(1 + groups) * r1 + r2 :].reshape(-1), me * biases.shape[0], biases.shape[0], 0
    )
    part = sum(jnp.sum(g * g) for g in (g_project, g_output, g_expand, g_reduce, g_bias))
    ga = jnp.sum(ga, axis=1)
    tiny = jnp.concatenate([part[None], ga[:2], jnp.zeros((5,), F32)])
    tiny = jnp.broadcast_to(tiny[:, None], (8, 128))
    for way in ("core", "y", "x"):
        tiny = tiny + move(tiny, way)
    tiny = tiny + sum(move(tiny, r) for r in range(1, nz))
    alpha_sum = tiny[1:3, 0]
    grad_norm = jnp.sqrt(tiny[0, 0] + jnp.sum(alpha_sum * alpha_sum))
    factor = jnp.minimum(1.0, clip_bound / (grad_norm + 1e-06))
    weights = (project_matrix, output_matrix, expand_matrix, reduce_matrix, biases, alphas)
    states = (
        (project_first, project_second),
        (output_first, output_second),
        (expand_first, expand_second),
        (reduce_first, reduce_second),
        (bias_first, bias_second),
        (alpha_first, alpha_second),
    )
    grads = (g_project, g_output, g_expand, g_reduce, g_bias, alpha_sum)
    rates = (matrix_rate, matrix_rate, matrix_rate, matrix_rate, matrix_rate, alpha_rate)
    decays = (decay_rate, decay_rate, decay_rate, decay_rate, 0.0, 0.0)
    results = []
    for weight, (m, v), g, rate, decay in zip(weights, states, grads, rates, decays):
        results.extend(adamw(weight, m, v, factor * g, rate, decay))
    mixed = jnp.transpose(mixed6, (1, 0, 2))
    input_grad = jnp.transpose(input6, (1, 0, 2))
    return (mixed, input_grad, *results, grad_norm)


def solution(mesh):
    ctx, dp = mesh.shape["ctx"], mesh.shape["dp"]
    row = P(BOTH, None)
    flat = P(BOTH)
    token = P("ctx", "dp", None)
    body = fast_body if (ctx == 4 and dp == 8) else generic_body
    return jax.shard_map(
        body,
        mesh=mesh,
        in_specs=(token, token, P("dp"), row, row, row, row, flat, P())
        + (row,) * 8
        + (flat, flat, P(), P()),
        out_specs=(token, token) + (row,) * 12 + (flat,) * 3 + (P(),) * 4,
        check_vma=False,
    )
```

```python
from functools import partial

import jax
import jax.numpy as jnp
from jax import lax
from jax.experimental import pallas as pl
from jax.experimental.pallas import tpu as pltpu
from jax.sharding import PartitionSpec as P

HEADS = 8
HEAD = 64
STEP = 10


clip_bound = 1.0
beta_one = 0.9
beta_two = 0.999
adam_eps = 1e-08
matrix_rate = 0.05
alpha_rate = 0.2
decay_rate = 0.1

BOTH = ("dp", "ctx")
F32 = jnp.float32
BF16 = jnp.bfloat16
VMEM_LIMIT = 56 * 1024 * 1024


def adamw(weight, first, second, grad, rate, decay):
    first = beta_one * first + (1.0 - beta_one) * grad
    second = beta_two * second + (1.0 - beta_two) * grad * grad
    mhat = first / (1.0 - beta_one**STEP)
    vhat = second / (1.0 - beta_two**STEP)
    weight = weight - rate * (mhat / (jnp.sqrt(vhat) + adam_eps) + decay * weight)
    return (first, second, weight)


def dot_nn(a, b):
    return lax.dot_general(a, b, (((1,), (0,)), ((), ())), preferred_element_type=F32)


def dot_nt(a, b):
    return lax.dot_general(a, b, (((1,), (1,)), ((), ())), preferred_element_type=F32)


def dot_tn(a, b):
    return lax.dot_general(a, b, (((0,), (0,)), ((), ())), preferred_element_type=F32)


CORE, CHIP_Y, CHIP_Z, CHIP_X, LENS, OWN, OTHER, FOUND = 0, 1, 2, 3, 4, 7, 10, 13


def block_places(info, rows):
    core, y = info[CORE], info[CHIP_Y]
    return [
        pl.multiple_of(b * rows, rows)
        for b in (
            2 * y + core,
            2 * (1 - y) + core,
            2 * y + 1 - core,
            2 * (1 - y) + 1 - core,
        )
    ]


def chip_index(info, r, fx, fy):
    z = info[CHIP_Z] ^ r
    x = info[CHIP_X] ^ fx
    y = info[CHIP_Y] ^ fy
    return (z * 2 + x) * 2 + y


PIECES = 4


def gathered_pieces(nz):
    places = ((0, 0), (1, 0), (0, 1), (1, 1))
    return [(i, r, r, fx, fy) for i, (fx, fy) in enumerate(places) for r in range(nz)]


def attend_forward(s, nz, info, *refs):
    assemble = s == 0
    refs = list(refs)
    x_refs = [refs.pop(0) for _ in range(4)]
    if assemble:
        pieces = [refs.pop(0) for _ in range(PIECES)]
        wq_ref, qkv_ref, ok_ref, os_ref, lse_ref, o_s, st_s = refs
        rows = pieces[0].shape[1]
        for which, at, r, fx, fy in gathered_pieces(nz):
            place = pl.multiple_of(chip_index(info, r, fx, fy) * rows, rows)
            wq_ref[pl.ds(place, rows), :] = pieces[which][at]
    else:
        wq_ref, qkv_ref, ok_ref, os_ref, lse_ref, o_s, st_s = refs
    length = info[LENS + s]
    rows = x_refs[0].shape[1]
    places = block_places(info, rows)
    w = wq_ref[...]
    for x_ref, place in zip(x_refs, places):
        qkv_ref[0, pl.ds(place, rows), :] = dot_nn(x_ref[0], w).astype(BF16)
    blocks = (length + rows - 1) // rows
    lane = lax.broadcasted_iota(jnp.int32, (rows, 128), 1)
    low_lane = lane < HEAD
    row_i = lax.broadcasted_iota(jnp.int32, (rows, rows), 0)
    col_i = lax.broadcasted_iota(jnp.int32, (rows, rows), 1)

    def one(qb, n, pair):
        at = pair * 128
        wide = 256
        q = qkv_ref[0, qb * rows : (qb + 1) * rows, pl.ds(at, 128)]
        k = qkv_ref[0, 0 : n * rows, pl.ds(wide + at, 128)]
        v = qkv_ref[0, 0 : n * rows, pl.ds(2 * wide + at, 128)]
        vx = jnp.concatenate([v, jnp.ones_like(v)], axis=1)
        base = (n - 1) * rows
        ok = (base + col_i) < length
        if n == qb + 1:
            ok = ok & (col_i <= row_i)
        res = []
        stats = st_s[qb * rows : (qb + 1) * rows, :]
        for h in range(2):
            mine = low_lane if h == 0 else jnp.logical_not(low_lane)
            qm = jnp.where(mine, q * jnp.asarray(HEAD**-0.5, BF16), jnp.zeros_like(q))
            sc = dot_nt(qm, k)
            last = jnp.where(ok, sc[:, base:], -1e30)
            if n > 1:
                sc = jnp.concatenate([sc[:, :base], last], axis=1)
            else:
                sc = last
            top = jnp.max(sc, axis=1, keepdims=True)
            e = jnp.exp(sc - top)
            ob = dot_nn(e.astype(BF16), vx)
            den = ob[:, 128:]
            res.append(ob[:, :128] / den)
            stats = jnp.where(lane == 2 * pair + h, top + jnp.log(den), stats)
        st_s[qb * rows : (qb + 1) * rows, :] = stats
        o_s[qb * rows : (qb + 1) * rows, pl.ds(at, 128)] = jnp.where(
            low_lane, res[0], res[1]
        ).astype(BF16)

    total = qkv_ref.shape[1] // rows
    st_s[...] = jnp.zeros_like(st_s)
    for qb in range(total):
        for n in range(1, qb + 2):
            cond = (blocks == n) if n < qb + 1 else (blocks >= n)

            @pl.when(cond)
            def _(qb=qb, n=n):
                for pair in range(2):
                    one(qb, n, pair)

    for b in range(2):
        ok_ref[0, b] = o_s[pl.ds(places[b], rows), :]
        os_ref[0, b] = o_s[pl.ds(places[2 + b], rows), :]
    lse_ref[0] = jnp.transpose(st_s[...])[:8]


def attend_backward(s, last_one, info, *refs):
    first = s == 0
    refs = list(refs)
    x_refs = [refs.pop(0) for _ in range(4)]
    wq_ref, qkv_ref, lse_ref, ok_ref, os_ref, dk_ref, dr_ref, dy_ref = (refs.pop(0) for _ in range(8))
    g_in = None if first else refs.pop(0)
    if last_one:
        qkeep_ref, qsend_ref, keep_ref, send_ref, do_s, r_s, dq_s, dk_s, dv_s, g_ref = refs
    else:
        g_ref, keep_ref, send_ref, do_s, r_s, dq_s, dk_s, dv_s = refs
    length = info[LENS + s]
    rows = x_refs[0].shape[1]
    places = block_places(info, rows)
    lane = lax.broadcasted_iota(jnp.int32, (rows, 128), 1)
    low_lane = lane < HEAD
    head_of = lax.broadcasted_iota(jnp.int32, (8, 256), 1) // HEAD
    pick = (head_of == lax.broadcasted_iota(jnp.int32, (8, 256), 0)).astype(F32)
    for b in range(4):
        do = (dk_ref if b < 2 else dr_ref)[0, b % 2]
        o = (ok_ref if b < 2 else os_ref)[0, b % 2]
        do_s[pl.ds(places[b], rows), :] = do
        prod = do.astype(F32) * o.astype(F32)
        r_s[:, pl.ds(places[b], rows)] = lax.dot_general(
            pick, prod, (((1,), (1,)), ((), ())),
            preferred_element_type=F32, precision=lax.Precision.HIGHEST)
    dk_s[...] = jnp.zeros_like(dk_s)
    dv_s[...] = jnp.zeros_like(dv_s)
    if first:
        g_ref[...] = jnp.zeros_like(g_ref)
    else:
        g_ref[...] = g_in[...]
    key_i = lax.broadcasted_iota(jnp.int32, (rows, rows), 0)
    qry_i = lax.broadcasted_iota(jnp.int32, (rows, rows), 1)
    scale = HEAD**-0.5

    def one(qb, pair):
        n = qb + 1
        at = pair * 128
        wide = 256
        span = slice(qb * rows, (qb + 1) * rows)
        q = qkv_ref[0, span, pl.ds(at, 128)]
        k = qkv_ref[0, 0 : n * rows, pl.ds(wide + at, 128)]
        v = qkv_ref[0, 0 : n * rows, pl.ds(2 * wide + at, 128)]
        do = do_s[span, pl.ds(at, 128)]
        base = qb * rows
        ok = (key_i <= qry_i) & ((base + key_i) < length)
        dqs = []
        dv = dk = None
        for h in range(2):
            head = 2 * pair + h
            mine = low_lane if h == 0 else jnp.logical_not(low_lane)
            qm = jnp.where(mine, q * jnp.asarray(scale, BF16), jnp.zeros_like(q))
            dom = jnp.where(mine, do, jnp.zeros_like(do))
            sc = dot_nt(k, qm)
            p = jnp.exp(sc - lse_ref[0, head : head + 1, span])
            last = jnp.where(ok, p[base:], 0.0)
            p = jnp.concatenate([p[:base], last], axis=0) if n > 1 else last
            dp = dot_nt(v, dom)
            ds = (p * (dp - r_s[head : head + 1, span])).astype(BF16)
            dvh = dot_nn(p.astype(BF16), dom)
            dkh = dot_nn(ds, qm)
            dv = dvh if dv is None else dv + dvh
            dk = dkh if dk is None else dk + dkh
            dqs.append(dot_tn(ds, k))
        dv_s[0 : n * rows, pl.ds(at, 128)] += dv
        dk_s[0 : n * rows, pl.ds(at, 128)] += dk
        dq_s[span, pl.ds(at, 128)] = (jnp.where(low_lane, dqs[0], dqs[1]) * scale).astype(BF16)

    total = qkv_ref.shape[1] // rows
    for qb in range(total):

        @pl.when(qb * rows < length)
        def _(qb=qb):
            for pair in range(2):
                one(qb, pair)

    w = wq_ref[...]
    for b in range(4):
        place = places[b]
        here = pl.ds(place, rows)

        @pl.when(place < length)
        def _(b=b, here=here):
            d = jnp.concatenate(
                [dq_s[here, :], dk_s[here, :].astype(BF16), dv_s[here, :].astype(BF16)], axis=1
            )
            g_ref[...] += dot_tn(x_refs[b][0], d)
            dx = dot_nt(d, w)
            if b < 2:
                keep_ref[0, b] = dy_ref[0, b] + dx
            else:
                send_ref[0, b - 2] = dx.astype(BF16)

        @pl.when(place >= length)
        def _(b=b):
            if b < 2:
                keep_ref[0, b] = jnp.zeros_like(keep_ref[0, b])
            else:
                send_ref[0, b - 2] = jnp.zeros_like(send_ref[0, b - 2])

    if last_one:
        nz = qkeep_ref.shape[1]
        part = g_ref.shape[0] // (nz * 4)
        x = info[CHIP_X]
        for z in range(nz):
            for y in range(2):
                for out, which in ((qkeep_ref, x), (qsend_ref, 1 - x)):
                    at = pl.multiple_of(((z * 2 + which) * 2 + y) * part, part)
                    out[y, z] = g_ref[pl.ds(at, part), :].astype(out.dtype)


def feed(nz, info, alphas, *refs):
    refs = list(refs)
    xm, xg, cm, cg = (refs.pop(0) for _ in range(4))
    own_o = [refs.pop(0) for _ in range(3)]
    oth_o = [refs.pop(0) for _ in range(3)]
    rails = [[refs.pop(0) for _ in range(PIECES)] for _ in range(2)]
    (mixm, mixg, dy_ref, dkeep, dsend, gsend, gkeep, ga_ref,
     wo_s, w1_s, w2_s, b_s, go_s, g1_s, g2_s, gb1_s, gb2_s, ga_s,
     h_s, gp_s, dpre_s) = refs
    step = pl.program_id(0)
    s, b = step // 2, step % 2
    core = info[CORE]
    chips = nz * 4
    width = wo_s.shape[1]
    groups = w1_s.shape[1] // width
    r1 = wo_s.shape[0] // (2 * chips)
    r2 = w2_s.shape[0] // (2 * chips)

    @pl.when(step == 0)
    def _():
        bias = None
        for rail in range(2):
            for which, at, r, fx, fy in gathered_pieces(nz):
                d = chip_index(info, r, fx, fy) * 2 + (core ^ rail)
                piece = rails[rail][which]
                small = pl.ds(pl.multiple_of(d * r1, r1), r1)
                wo_s[small, :] = piece[at, 0:r1]
                for j in range(groups):
                    w1_s[small, j * width : (j + 1) * width] = piece[at, (1 + j) * r1 : (2 + j) * r1]
                first = (1 + groups) * r1
                w2_s[pl.ds(pl.multiple_of(d * r2, r2), r2), :] = piece[at, first : first + r2]
                part = piece[at, first + r2 : first + r2 + 16].astype(F32)
                bias = part if bias is None else bias + part
        b_s[...] = bias
        for ref in (go_s, g1_s, g2_s, gb1_s, gb2_s, ga_s):
            ref[...] = jnp.zeros_like(ref)

    rows = xm.shape[1]
    block = jnp.where(b == 0, 2 * info[CHIP_Y] + core, 2 * (1 - info[CHIP_Y]) + core)
    length = info[LENS + s]
    begin = block * rows

    def pick3(three):
        return jnp.where(s == 0, three[0][0, b], jnp.where(s == 1, three[1][0, b], three[2][0, b]))

    o_own = pick3(own_o)
    o_oth = pick3(oth_o)
    here = pl.ds(pl.multiple_of(core * 256, 256), 256)
    there = pl.ds(pl.multiple_of((1 - core) * 256, 256), 256)
    a0, a1 = alphas[0], alphas[1]
    x = jnp.where(b == 0, xm[0], xg[0]).astype(F32)
    branch = dot_nn(o_own, wo_s[here, :]) + dot_nn(o_oth, wo_s[there, :])
    y = x + a0 * branch
    yb = y.astype(BF16)
    f = None
    for j in range(groups):
        cols = slice(j * width, (j + 1) * width)
        pre = dot_nn(yb, w1_s[:, cols]) + b_s[j : j + 1, :]
        cdf = 0.5 + 0.5 * lax.erf(pre * (0.5**0.5))
        h = (pre * cdf).astype(BF16)
        h_s[:, cols] = h
        gp_s[:, cols] = cdf + pre * (jnp.exp(-0.5 * pre * pre) * 0.3989422804014327)
        part = dot_nn(h, w2_s[cols, :])
        f = part if f is None else f + part
    f = f + b_s[groups : groups + 1, :]
    mixed = (y + a1 * f).astype(BF16)

    @pl.when(b == 0)
    def _():
        mixm[0] = mixed

    @pl.when(b == 1)
    def _():
        mixg[0] = mixed

    @pl.when(begin < length)
    def _():
        row = lax.broadcasted_iota(jnp.int32, (rows, width), 0)
        cot = jnp.where(b == 0, cm[0], cg[0]).astype(F32)
        g = jnp.where(begin + row < length, cot, 0.0)
        df = (a1 * g).astype(BF16)
        gb2_s[...] += jnp.sum(df.astype(F32).reshape(rows // 8, 8, width), axis=0)
        dy = g
        for j in range(groups):
            cols = slice(j * width, (j + 1) * width)
            dh = dot_nt(df, w2_s[cols, :])
            dpre_f = dh * gp_s[:, cols]
            dpre = dpre_f.astype(BF16)
            gb1_s[:, cols] += jnp.sum(dpre.astype(F32).reshape(rows // 8, 8, width), axis=0)
            g2_s[cols, :] += dot_tn(h_s[:, cols], df)
            g1_s[:, cols] += dot_tn(yb, dpre)
            dy = dy + dot_nt(dpre, w1_s[:, cols])
        ga_s[0:8, :] += jnp.sum((branch * dy).reshape(rows // 8, 8, width), axis=0)
        ga_s[8:16, :] += jnp.sum((f * g).reshape(rows // 8, 8, width), axis=0)
        db = (a0 * dy).astype(BF16)
        go_s[here, :] += dot_tn(o_own, db)
        go_s[there, :] += dot_tn(o_oth, db)
        dkeep[0, 0] = dot_nt(db, wo_s[here, :]).astype(BF16)
        dsend[0, 0] = dot_nt(db, wo_s[there, :]).astype(BF16)
        dy_ref[0, 0] = dy

    @pl.when(begin >= length)
    def _():
        dkeep[...] = jnp.zeros_like(dkeep)
        dsend[...] = jnp.zeros_like(dsend)
        dy_ref[...] = jnp.zeros_like(dy_ref)

    @pl.when(step == pl.num_programs(0) - 1)
    def _():
        gb = jnp.concatenate(
            [jnp.sum(gb1_s[:, j * width : (j + 1) * width], axis=0, keepdims=True) for j in range(groups)]
            + [jnp.sum(gb2_s[...], axis=0, keepdims=True), jnp.zeros((16 - groups - 1, width), F32)],
            axis=0,
        ).astype(BF16)
        for out, whose in ((gkeep, core), (gsend, 1 - core)):
            for z in range(nz):
                for cx in range(2):
                    for cy in range(2):
                        d = ((z * 2 + cx) * 2 + cy) * 2 + whose
                        small = pl.ds(pl.multiple_of(d * r1, r1), r1)
                        out[0, cx, cy, z, 0:r1] = go_s[small, :].astype(BF16)
                        for j in range(groups):
                            out[0, cx, cy, z, (1 + j) * r1 : (2 + j) * r1] = g1_s[
                                small, j * width : (j + 1) * width
                            ].astype(BF16)
                        out[1, cy, cx, z, 0:r2] = g2_s[
                            pl.ds(pl.multiple_of(d * r2, r2), r2), :
                        ].astype(BF16)
                        out[1, cy, cx, z, r2 : r2 + 16] = gb
        ga_ref[0:1, :] = jnp.sum(ga_s[0:8, :], axis=0, keepdims=True)
        ga_ref[1:2, :] = jnp.sum(ga_s[8:16, :], axis=0, keepdims=True)


def prepare(place, lengths, wq, x_ref, c_ref, info, w_own, w_give, xg_ref, cg_ref, sems):
    six = lengths.shape[0]
    seqs = six // 2
    y = place[1]
    for i in range(4):
        info[i] = place[i]
    ranks = []
    for i in range(six):
        rank = jnp.int32(0)
        for j in range(six):
            if j != i:
                longer = lengths[j] >= lengths[i] if j < i else lengths[j] > lengths[i]
                rank = rank + longer.astype(jnp.int32)
        ranks.append(rank)
    order = [0] + list(range(3, six, 2)) + [1] + list(range(2, six, 2))
    ids = []
    for r in order:
        ids.append(sum(jnp.where(ranks[i] == r, i, 0) for i in range(six)))
    own = [jnp.where(y == 0, ids[s], ids[seqs + s]) for s in range(seqs)]
    other = [jnp.where(y == 0, ids[seqs + s], ids[s]) for s in range(seqs)]
    copies = []
    for s in range(seqs):
        copies.append(pltpu.make_async_copy(x_ref.at[other[s]], xg_ref.at[s], sems.at[s]))
        copies.append(pltpu.make_async_copy(c_ref.at[other[s]], cg_ref.at[s], sems.at[seqs + s]))
    for copy in copies:
        copy.start()
    for s in range(seqs):
        info[LENS + s] = lengths[own[s]]
        info[OWN + s] = own[s]
        info[OTHER + s] = other[s]
    for s in range(seqs):
        info[FOUND + own[s]] = s
        info[FOUND + other[s]] = seqs + s
    wide = wq.shape[1] // 6
    core = place[0]
    for j in range(3):
        left = wq[:, 2 * j * wide : (2 * j + 1) * wide]
        right = wq[:, (2 * j + 1) * wide : (2 * j + 2) * wide]
        cols = slice(j * wide, (j + 1) * wide)
        w_own[:, cols] = jnp.where(core == 0, left, right).astype(BF16)
        w_give[:, cols] = jnp.where(core == 0, right, left).astype(BF16)
    for copy in copies:
        copy.wait()


def pack(wo, w1, w2, bias, out):
    rows, width = wo.shape
    groups = w1.shape[1] // width
    out[0:rows] = wo[...].astype(BF16)
    for j in range(groups):
        out[(1 + j) * rows : (2 + j) * rows] = w1[:, j * width : (j + 1) * width].astype(BF16)
    first = (1 + groups) * rows
    out[first : first + w2.shape[0]] = w2[...].astype(BF16)
    out[first + w2.shape[0] :] = bias[...]


def finish(info, gq, r1, r2, r3, blob, ga, q_own, q_give, tiny):
    total = gq[info[CHIP_Z]]
    for r in (r1, r2, r3):
        total = total + r[...].astype(F32)
    rows = q_own.shape[0]
    core = info[CORE]
    tiny_rows = tiny.shape[0]
    sums = jnp.sum(total * total)
    main = blob.shape[0] - 16
    own = blob[0:main, :]
    sums = sums + jnp.sum(own * own)
    me = ((info[CHIP_Z] * 2 + info[CHIP_X]) * 2 + info[CHIP_Y]) * 2 + core
    bias = blob[main:, :]
    width = bias.shape[1]
    count = 5 * width // tiny_rows
    flat = lax.broadcasted_iota(jnp.int32, bias.shape, 0) * width + lax.broadcasted_iota(
        jnp.int32, bias.shape, 1
    )
    ours = (flat >= me * count) & (flat < (me + 1) * count)
    sums = sums + jnp.sum(jnp.where(ours, bias * bias, 0.0))
    low, high = total[:rows], total[rows:]
    q_own[...] = jnp.where(core == 0, low, high)
    q_give[...] = jnp.where(core == 0, high, low)
    lane = lax.broadcasted_iota(jnp.int32, tiny.shape, 1)
    a0, a1 = jnp.sum(ga[0:1, :]), jnp.sum(ga[1:2, :])
    tiny[...] = jnp.where(lane == 0, sums, jnp.where(lane == 1, a0, jnp.where(lane == 2, a1, 0.0)))


def placed(info, mixm, mixr, k0, k1, k2, r0, r1, r2, b0, b12, mixed, grad):
    for s in range(mixm.shape[0]):
        mixed[info[OWN + s]] = mixm[s]
        mixed[info[OTHER + s]] = mixr[s]
    for s, (k, r) in enumerate(((k0, r0), (k1, r1), (k2, r2))):
        grad[info[OWN + s]] = k[0, 0] + r[0, 0].astype(F32)
    for s, (ref, at) in enumerate(((b0, 0), (b12, 0), (b12, 1))):
        grad[info[OTHER + s]] = ref[at].astype(F32)


def update(info, tiny, q_own, q_got, blob, g_bias, *refs):
    ins, outs = refs[:18], refs[18:]
    squares = jnp.sum(tiny[:, 0:1])
    a0, a1 = jnp.sum(tiny[:, 1:2]), jnp.sum(tiny[:, 2:3])
    norm = jnp.sqrt(jnp.zeros((1, 1), F32) + (squares + a0 * a0 + a1 * a1))
    factor = jnp.minimum(1.0, clip_bound / (norm + 1e-06))
    outs[18][...] = norm
    rows = q_own.shape[0]
    wide = q_own.shape[1] // 3

    def put(i, place, grad, rate, decay):
        if grad.ndim == 1:
            f = jnp.zeros(grad.shape, F32) + factor[0, 0]
        else:
            f = factor
        res = adamw(ins[3 * i][place], ins[3 * i + 1][place], ins[3 * i + 2][place], f * grad, rate, decay)
        for j in range(3):
            outs[3 * i + j][place] = res[j]

    core = info[CORE]
    for j in range(3):
        left = q_own[:, j * wide : (j + 1) * wide]
        right = q_got[:, j * wide : (j + 1) * wide]
        both = (jnp.where(core == 0, left, right), jnp.where(core == 0, right, left))
        for k in range(2):
            at = (2 * j + k) * wide
            put(0, (slice(None), slice(at, at + wide)), both[k], matrix_rate, decay_rate)
    width = blob.shape[1]
    groups = ins[6].shape[1] // width
    put(1, (slice(None), slice(None)), blob[0:rows, :], matrix_rate, decay_rate)
    for j in range(groups):
        put(2, (slice(None), slice(j * width, (j + 1) * width)), blob[(1 + j) * rows : (2 + j) * rows, :],
            matrix_rate, decay_rate)
    first = (1 + groups) * rows
    put(3, (slice(None), slice(None)), blob[first : first + ins[9].shape[0], :], matrix_rate, decay_rate)
    put(4, (slice(None), slice(None)), g_bias[...], matrix_rate, 0.0)
    lane = lax.broadcasted_iota(jnp.int32, (1, 2), 1)
    put(5, (slice(None), slice(None)), jnp.where(lane == 0, a0, a1), alpha_rate, 0.0)


def whole(shape):
    return pl.BlockSpec(shape, lambda *_: (0,) * len(shape))


SMEM = pl.BlockSpec(memory_space=pltpu.SMEM)
ANY = pl.BlockSpec(memory_space=pl.ANY)


def routes(nz):
    def perm(to):
        out = []
        for z in range(nz):
            for x in range(2):
                for y in range(2):
                    for c in range(2):
                        z2, x2, y2, c2 = to(z, x, y, c)
                        out.append((((z * 2 + x) * 4 + y * 2 + c), ((z2 * 2 + x2) * 4 + y2 * 2 + c2)))
        return out

    table = {
        "core": perm(lambda z, x, y, c: (z, x, y, 1 - c)),
        "y": perm(lambda z, x, y, c: (z, x, 1 - y, c)),
        "x": perm(lambda z, x, y, c: (z, 1 - x, y, c)),
        "xy": perm(lambda z, x, y, c: (z, 1 - x, 1 - y, c)),
    }
    for r in range(1, nz):
        table[r] = perm(lambda z, x, y, c, r=r: (z ^ r, x, y, c))
    return table


def generic_body(
    tokens,
    cotangent,
    lengths,
    project_matrix,
    output_matrix,
    expand_matrix,
    reduce_matrix,
    biases,
    alphas,
    project_first,
    project_second,
    output_first,
    output_second,
    expand_first,
    expand_second,
    reduce_first,
    reduce_second,
    bias_first,
    bias_second,
    alpha_first,
    alpha_second,
):
    slot_dev, seq_dev, width = tokens.shape
    ctx_index = lax.axis_index("ctx")
    qpos = ctx_index * slot_dev + jnp.arange(slot_dev, dtype=jnp.int32)
    gathered = (
        lax.all_gather(project_matrix.astype(jnp.bfloat16), ("dp", "ctx"), axis=0, tiled=True),
        lax.all_gather(output_matrix.astype(jnp.bfloat16), ("dp", "ctx"), axis=0, tiled=True),
        lax.all_gather(expand_matrix.astype(jnp.bfloat16), ("dp", "ctx"), axis=0, tiled=True),
        lax.all_gather(reduce_matrix.astype(jnp.bfloat16), ("dp", "ctx"), axis=0, tiled=True),
        lax.all_gather(biases.astype(jnp.bfloat16), ("dp", "ctx"), axis=0, tiled=True),
    )
    w_project, w_output, w_expand, w_reduce, bias_all = gathered
    hidden_width = w_expand.shape[1]
    scale = HEAD ** (-0.5)
    flat = tokens.reshape(-1, width)
    query_key_value = jnp.dot(flat, w_project, preferred_element_type=jnp.float32).astype(
        jnp.bfloat16
    )
    query_key_value = query_key_value.reshape(slot_dev, seq_dev, 3 * width)
    query = query_key_value[..., :width].reshape(slot_dev, seq_dev, HEADS, HEAD)
    kv_all = lax.all_gather(query_key_value[..., width:], "ctx", axis=0, tiled=True)
    length = kv_all.shape[0]
    keys = kv_all[..., :width].reshape(length, seq_dev, HEADS, HEAD)
    values = kv_all[..., width:].reshape(length, seq_dev, HEADS, HEAD)
    scores = jnp.einsum("qshe,kshe->shqk", query, keys, preferred_element_type=jnp.float32) * scale
    kpos = jnp.arange(length, dtype=jnp.int32)
    allowed = (kpos[None, None, :] <= qpos[None, :, None]) & (
        kpos[None, None, :] < lengths[:, None, None]
    )
    masked = jnp.where(allowed[:, None], scores, -1e30)
    top = jnp.max(masked, axis=-1, keepdims=True)
    expo = jnp.exp(masked - top)
    prob = expo / jnp.sum(expo, axis=-1, keepdims=True)
    prob_low = prob.astype(jnp.bfloat16)
    attended_rows = jnp.einsum(
        "shqk,kshe->qshe", prob_low, values, preferred_element_type=jnp.float32
    )
    attended_rows = attended_rows.astype(jnp.bfloat16).reshape(slot_dev * seq_dev, width)
    branch_output = jnp.dot(attended_rows, w_output, preferred_element_type=jnp.float32)
    residual_stream = flat.astype(jnp.float32) + alphas[0] * branch_output
    resid_low = residual_stream.astype(jnp.bfloat16)
    bias_float = bias_all.astype(jnp.float32)
    before_activation = (
        jnp.dot(resid_low, w_expand, preferred_element_type=jnp.float32) + bias_float[:hidden_width]
    )
    activate = partial(jax.nn.gelu, approximate=False)
    hidden_rows = activate(before_activation).astype(jnp.bfloat16)
    feed_output = (
        jnp.dot(hidden_rows, w_reduce, preferred_element_type=jnp.float32)
        + bias_float[hidden_width:]
    )
    mixed = (residual_stream + alphas[1] * feed_output).astype(jnp.bfloat16).reshape(tokens.shape)
    valid = (qpos[:, None] < lengths[None, :]).astype(jnp.float32).reshape(-1, 1)
    pull = cotangent.reshape(-1, width).astype(jnp.float32) * valid
    d_ffout = (alphas[1] * pull).astype(jnp.bfloat16)
    g_reduce = jnp.dot(hidden_rows.T, d_ffout, preferred_element_type=jnp.float32)
    g_second_bias = jnp.sum(d_ffout.astype(jnp.float32), axis=0)
    d_hidden = jnp.dot(d_ffout, w_reduce.T, preferred_element_type=jnp.float32)
    d_pre = jax.vjp(activate, before_activation)[1](d_hidden)[0].astype(jnp.bfloat16)
    g_expand = jnp.dot(resid_low.T, d_pre, preferred_element_type=jnp.float32)
    g_first_bias = jnp.sum(d_pre.astype(jnp.float32), axis=0)
    d_resid = pull + jnp.dot(d_pre, w_expand.T, preferred_element_type=jnp.float32)
    g_alpha = jnp.stack([jnp.sum(branch_output * d_resid), jnp.sum(feed_output * pull)])
    d_branch = (alphas[0] * d_resid).astype(jnp.bfloat16)
    g_output = jnp.dot(attended_rows.T, d_branch, preferred_element_type=jnp.float32)
    d_att = jnp.dot(d_branch, w_output.T, preferred_element_type=jnp.float32).astype(jnp.bfloat16)
    d_att = d_att.reshape(slot_dev, seq_dev, HEADS, HEAD)
    d_prob = jnp.einsum("qshe,kshe->shqk", d_att, values, preferred_element_type=jnp.float32)
    d_scores = (prob * (d_prob - jnp.sum(prob * d_prob, axis=-1, keepdims=True))).astype(
        jnp.bfloat16
    )
    d_query = (
        jnp.einsum("shqk,kshe->qshe", d_scores, keys, preferred_element_type=jnp.float32) * scale
    )
    count = lax.axis_size("ctx") * slot_dev
    g_keys = (
        jnp.einsum("shqk,qshe->kshe", d_scores, query, preferred_element_type=jnp.float32) * scale
    )
    g_values = jnp.einsum("shqk,qshe->kshe", prob_low, d_att, preferred_element_type=jnp.float32)
    d_kv = lax.psum_scatter(
        jnp.concatenate(
            [g_keys.reshape(count, seq_dev, width), g_values.reshape(count, seq_dev, width)],
            axis=-1,
        ).astype(jnp.bfloat16),
        "ctx",
        scatter_dimension=0,
        tiled=True,
    ).astype(jnp.float32)
    d_qkv = jnp.concatenate([d_query.reshape(slot_dev, seq_dev, width), d_kv], axis=-1)
    d_qkv = d_qkv.astype(jnp.bfloat16).reshape(-1, 3 * width)
    g_project = jnp.dot(flat.T, d_qkv, preferred_element_type=jnp.float32)
    input_grad = (
        d_resid + jnp.dot(d_qkv, w_project.T, preferred_element_type=jnp.float32)
    ).reshape(tokens.shape)
    g_bias = jnp.concatenate([g_first_bias, g_second_bias])
    devices = lax.axis_size(("dp", "ctx"))
    device_index = lax.axis_index(("dp", "ctx"))
    summed = lax.psum((g_project, g_output, g_expand, g_reduce, g_bias, g_alpha), ("dp", "ctx"))
    squares = jnp.float32(0.0)
    for grad in summed:
        squares = squares + jnp.sum(grad * grad)
    owned = []
    for grad in summed[:5]:
        rows = grad.shape[0] // devices
        owned.append(lax.dynamic_slice_in_dim(grad, device_index * rows, rows, 0))
    alpha_sum = summed[5]
    grad_norm = jnp.sqrt(squares)
    factor = jnp.minimum(1.0, clip_bound / (grad_norm + 1e-06))
    weights = (project_matrix, output_matrix, expand_matrix, reduce_matrix, biases, alphas)
    states = (
        (project_first, project_second),
        (output_first, output_second),
        (expand_first, expand_second),
        (reduce_first, reduce_second),
        (bias_first, bias_second),
        (alpha_first, alpha_second),
    )
    grads = (owned[0], owned[1], owned[2], owned[3], owned[4], alpha_sum)
    rates = (matrix_rate, matrix_rate, matrix_rate, matrix_rate, matrix_rate, alpha_rate)
    decays = (decay_rate, decay_rate, decay_rate, decay_rate, 0.0, 0.0)
    results = []
    for weight, (first, second), grad, rate, decay in zip(weights, states, grads, rates, decays):
        results.extend(adamw(weight, first, second, factor * grad, rate, decay))
    return (
        mixed,
        input_grad,
        results[0],
        results[1],
        results[2],
        results[3],
        results[4],
        results[5],
        results[6],
        results[7],
        results[8],
        results[9],
        results[10],
        results[11],
        results[12],
        results[13],
        results[14],
        results[15],
        results[16],
        results[17],
        grad_norm,
    )


def fast_body(
    tokens,
    cotangent,
    lengths,
    project_matrix,
    output_matrix,
    expand_matrix,
    reduce_matrix,
    biases,
    alphas,
    project_first,
    project_second,
    output_first,
    output_second,
    expand_first,
    expand_second,
    reduce_first,
    reduce_second,
    bias_first,
    bias_second,
    alpha_first,
    alpha_second,
):
    rows, seq_dev, width = tokens.shape
    hidden = expand_matrix.shape[1]
    devices = lax.axis_size(BOTH)
    nz = devices // 8
    seqs = seq_dev // 2
    slots = 4 * rows
    wide = width // 2
    table = routes(nz)

    def move(v, way):
        return lax.ppermute(v, BOTH, table[way])

    def after(v, *deps):
        return lax.optimization_barrier((v,) + deps)[0]

    def at(v, axis, index):
        return lax.dynamic_index_in_dim(v, index, axis, False)

    def add(a, b):
        return a.astype(F32) + b.astype(F32)

    def cost(us):
        return pl.CostEstimate(flops=int(us * 1.1e9), transcendentals=0, bytes_accessed=1 << 20)

    params = pltpu.CompilerParams(vmem_limit_bytes=VMEM_LIMIT)

    def call(kernel, name, us, grid, in_specs, out_specs, out_shape, scratch, *args):
        return pl.pallas_call(
            kernel,
            grid_spec=pltpu.PrefetchScalarGridSpec(
                num_scalar_prefetch=1,
                grid=grid,
                in_specs=in_specs,
                out_specs=out_specs,
                scratch_shapes=scratch,
            ),
            out_shape=out_shape,
            compiler_params=params,
            cost_estimate=cost(us),
            name=name,
        )(*args)

    def shape(dims, kind):
        return jax.ShapeDtypeStruct(dims, kind)

    ctx, dp = lax.axis_index("ctx"), lax.axis_index("dp")
    y, c, z, x = ctx // 2, ctx % 2, dp // 2, dp % 2
    me = dp * 4 + ctx

    x6 = jnp.transpose(tokens, (1, 0, 2))
    c6 = jnp.transpose(cotangent, (1, 0, 2))
    tok = (1, rows, width)

    def flat3(f):
        return pl.BlockSpec(tok, lambda *a: (f(*a), 0, 0))

    r1, r2 = output_matrix.shape[0], reduce_matrix.shape[0]
    groups = hidden // width
    blob_rows = (1 + groups) * r1 + r2 + 16
    bias_rows = jnp.zeros((16 * width,), BF16)
    bias_rows = lax.dynamic_update_slice_in_dim(
        bias_rows, biases.astype(BF16), me * biases.shape[0], 0
    ).reshape(16, width)
    vmem = pl.BlockSpec(memory_space=pltpu.VMEM)
    blob = pl.pallas_call(
        pack,
        in_specs=[vmem] * 4,
        out_specs=vmem,
        out_shape=shape((blob_rows, width), BF16),
        compiler_params=params,
        cost_estimate=cost(1),
        name="pack",
    )(output_matrix, expand_matrix, reduce_matrix, bias_rows)
    bz1 = move(blob, 1)
    x6_o = move(after(x6, blob), "core")

    place = jnp.stack([c, y, z, x]).astype(jnp.int32)
    info, wq_own, wq_give, x_give, c_give = pl.pallas_call(
        prepare,
        in_specs=[SMEM, SMEM, vmem, ANY, ANY],
        out_specs=[SMEM, vmem, vmem, vmem, vmem],
        out_shape=[
            shape((FOUND + seq_dev,), jnp.int32),
            shape((project_matrix.shape[0], 3 * wide), BF16),
            shape((project_matrix.shape[0], 3 * wide), BF16),
            shape((seqs, rows, width), BF16),
            shape((seqs, rows, width), BF16),
        ],
        scratch_shapes=[pltpu.SemaphoreType.DMA((seq_dev,))],
        compiler_params=params,
        cost_estimate=cost(2),
        name="prepare",
    )(after(place, blob), lengths, project_matrix, x6, c6)
    wq_got = move(wq_give, "core")
    wq_chip = jnp.where(
        c == 0, jnp.concatenate([wq_own, wq_got], 0), jnp.concatenate([wq_got, wq_own], 0)
    )
    got = move(after(x_give, bz1, x6_o, wq_chip), "y")
    wz = [move(wq_chip, r) for r in range(1, nz)]
    wa = jnp.stack([wq_chip] + wz)
    bz01 = jnp.stack([blob, bz1])
    bz23 = move(after(bz01, *wz), 2)
    wax, way, wad = move(wa, "x"), move(wa, "y"), move(wa, "xy")
    ba = jnp.concatenate([bz01, after(bz23, wax, way, wad)], 0)
    got_o = move(after(got, ba, wa), "core")
    bax, bay = move(ba, "x"), move(ba, "y")

    def seq_of(s):
        own, other = flat3(lambda *a: a[-1][OWN + s]), flat3(lambda *a: s)
        four = [(x6, own), (got, other), (x6_o, own), (got_o, other)]
        return [f[0] for f in four], [f[1] for f in four]

    o_shape = (1, 2, rows, wide)
    kept = []
    wq_full = None
    fwd_out = [
        shape((1, slots, 3 * wide), BF16),
        shape(o_shape, BF16),
        shape(o_shape, BF16),
        shape((1, 8, slots), F32),
    ]
    for s in range(seqs):
        weight_in = (wa, wax, way, wad) if s == 0 else (wq_full,)
        deps = (ba,) if s == 0 else (kept[-1][3], bax, bay) if s == 1 else (kept[-1][3],)
        x_in, x_specs = seq_of(s)
        outs = ([shape((width, 3 * wide), BF16)] if s == 0 else []) + fwd_out
        res = call(
            partial(attend_forward, s, nz), "attend_forward", 2, (1,),
            x_specs + [whole(v.shape) for v in weight_in],
            [whole(v.shape) for v in outs], outs,
            [pltpu.VMEM((slots, wide), BF16), pltpu.VMEM((slots, 128), F32)],
            after(info, *deps), *x_in, *weight_in)
        if s == 0:
            wq_full = res[0]
            res = res[1:]
        if s == 0:
            bad = move(after(bay, res[3]), "x")
            c_got = move(after(c_give, bay, res[3]), "y")
            ba_o = move(after(ba, res[3]), "core")
        o_give = after(res[2], c_got) if s == seqs - 1 else res[2]
        kept.append(tuple(res) + (move(o_give, "core"),))
        if s == seqs - 1:
            bax_o, bay_o = (move(after(v, kept[1][3]), "core") for v in (bax, bay))
    rail = (ba, bax, bay, bad)
    rail_o = (ba_o, bax_o, bay_o, move(after(bad, kept[1][4], kept[2][4]), "core"))

    def half_block(dims):
        return pl.BlockSpec(dims, lambda t, i: (t // 2, t % 2, 0, 0))

    own_o = [k[1] for k in kept]
    oth_o = [k[4] for k in kept]
    act = half_block((1, 1, rows, wide))
    feed_in = (x6, got, c6, c_got, *own_o, *oth_o, *rail, *rail_o)
    by_seq = flat3(lambda t, i: t // 2)
    by_own = flat3(lambda t, i: i[OWN + t // 2])
    feed_out = [
        shape((seqs, rows, width), BF16),
        shape((seqs, rows, width), BF16),
        shape((seqs, 2, rows, width), F32),
        shape((seqs, 2, rows, wide), BF16),
        shape((seqs, 2, rows, wide), BF16),
        shape((2, 2, 2, nz, blob_rows // 2, width), BF16),
        shape((2, 2, 2, nz, blob_rows // 2, width), BF16),
        shape((8, width), F32),
    ]
    mixed_m, mixed_g, dy, do_keep, do_send, g_send, g_keep, ga = call(
        partial(feed, nz), "feed", 35, (2 * seqs,),
        [SMEM, by_own, by_seq, by_own, by_seq]
        + [whole(v.shape) for v in feed_in[4:]],
        [by_seq, by_seq, half_block((1, 1, rows, width)), act, act] + [whole(v.shape) for v in feed_out[5:]],
        feed_out,
        [
            pltpu.VMEM((width, width), BF16),
            pltpu.VMEM((width, hidden), BF16),
            pltpu.VMEM((hidden, width), BF16),
            pltpu.VMEM((16, width), F32),
            pltpu.VMEM((width, width), F32),
            pltpu.VMEM((width, hidden), F32),
            pltpu.VMEM((hidden, width), F32),
            pltpu.VMEM((8, hidden), F32),
            pltpu.VMEM((8, width), F32),
            pltpu.VMEM((16, width), F32),
            pltpu.VMEM((rows, hidden), BF16),
            pltpu.VMEM((rows, hidden), F32),
            pltpu.VMEM((rows, hidden), BF16),
        ],
        info, alphas, *feed_in)

    do_recv = move(do_send, "core")
    g_recv = move(after(g_send, do_recv), "core")
    mixed_r = move(after(mixed_g, do_recv), "y")

    def backward(s, grad, *deps):
        last = s == seqs - 1
        qkv, ok, osend, lse, _ = kept[s]
        ins = (wq_full, qkv, lse, ok, osend, do_keep, do_recv, dy) + (() if s == 0 else (grad,))
        own = pl.BlockSpec((1, 2, rows, wide), lambda *_: (s, 0, 0, 0))
        specs = [whole(v.shape) for v in ins[:5]]
        specs += [own, own, pl.BlockSpec((1, 2, rows, width), lambda *_: (s, 0, 0, 0))]
        specs += [] if s == 0 else [whole(grad.shape)]
        g_out = [shape((width, 3 * wide), F32)]
        if last:
            g_out = [shape((2, nz, 2 * r1, 3 * wide), F32), shape((2, nz, 2 * r1, 3 * wide), BF16)]
        outs = g_out + [shape((1, 2, rows, width), F32), shape((1, 2, rows, width), BF16)]
        x_in, x_specs = seq_of(s)
        return call(
            partial(attend_backward, s, last), "attend_backward", 13, (1,),
            x_specs + specs, [whole(v.shape) for v in outs], outs,
            [
                pltpu.VMEM((slots, wide), BF16),
                pltpu.VMEM((8, slots), F32),
                pltpu.VMEM((slots, wide), BF16),
                pltpu.VMEM((slots, wide), F32),
                pltpu.VMEM((slots, wide), F32),
            ] + ([pltpu.VMEM((width, 3 * wide), F32)] if last else []),
            after(info, *deps) if deps else info, *x_in, *ins)

    grad, keep0, send0 = backward(0, None)
    g_recv_late = after(g_recv, send0)
    recv0 = move(after(send0, g_recv_late), "core")
    both = add(g_keep, g_recv_late).astype(BF16)
    fa, fb = both[0], both[1]
    ga_send, gb_send = at(fa, 0, 1 - x), at(fb, 0, 1 - y)
    ra, rb = move(ga_send, "x"), move(gb_send, "y")
    grad, keep1, send1 = backward(1, grad, ga_send, gb_send)
    ra, rb = after(ra, send1), after(rb, send1)
    recv1 = move(after(send1, ra, rb), "core")
    fa = add(at(fa, 0, x), ra).astype(BF16)
    fb = add(at(fb, 0, y), rb).astype(BF16)
    ga_send, gb_send = at(fa, 0, 1 - y), at(fb, 0, 1 - x)
    ra, rb = move(ga_send, "y"), move(gb_send, "x")
    got0_grad = (keep0[:, 1] + after(recv0, ga_send)[:, 1].astype(F32)).astype(BF16)
    back0 = move(got0_grad, "y")
    qkeep, qsend, keep2, send2 = backward(2, grad, ga_send, gb_send, got0_grad, mixed_r)
    qr = move(after(qsend, recv1, ra, rb), "x")
    recv2 = move(send2, "core")
    ra, rb = after(ra, qr), after(rb, qr)
    fv = jnp.concatenate([add(at(fa, 0, y), ra), add(at(fb, 0, x), rb)], 1).astype(BF16)
    fgot = [move(at(fv, 0, z ^ r), r) for r in range(1, nz)]
    gq = add(qkeep, qr)
    qr = move(after(at(gq, 0, 1 - y).astype(BF16), back0), "y")
    blob_sum = at(fv, 0, z).astype(F32)
    for g in fgot:
        blob_sum = blob_sum + g.astype(F32)
    back12 = move(
        after(
            jnp.concatenate(
                [(k[:, 1] + r[:, 1].astype(F32)).astype(BF16) for k, r in ((keep1, recv1), (keep2, recv2))],
                0,
            ),
            gq,
        ),
        "y",
    )
    gq = add(at(gq, 0, y), qr)
    qgot = [move(at(gq, 0, z ^ r).astype(BF16), r) for r in range(1, nz)]
    q_own, q_give, tiny = call(
        finish, "finish", 1, (1,),
        [whole(v.shape) for v in (gq, *qgot, blob_sum, ga)],
        [whole((r1, 3 * wide)), whole((r1, 3 * wide)), whole((devices, 128))],
        [shape((r1, 3 * wide), F32), shape((r1, 3 * wide), F32), shape((devices, 128), F32)],
        [], info, gq, *qgot, blob_sum, ga)
    tiny = lax.all_to_all(tiny.reshape(devices, 1, 128), BOTH, 0, 0).reshape(devices, 128)
    q_got = move(q_give, "core")

    half = pl.BlockSpec((1, 1, rows, width), lambda *_: (0, 0, 0, 0))
    mixed6, input6 = call(
        placed, "placed", 4, (1,),
        [whole(mixed_m.shape)] * 2 + [half] * 6 + [whole(back0.shape), whole(back12.shape)],
        [whole((seq_dev, rows, width))] * 2,
        [shape((seq_dev, rows, width), BF16), shape((seq_dev, rows, width), F32)],
        [], info, mixed_m, mixed_r, keep0, keep1, keep2, recv0, recv1, recv2, back0, back12)

    g_bias = lax.dynamic_slice_in_dim(
        blob_sum[blob_rows - 16 :].reshape(-1), me * biases.shape[0], biases.shape[0], 0
    )
    states = (
        project_matrix, project_first, project_second,
        output_matrix, output_first, output_second,
        expand_matrix, expand_first, expand_second,
        reduce_matrix, reduce_first, reduce_second,
        biases[None], bias_first[None], bias_second[None],
        alphas[None], alpha_first[None], alpha_second[None],
    )
    outs = [shape(v.shape, F32) for v in states] + [shape((1, 1), F32)]
    ins = (tiny, q_own, q_got, blob_sum, g_bias[None], *states)
    res = call(
        update, "update", 3, (1,), [whole(v.shape) for v in ins], [whole(v.shape) for v in outs], outs, [],
        after(info, input6), *ins)
    mixed = jnp.transpose(mixed6, (1, 0, 2))
    input_grad = jnp.transpose(input6, (1, 0, 2))
    results = list(res[:12]) + [v[0] for v in res[12:18]]
    return (mixed, input_grad, *results, res[18][0, 0])


def solution(mesh):
    ctx, dp = mesh.shape["ctx"], mesh.shape["dp"]
    row = P(BOTH, None)
    flat = P(BOTH)
    token = P("ctx", "dp", None)
    body = fast_body if (ctx == 4 and dp == 8) else generic_body
    return jax.shard_map(
        body,
        mesh=mesh,
        in_specs=(token, token, P("dp"), row, row, row, row, flat, P())
        + (row,) * 8
        + (flat, flat, P(), P()),
        out_specs=(token, token) + (row,) * 12 + (flat,) * 3 + (P(),) * 4,
        check_vma=False,
    )
```

```python
from functools import partial

import jax
import jax.numpy as jnp
from jax import lax
from jax.experimental import pallas as pl
from jax.experimental.pallas import tpu as pltpu
from jax.sharding import PartitionSpec as P

HEADS = 8
HEAD = 64
STEP = 10


clip_bound = 1.0
beta_one = 0.9
beta_two = 0.999
adam_eps = 1e-08
matrix_rate = 0.05
alpha_rate = 0.2
decay_rate = 0.1

BOTH = ("dp", "ctx")
F32 = jnp.float32
BF16 = jnp.bfloat16
VMEM_LIMIT = 56 * 1024 * 1024


def adamw(weight, first, second, grad, rate, decay):
    first = beta_one * first + (1.0 - beta_one) * grad
    second = beta_two * second + (1.0 - beta_two) * grad * grad
    mhat = first / (1.0 - beta_one**STEP)
    vhat = second / (1.0 - beta_two**STEP)
    weight = weight - rate * (mhat / (jnp.sqrt(vhat) + adam_eps) + decay * weight)
    return (first, second, weight)


def dot_nn(a, b):
    return lax.dot_general(a, b, (((1,), (0,)), ((), ())), preferred_element_type=F32)


def dot_nt(a, b):
    return lax.dot_general(a, b, (((1,), (1,)), ((), ())), preferred_element_type=F32)


def dot_tn(a, b):
    return lax.dot_general(a, b, (((0,), (0,)), ((), ())), preferred_element_type=F32)


CORE, CHIP_Y, CHIP_Z, CHIP_X, LENS, OWN, OTHER, FOUND = 0, 1, 2, 3, 4, 7, 10, 13


def block_places(info, rows):
    core, y = info[CORE], info[CHIP_Y]
    return [
        pl.multiple_of(b * rows, rows)
        for b in (
            2 * y + core,
            2 * (1 - y) + core,
            2 * y + 1 - core,
            2 * (1 - y) + 1 - core,
        )
    ]


def chip_index(info, r, fx, fy):
    z = info[CHIP_Z] ^ r
    x = info[CHIP_X] ^ fx
    y = info[CHIP_Y] ^ fy
    return (z * 2 + x) * 2 + y


PIECES = 4


def gathered_pieces(nz):
    places = ((0, 0), (1, 0), (0, 1), (1, 1))
    return [(i, r, r, fx, fy) for i, (fx, fy) in enumerate(places) for r in range(nz)]


def sequence_copies(s, info, four, x_s, sems):
    own = info[OWN + s]
    at = (own, s, own, s)
    return [pltpu.make_async_copy(v.at[i], x_s.at[b], sems.at[b]) for b, (v, i) in enumerate(zip(four, at))]


def attend_forward(s, nz, info, *refs):
    assemble = s == 0
    refs = list(refs)
    four = [refs.pop(0) for _ in range(4)]
    x_s, qkv_ref, oo_s, sems = refs[-4:]
    refs = refs[:-4]
    copies = sequence_copies(s, info, four, x_s, sems)
    for copy in copies:
        copy.start()
    if assemble:
        pieces = [refs.pop(0) for _ in range(PIECES)]
        wq_ref, qkv_out, ok_out, os_out, lse_ref, o_s, st_s = refs
        rows = pieces[0].shape[1]
        for which, at, r, fx, fy in gathered_pieces(nz):
            place = pl.multiple_of(chip_index(info, r, fx, fy) * rows, rows)
            wq_ref[pl.ds(place, rows), :] = pieces[which][at]
    else:
        wq_ref, qkv_out, ok_out, os_out, lse_ref, o_s, st_s = refs
    length = info[LENS + s]
    rows = x_s.shape[1]
    places = block_places(info, rows)
    w = wq_ref[...]
    for b, place in enumerate(places):
        copies[b].wait()
        qkv_ref[0, pl.ds(place, rows), :] = dot_nn(x_s[b], w).astype(BF16)
    out = pltpu.make_async_copy(qkv_ref, qkv_out, sems.at[4])
    out.start()
    blocks = (length + rows - 1) // rows
    lane = lax.broadcasted_iota(jnp.int32, (rows, 128), 1)
    low_lane = lane < HEAD
    row_i = lax.broadcasted_iota(jnp.int32, (rows, rows), 0)
    col_i = lax.broadcasted_iota(jnp.int32, (rows, rows), 1)

    def one(qb, n, pair):
        at = pair * 128
        wide = 256
        q = qkv_ref[0, qb * rows : (qb + 1) * rows, pl.ds(at, 128)]
        k = qkv_ref[0, 0 : n * rows, pl.ds(wide + at, 128)]
        v = qkv_ref[0, 0 : n * rows, pl.ds(2 * wide + at, 128)]
        vx = jnp.concatenate([v, jnp.ones_like(v)], axis=1)
        base = (n - 1) * rows
        ok = (base + col_i) < length
        if n == qb + 1:
            ok = ok & (col_i <= row_i)
        res = []
        stats = st_s[qb * rows : (qb + 1) * rows, :]
        for h in range(2):
            mine = low_lane if h == 0 else jnp.logical_not(low_lane)
            qm = jnp.where(mine, q * jnp.asarray(HEAD**-0.5, BF16), jnp.zeros_like(q))
            sc = dot_nt(qm, k)
            last = jnp.where(ok, sc[:, base:], -1e30)
            if n > 1:
                sc = jnp.concatenate([sc[:, :base], last], axis=1)
            else:
                sc = last
            top = jnp.max(sc, axis=1, keepdims=True)
            e = jnp.exp(sc - top)
            ob = dot_nn(e.astype(BF16), vx)
            den = ob[:, 128:]
            res.append(ob[:, :128] / den)
            stats = jnp.where(lane == 2 * pair + h, top + jnp.log(den), stats)
        st_s[qb * rows : (qb + 1) * rows, :] = stats
        o_s[qb * rows : (qb + 1) * rows, pl.ds(at, 128)] = jnp.where(
            low_lane, res[0], res[1]
        ).astype(BF16)

    total = qkv_ref.shape[1] // rows
    st_s[...] = jnp.zeros_like(st_s)
    for qb in range(total):
        for n in range(1, qb + 2):
            cond = (blocks == n) if n < qb + 1 else (blocks >= n)

            @pl.when(cond)
            def _(qb=qb, n=n):
                for pair in range(2):
                    one(qb, n, pair)

    for b in range(4):
        oo_s[b // 2, 0, b % 2] = o_s[pl.ds(places[b], rows), :]
    outs = [out]
    for i, dst in ((0, ok_out), (1, os_out)):
        outs.append(pltpu.make_async_copy(oo_s.at[i], dst, sems.at[5 + i]))
        outs[-1].start()
    lse_ref[0] = jnp.transpose(st_s[...])[:8]
    for copy in outs:
        copy.wait()


def attend_backward(s, grad_in, last_one, info, *refs):
    refs = list(refs)
    four = [refs.pop(0) for _ in range(4)]
    wq_ref, qkv_in, lse_in, ok_in, os_in, dk_in, dr_in = (refs.pop(0) for _ in range(7))
    g_in = refs.pop(0) if grad_in else None
    scratch = refs[-15:]
    (do_s, r_s, dq_s, dk_s, dv_s, x_s, w_s, qkv_ref, lse_ref, o_in, d_in, g_ref, keep_ref, send_ref,
     sems) = scratch
    refs = refs[:-15]
    if last_one:
        qkeep_out, qsend_out, keep_out, send_out, qkeep_ref, qsend_ref = refs
    else:
        g_out, keep_out, send_out = refs
    wanted = [
        (dk_in.at[s], d_in.at[0]),
        (dr_in.at[s], d_in.at[1]),
        (ok_in.at[0], o_in.at[0]),
        (os_in.at[0], o_in.at[1]),
        (lse_in, lse_ref),
        (qkv_in, qkv_ref),
        (wq_ref, w_s),
    ]
    if grad_in:
        wanted.append((g_in, g_ref))
    early = [pltpu.make_async_copy(src, dst, sems.at[4 + i]) for i, (src, dst) in enumerate(wanted)]
    late = sequence_copies(s, info, four, x_s, sems) + early[6:]
    early = early[:6]
    for copy in early:
        copy.start()
    for copy in early:
        copy.wait()
    for copy in late:
        copy.start()
    length = info[LENS + s]
    rows = x_s.shape[1]
    places = block_places(info, rows)
    lane = lax.broadcasted_iota(jnp.int32, (rows, 128), 1)
    low_lane = lane < HEAD
    head_of = lax.broadcasted_iota(jnp.int32, (8, 256), 1) // HEAD
    pick = (head_of == lax.broadcasted_iota(jnp.int32, (8, 256), 0)).astype(BF16)
    for b in range(4):
        do = d_in[b // 2, b % 2]
        o = o_in[b // 2, b % 2]
        do_s[pl.ds(places[b], rows), :] = do
        prod = do.astype(F32) * o.astype(F32)
        high = prod.astype(BF16)
        low = (prod - high.astype(F32)).astype(BF16)
        r_s[:, pl.ds(places[b], rows)] = dot_nt(pick, high) + dot_nt(pick, low)
    dk_s[...] = jnp.zeros_like(dk_s)
    dv_s[...] = jnp.zeros_like(dv_s)
    if not grad_in:
        g_ref[...] = jnp.zeros_like(g_ref)
    key_i = lax.broadcasted_iota(jnp.int32, (rows, rows), 0)
    qry_i = lax.broadcasted_iota(jnp.int32, (rows, rows), 1)
    scale = HEAD**-0.5

    def one_all(qb):
        n = qb + 1
        wide = 256
        span = slice(qb * rows, (qb + 1) * rows)
        ok = (key_i <= qry_i) & ((qb * rows + key_i) < length)
        qms, doms, dqs = [], [], [None] * 4
        for pair in range(2):
            at = pair * 128
            q = qkv_ref[0, span, at : at + 128]
            do = do_s[span, at : at + 128]
            for h in range(2):
                mine = low_lane if h == 0 else jnp.logical_not(low_lane)
                qms.append(jnp.where(mine, q * jnp.asarray(scale, BF16), jnp.zeros_like(q)))
                doms.append(jnp.where(mine, do, jnp.zeros_like(do)))
        for kb in range(n):
            keys = slice(kb * rows, (kb + 1) * rows)
            ks = [qkv_ref[0, keys, wide + 128 * pr : wide + 128 * pr + 128] for pr in range(2)]
            vs = [qkv_ref[0, keys, 2 * wide + 128 * pr : 2 * wide + 128 * pr + 128] for pr in range(2)]
            scs = [dot_nt(ks[h // 2], qms[h]) for h in range(4)]
            dps = [dot_nt(vs[h // 2], doms[h]) for h in range(4)]
            ps, dss = [], []
            for h in range(4):
                p = jnp.exp(scs[h] - lse_ref[0, h : h + 1, span])
                if kb == qb:
                    p = jnp.where(ok, p, 0.0)
                dss.append((p * (dps[h] - r_s[h : h + 1, span])).astype(BF16))
                ps.append(p.astype(BF16))
            for pr in range(2):
                at = slice(128 * pr, 128 * pr + 128)
                dv_s[keys, at] += dot_nn(ps[2 * pr], doms[2 * pr]) + dot_nn(ps[2 * pr + 1], doms[2 * pr + 1])
                dk_s[keys, at] += dot_nn(dss[2 * pr], qms[2 * pr]) + dot_nn(dss[2 * pr + 1], qms[2 * pr + 1])
            for h in range(4):
                dqh = dot_tn(dss[h], ks[h // 2])
                dqs[h] = dqh if dqs[h] is None else dqs[h] + dqh
        for pr in range(2):
            dq_s[span, 128 * pr : 128 * pr + 128] = (
                jnp.where(low_lane, dqs[2 * pr], dqs[2 * pr + 1]) * scale
            ).astype(BF16)

    total = qkv_ref.shape[1] // rows
    for qb in range(total):

        @pl.when(qb * rows < length)
        def _(qb=qb):
            one_all(qb)

    for copy in late:
        copy.wait()
    w = w_s[...]
    outs = []

    def send_out_copy(src, dst):
        outs.append(pltpu.make_async_copy(src, dst, sems.at[13 + len(outs)]))
        outs[-1].start()

    for b in (2, 3, 0, 1):
        place = places[b]
        here = pl.ds(place, rows)

        @pl.when(place < length)
        def _(b=b, here=here):
            d = jnp.concatenate(
                [dq_s[here, :], dk_s[here, :].astype(BF16), dv_s[here, :].astype(BF16)], axis=1
            )
            g_ref[...] += dot_tn(x_s[b], d)
            dx = dot_nt(d, w)
            if b < 2:
                keep_ref[b] = dx.astype(BF16)
            else:
                send_ref[b - 2] = dx.astype(BF16)

        @pl.when(place >= length)
        def _(b=b):
            if b < 2:
                keep_ref[b] = jnp.zeros_like(keep_ref[b])
            else:
                send_ref[b - 2] = jnp.zeros_like(send_ref[b - 2])

        if b == 3:
            send_out_copy(send_ref, send_out.at[0])
        if b == 0:
            send_out_copy(keep_ref.at[0], keep_out.at[0, 0])
    if last_one:
        nz = qkeep_ref.shape[1]
        part = g_ref.shape[0] // (nz * 4)
        for out, dst, fx in ((qsend_ref, qsend_out, 1), (qkeep_ref, qkeep_out, 0)):
            for r in range(nz):
                for fy in range(2):
                    at = pl.multiple_of(chip_index(info, r, fx, fy) * part, part)
                    out[fy, r] = g_ref[pl.ds(at, part), :].astype(out.dtype)
            send_out_copy(out, dst)
    else:
        send_out_copy(g_ref, g_out)
    send_out_copy(keep_ref.at[1], keep_out.at[0, 1])
    for copy in outs:
        copy.wait()


def feed(nz, info, alphas, *refs):
    refs = list(refs)
    xm, xg, cm, cg = (refs.pop(0) for _ in range(4))
    own_o = [refs.pop(0) for _ in range(3)]
    oth_o = [refs.pop(0) for _ in range(3)]
    rails = [[refs.pop(0) for _ in range(PIECES)] for _ in range(2)]
    (mixm, mixg, dy_ref, dkeep, dsend, gsend, gkeep, ga_ref,
     wo_s, w1_s, w2_s, b_s, go_s, g1_s, g2_s, gb1_s, gb2_s, ga_s,
     h_s, gp_s, yb_s, br_s, f_s, oo_s) = refs
    step = s = pl.program_id(0)
    core = info[CORE]
    chips = nz * 4
    width = wo_s.shape[1]
    groups = w1_s.shape[1] // width
    r1 = wo_s.shape[0] // (2 * chips)
    r2 = w2_s.shape[0] // (2 * chips)

    @pl.when(step == 0)
    def _():
        bias = None
        for rail in range(2):
            for which, at, r, fx, fy in gathered_pieces(nz):
                d = chip_index(info, r, fx, fy) * 2 + (core ^ rail)
                piece = rails[rail][which]
                small = pl.ds(pl.multiple_of(d * r1, r1), r1)
                wo_s[small, :] = piece[at, 0:r1]
                for j in range(groups):
                    w1_s[small, j * width : (j + 1) * width] = piece[at, (1 + j) * r1 : (2 + j) * r1]
                first = (1 + groups) * r1
                w2_s[pl.ds(pl.multiple_of(d * r2, r2), r2), :] = piece[at, first : first + r2]
                part = piece[at, first + r2 : first + r2 + 16].astype(F32)
                bias = part if bias is None else bias + part
        b_s[...] = bias
        for ref in (go_s, g1_s, g2_s, gb1_s, gb2_s, ga_s):
            ref[...] = jnp.zeros_like(ref)

    rows = xm.shape[1]
    both = 2 * rows
    y_here = info[CHIP_Y]
    length = info[LENS + s]
    begins = [(2 * y_here + core) * rows, (2 * (1 - y_here) + core) * rows]

    def pick3(three):
        return jnp.where(s == 0, three[0][0], jnp.where(s == 1, three[1][0], three[2][0])).reshape(both, -1)

    here = pl.ds(pl.multiple_of(core * 256, 256), 256)
    there = pl.ds(pl.multiple_of((1 - core) * 256, 256), 256)
    a0, a1 = alphas[0], alphas[1]
    oo_s[0] = pick3(own_o)
    oo_s[1] = pick3(oth_o)
    x = jnp.concatenate([xm[0], xg[0]], axis=0).astype(F32)
    branch = dot_nn(oo_s[0], wo_s[here, :]) + dot_nn(oo_s[1], wo_s[there, :])
    y = x + a0 * branch
    br_s[...] = branch
    yb = y.astype(BF16)
    yb_s[...] = yb
    f = None
    for j in range(groups):
        cols = slice(j * width, (j + 1) * width)
        pre = dot_nn(yb, w1_s[:, cols]) + b_s[j : j + 1, :]
        cdf = 0.5 + 0.5 * lax.erf(pre * (0.5**0.5))
        h = (pre * cdf).astype(BF16)
        h_s[:, cols] = h
        gp_s[:, cols] = cdf + pre * (jnp.exp(-0.5 * pre * pre) * 0.3989422804014327)
        part = dot_nn(h, w2_s[cols, :])
        f = part if f is None else f + part
    f = f + b_s[groups : groups + 1, :]
    f_s[...] = f
    mixed = (y + a1 * f).astype(BF16)
    mixm[0] = mixed[:rows]
    mixg[0] = mixed[rows:]

    def back(at, count, cot, begin_rows):
        span = pl.ds(at, count)
        g = jnp.where(begin_rows < length, cot.astype(F32), 0.0)
        df = (a1 * g).astype(BF16)
        gb2_s[...] += jnp.sum(df.astype(F32).reshape(count // 8, 8, width), axis=0)
        yb = yb_s[span, :]
        dy = g
        for j in range(groups):
            cols = slice(j * width, (j + 1) * width)
            dh = dot_nt(df, w2_s[cols, :])
            dpre = (dh * gp_s[span, cols]).astype(BF16)
            gb1_s[:, cols] += jnp.sum(dpre.astype(F32).reshape(count // 8, 8, width), axis=0)
            g2_s[cols, :] += dot_tn(h_s[span, cols], df)
            g1_s[:, cols] += dot_tn(yb, dpre)
            dy = dy + dot_nt(dpre, w1_s[:, cols])
        ga_s[0:8, :] += jnp.sum((br_s[span, :] * dy).reshape(count // 8, 8, width), axis=0)
        ga_s[8:16, :] += jnp.sum((f_s[span, :] * g).reshape(count // 8, 8, width), axis=0)
        db = (a0 * dy).astype(BF16)
        go_s[here, :] += dot_tn(oo_s[0, span, :], db)
        go_s[there, :] += dot_tn(oo_s[1, span, :], db)
        return dy, dot_nt(db, wo_s[here, :]).astype(BF16), dot_nt(db, wo_s[there, :]).astype(BF16)

    late = jnp.maximum(begins[0], begins[1])
    early = jnp.minimum(begins[0], begins[1])
    row = lax.broadcasted_iota(jnp.int32, (rows, width), 0)

    @pl.when(late < length)
    def _():
        where = jnp.concatenate([begins[0] + row, begins[1] + row], axis=0)
        dy, keep, send = back(0, both, jnp.concatenate([cm[0], cg[0]], axis=0), where)
        dy_ref[0] = dy.reshape(2, rows, width)
        dkeep[0] = keep.reshape(2, rows, -1)
        dsend[0] = send.reshape(2, rows, -1)

    @pl.when(late >= length)
    def _():
        dkeep[...] = jnp.zeros_like(dkeep)
        dsend[...] = jnp.zeros_like(dsend)
        dy_ref[...] = jnp.zeros_like(dy_ref)

        @pl.when(early < length)
        def _():
            half = pl.multiple_of(y_here * rows, rows)
            cot = jnp.where(y_here == 0, cm[0], cg[0])
            dy, keep, send = back(half, rows, cot, early + row)
            dy_ref[0, y_here] = dy
            dkeep[0, y_here] = keep
            dsend[0, y_here] = send

    @pl.when(step == pl.num_programs(0) - 1)
    def _():
        gb = jnp.concatenate(
            [jnp.sum(gb1_s[:, j * width : (j + 1) * width], axis=0, keepdims=True) for j in range(groups)]
            + [jnp.sum(gb2_s[...], axis=0, keepdims=True), jnp.zeros((16 - groups - 1, width), F32)],
            axis=0,
        ).astype(BF16)
        for out, whose in ((gkeep, core), (gsend, 1 - core)):
            for r in range(nz):
                for fx in range(2):
                    for fy in range(2):
                        d = chip_index(info, r, fx, fy) * 2 + whose
                        small = pl.ds(pl.multiple_of(d * r1, r1), r1)
                        out[0, fx, fy, r, 0:r1] = go_s[small, :].astype(BF16)
                        for j in range(groups):
                            out[0, fx, fy, r, (1 + j) * r1 : (2 + j) * r1] = g1_s[
                                small, j * width : (j + 1) * width
                            ].astype(BF16)
                        out[1, fy, fx, r, 0:r2] = g2_s[
                            pl.ds(pl.multiple_of(d * r2, r2), r2), :
                        ].astype(BF16)
                        out[1, fy, fx, r, r2 : r2 + 16] = gb
        ga_ref[0:1, :] = jnp.sum(ga_s[0:8, :], axis=0, keepdims=True)
        ga_ref[1:2, :] = jnp.sum(ga_s[8:16, :], axis=0, keepdims=True)


def prepare(place, lengths, wq, x_ref, c_ref, info, w_own, w_give, xg_ref, cg_ref, sems):
    six = lengths.shape[0]
    seqs = six // 2
    y = place[1]
    for i in range(4):
        info[i] = place[i]
    ranks = []
    for i in range(six):
        rank = jnp.int32(0)
        for j in range(six):
            if j != i:
                longer = lengths[j] >= lengths[i] if j < i else lengths[j] > lengths[i]
                rank = rank + longer.astype(jnp.int32)
        ranks.append(rank)
    order = [0] + list(range(3, six, 2)) + [1] + list(range(2, six, 2))
    ids = []
    for r in order:
        ids.append(sum(jnp.where(ranks[i] == r, i, 0) for i in range(six)))
    own = [jnp.where(y == 0, ids[s], ids[seqs + s]) for s in range(seqs)]
    other = [jnp.where(y == 0, ids[seqs + s], ids[s]) for s in range(seqs)]
    copies = []
    for s in range(seqs):
        copies.append(pltpu.make_async_copy(x_ref.at[other[s]], xg_ref.at[s], sems.at[s]))
        copies.append(pltpu.make_async_copy(c_ref.at[other[s]], cg_ref.at[s], sems.at[seqs + s]))
    for copy in copies:
        copy.start()
    for s in range(seqs):
        info[LENS + s] = lengths[own[s]]
        info[OWN + s] = own[s]
        info[OTHER + s] = other[s]
    for s in range(seqs):
        info[FOUND + own[s]] = s
        info[FOUND + other[s]] = seqs + s
    wide = wq.shape[1] // 6
    core = place[0]
    for j in range(3):
        left = wq[:, 2 * j * wide : (2 * j + 1) * wide]
        right = wq[:, (2 * j + 1) * wide : (2 * j + 2) * wide]
        cols = slice(j * wide, (j + 1) * wide)
        w_own[:, cols] = jnp.where(core == 0, left, right).astype(BF16)
        w_give[:, cols] = jnp.where(core == 0, right, left).astype(BF16)
    for copy in copies:
        copy.wait()


def pack(wo, w1, w2, bias, out):
    rows, width = wo.shape
    groups = w1.shape[1] // width
    out[0:rows] = wo[...].astype(BF16)
    for j in range(groups):
        out[(1 + j) * rows : (2 + j) * rows] = w1[:, j * width : (j + 1) * width].astype(BF16)
    first = (1 + groups) * rows
    out[first : first + w2.shape[0]] = w2[...].astype(BF16)
    out[first + w2.shape[0] :] = bias[...]


def finish(info, gq, r1, r2, r3, fv, f1, f2, f3, ga, q_own, q_give, tiny, blob):
    total = gq[0]
    for r in (r1, r2, r3):
        total = total + r[...].astype(F32)
    rows = q_own.shape[0]
    core = info[CORE]
    tiny_rows = tiny.shape[0]
    sums = jnp.sum(total * total)
    blob[...] = fv[0].astype(F32) + f1[...].astype(F32) + f2[...].astype(F32) + f3[...].astype(F32)
    main = blob.shape[0] - 16
    own = blob[0:main, :]
    sums = sums + jnp.sum(own * own)
    me = ((info[CHIP_Z] * 2 + info[CHIP_X]) * 2 + info[CHIP_Y]) * 2 + core
    bias = blob[main:, :]
    width = bias.shape[1]
    count = 5 * width // tiny_rows
    flat = lax.broadcasted_iota(jnp.int32, bias.shape, 0) * width + lax.broadcasted_iota(
        jnp.int32, bias.shape, 1
    )
    ours = (flat >= me * count) & (flat < (me + 1) * count)
    sums = sums + jnp.sum(jnp.where(ours, bias * bias, 0.0))
    low, high = total[:rows], total[rows:]
    q_own[...] = jnp.where(core == 0, low, high)
    q_give[...] = jnp.where(core == 0, high, low)
    lane = lax.broadcasted_iota(jnp.int32, tiny.shape, 1)
    a0, a1 = jnp.sum(ga[0:1, :]), jnp.sum(ga[1:2, :])
    tiny[...] = jnp.where(lane == 0, sums, jnp.where(lane == 1, a0, jnp.where(lane == 2, a1, 0.0)))


def placed(info, mixm, mixr, dy, k0, k1, k2, r0, r1, r2, mixed, grad):
    for s in range(mixm.shape[0]):
        mixed[info[OWN + s]] = mixm[s]
        mixed[info[OTHER + s]] = mixr[s]
    for s, (k, r) in enumerate(((k0, r0), (k1, r1), (k2, r2))):
        grad[info[OWN + s]] = dy[s, 0] + (k[0, 0].astype(F32) + r[0, 0].astype(F32))


def placed_rest(info, back, grad_in, grad):
    grad[0] = back[0].astype(F32)


def update(info, tiny, q_own, q_got, blob, g_bias, *refs):
    ins, outs = refs[:18], refs[18:]
    squares = jnp.sum(tiny[:, 0:1])
    a0, a1 = jnp.sum(tiny[:, 1:2]), jnp.sum(tiny[:, 2:3])
    norm = jnp.sqrt(jnp.zeros((1, 1), F32) + (squares + a0 * a0 + a1 * a1))
    factor = jnp.minimum(1.0, clip_bound / (norm + 1e-06))
    outs[18][...] = norm
    rows = q_own.shape[0]
    wide = q_own.shape[1] // 3

    def put(i, place, grad, rate, decay):
        if grad.ndim == 1:
            f = jnp.zeros(grad.shape, F32) + factor[0, 0]
        else:
            f = factor
        res = adamw(ins[3 * i][place], ins[3 * i + 1][place], ins[3 * i + 2][place], f * grad, rate, decay)
        for j in range(3):
            outs[3 * i + j][place] = res[j]

    core = info[CORE]
    for j in range(3):
        left = q_own[:, j * wide : (j + 1) * wide]
        right = q_got[:, j * wide : (j + 1) * wide]
        both = (jnp.where(core == 0, left, right), jnp.where(core == 0, right, left))
        for k in range(2):
            at = (2 * j + k) * wide
            put(0, (slice(None), slice(at, at + wide)), both[k], matrix_rate, decay_rate)
    width = blob.shape[1]
    groups = ins[6].shape[1] // width
    put(1, (slice(None), slice(None)), blob[0:rows, :], matrix_rate, decay_rate)
    for j in range(groups):
        put(2, (slice(None), slice(j * width, (j + 1) * width)), blob[(1 + j) * rows : (2 + j) * rows, :],
            matrix_rate, decay_rate)
    first = (1 + groups) * rows
    put(3, (slice(None), slice(None)), blob[first : first + ins[9].shape[0], :], matrix_rate, decay_rate)
    put(4, (slice(None), slice(None)), g_bias[...], matrix_rate, 0.0)
    lane = lax.broadcasted_iota(jnp.int32, (1, 2), 1)
    put(5, (slice(None), slice(None)), jnp.where(lane == 0, a0, a1), alpha_rate, 0.0)


def whole(shape):
    return pl.BlockSpec(shape, lambda *_: (0,) * len(shape))


SMEM = pl.BlockSpec(memory_space=pltpu.SMEM)
ANY = pl.BlockSpec(memory_space=pl.ANY)


def routes(nz):
    def perm(to):
        out = []
        for z in range(nz):
            for x in range(2):
                for y in range(2):
                    for c in range(2):
                        z2, x2, y2, c2 = to(z, x, y, c)
                        out.append((((z * 2 + x) * 4 + y * 2 + c), ((z2 * 2 + x2) * 4 + y2 * 2 + c2)))
        return out

    table = {
        "core": perm(lambda z, x, y, c: (z, x, y, 1 - c)),
        "y": perm(lambda z, x, y, c: (z, x, 1 - y, c)),
        "x": perm(lambda z, x, y, c: (z, 1 - x, y, c)),
        "xy": perm(lambda z, x, y, c: (z, 1 - x, 1 - y, c)),
    }
    for r in range(1, nz):
        table[r] = perm(lambda z, x, y, c, r=r: (z ^ r, x, y, c))
    return table


def generic_body(
    tokens,
    cotangent,
    lengths,
    project_matrix,
    output_matrix,
    expand_matrix,
    reduce_matrix,
    biases,
    alphas,
    project_first,
    project_second,
    output_first,
    output_second,
    expand_first,
    expand_second,
    reduce_first,
    reduce_second,
    bias_first,
    bias_second,
    alpha_first,
    alpha_second,
):
    slot_dev, seq_dev, width = tokens.shape
    ctx_index = lax.axis_index("ctx")
    qpos = ctx_index * slot_dev + jnp.arange(slot_dev, dtype=jnp.int32)
    gathered = (
        lax.all_gather(project_matrix.astype(jnp.bfloat16), ("dp", "ctx"), axis=0, tiled=True),
        lax.all_gather(output_matrix.astype(jnp.bfloat16), ("dp", "ctx"), axis=0, tiled=True),
        lax.all_gather(expand_matrix.astype(jnp.bfloat16), ("dp", "ctx"), axis=0, tiled=True),
        lax.all_gather(reduce_matrix.astype(jnp.bfloat16), ("dp", "ctx"), axis=0, tiled=True),
        lax.all_gather(biases.astype(jnp.bfloat16), ("dp", "ctx"), axis=0, tiled=True),
    )
    w_project, w_output, w_expand, w_reduce, bias_all = gathered
    hidden_width = w_expand.shape[1]
    scale = HEAD ** (-0.5)
    flat = tokens.reshape(-1, width)
    query_key_value = jnp.dot(flat, w_project, preferred_element_type=jnp.float32).astype(
        jnp.bfloat16
    )
    query_key_value = query_key_value.reshape(slot_dev, seq_dev, 3 * width)
    query = query_key_value[..., :width].reshape(slot_dev, seq_dev, HEADS, HEAD)
    kv_all = lax.all_gather(query_key_value[..., width:], "ctx", axis=0, tiled=True)
    length = kv_all.shape[0]
    keys = kv_all[..., :width].reshape(length, seq_dev, HEADS, HEAD)
    values = kv_all[..., width:].reshape(length, seq_dev, HEADS, HEAD)
    scores = jnp.einsum("qshe,kshe->shqk", query, keys, preferred_element_type=jnp.float32) * scale
    kpos = jnp.arange(length, dtype=jnp.int32)
    allowed = (kpos[None, None, :] <= qpos[None, :, None]) & (
        kpos[None, None, :] < lengths[:, None, None]
    )
    masked = jnp.where(allowed[:, None], scores, -1e30)
    top = jnp.max(masked, axis=-1, keepdims=True)
    expo = jnp.exp(masked - top)
    prob = expo / jnp.sum(expo, axis=-1, keepdims=True)
    prob_low = prob.astype(jnp.bfloat16)
    attended_rows = jnp.einsum(
        "shqk,kshe->qshe", prob_low, values, preferred_element_type=jnp.float32
    )
    attended_rows = attended_rows.astype(jnp.bfloat16).reshape(slot_dev * seq_dev, width)
    branch_output = jnp.dot(attended_rows, w_output, preferred_element_type=jnp.float32)
    residual_stream = flat.astype(jnp.float32) + alphas[0] * branch_output
    resid_low = residual_stream.astype(jnp.bfloat16)
    bias_float = bias_all.astype(jnp.float32)
    before_activation = (
        jnp.dot(resid_low, w_expand, preferred_element_type=jnp.float32) + bias_float[:hidden_width]
    )
    activate = partial(jax.nn.gelu, approximate=False)
    hidden_rows = activate(before_activation).astype(jnp.bfloat16)
    feed_output = (
        jnp.dot(hidden_rows, w_reduce, preferred_element_type=jnp.float32)
        + bias_float[hidden_width:]
    )
    mixed = (residual_stream + alphas[1] * feed_output).astype(jnp.bfloat16).reshape(tokens.shape)
    valid = (qpos[:, None] < lengths[None, :]).astype(jnp.float32).reshape(-1, 1)
    pull = cotangent.reshape(-1, width).astype(jnp.float32) * valid
    d_ffout = (alphas[1] * pull).astype(jnp.bfloat16)
    g_reduce = jnp.dot(hidden_rows.T, d_ffout, preferred_element_type=jnp.float32)
    g_second_bias = jnp.sum(d_ffout.astype(jnp.float32), axis=0)
    d_hidden = jnp.dot(d_ffout, w_reduce.T, preferred_element_type=jnp.float32)
    d_pre = jax.vjp(activate, before_activation)[1](d_hidden)[0].astype(jnp.bfloat16)
    g_expand = jnp.dot(resid_low.T, d_pre, preferred_element_type=jnp.float32)
    g_first_bias = jnp.sum(d_pre.astype(jnp.float32), axis=0)
    d_resid = pull + jnp.dot(d_pre, w_expand.T, preferred_element_type=jnp.float32)
    g_alpha = jnp.stack([jnp.sum(branch_output * d_resid), jnp.sum(feed_output * pull)])
    d_branch = (alphas[0] * d_resid).astype(jnp.bfloat16)
    g_output = jnp.dot(attended_rows.T, d_branch, preferred_element_type=jnp.float32)
    d_att = jnp.dot(d_branch, w_output.T, preferred_element_type=jnp.float32).astype(jnp.bfloat16)
    d_att = d_att.reshape(slot_dev, seq_dev, HEADS, HEAD)
    d_prob = jnp.einsum("qshe,kshe->shqk", d_att, values, preferred_element_type=jnp.float32)
    d_scores = (prob * (d_prob - jnp.sum(prob * d_prob, axis=-1, keepdims=True))).astype(
        jnp.bfloat16
    )
    d_query = (
        jnp.einsum("shqk,kshe->qshe", d_scores, keys, preferred_element_type=jnp.float32) * scale
    )
    count = lax.axis_size("ctx") * slot_dev
    g_keys = (
        jnp.einsum("shqk,qshe->kshe", d_scores, query, preferred_element_type=jnp.float32) * scale
    )
    g_values = jnp.einsum("shqk,qshe->kshe", prob_low, d_att, preferred_element_type=jnp.float32)
    d_kv = lax.psum_scatter(
        jnp.concatenate(
            [g_keys.reshape(count, seq_dev, width), g_values.reshape(count, seq_dev, width)],
            axis=-1,
        ).astype(jnp.bfloat16),
        "ctx",
        scatter_dimension=0,
        tiled=True,
    ).astype(jnp.float32)
    d_qkv = jnp.concatenate([d_query.reshape(slot_dev, seq_dev, width), d_kv], axis=-1)
    d_qkv = d_qkv.astype(jnp.bfloat16).reshape(-1, 3 * width)
    g_project = jnp.dot(flat.T, d_qkv, preferred_element_type=jnp.float32)
    input_grad = (
        d_resid + jnp.dot(d_qkv, w_project.T, preferred_element_type=jnp.float32)
    ).reshape(tokens.shape)
    g_bias = jnp.concatenate([g_first_bias, g_second_bias])
    devices = lax.axis_size(("dp", "ctx"))
    device_index = lax.axis_index(("dp", "ctx"))
    summed = lax.psum((g_project, g_output, g_expand, g_reduce, g_bias, g_alpha), ("dp", "ctx"))
    squares = jnp.float32(0.0)
    for grad in summed:
        squares = squares + jnp.sum(grad * grad)
    owned = []
    for grad in summed[:5]:
        rows = grad.shape[0] // devices
        owned.append(lax.dynamic_slice_in_dim(grad, device_index * rows, rows, 0))
    alpha_sum = summed[5]
    grad_norm = jnp.sqrt(squares)
    factor = jnp.minimum(1.0, clip_bound / (grad_norm + 1e-06))
    weights = (project_matrix, output_matrix, expand_matrix, reduce_matrix, biases, alphas)
    states = (
        (project_first, project_second),
        (output_first, output_second),
        (expand_first, expand_second),
        (reduce_first, reduce_second),
        (bias_first, bias_second),
        (alpha_first, alpha_second),
    )
    grads = (owned[0], owned[1], owned[2], owned[3], owned[4], alpha_sum)
    rates = (matrix_rate, matrix_rate, matrix_rate, matrix_rate, matrix_rate, alpha_rate)
    decays = (decay_rate, decay_rate, decay_rate, decay_rate, 0.0, 0.0)
    results = []
    for weight, (first, second), grad, rate, decay in zip(weights, states, grads, rates, decays):
        results.extend(adamw(weight, first, second, factor * grad, rate, decay))
    return (
        mixed,
        input_grad,
        results[0],
        results[1],
        results[2],
        results[3],
        results[4],
        results[5],
        results[6],
        results[7],
        results[8],
        results[9],
        results[10],
        results[11],
        results[12],
        results[13],
        results[14],
        results[15],
        results[16],
        results[17],
        grad_norm,
    )


def cost(us):
    return pl.CostEstimate(flops=int(us * 1.1e9), transcendentals=0, bytes_accessed=1 << 20)


def params():
    return pltpu.CompilerParams(vmem_limit_bytes=VMEM_LIMIT)


def call(kernel, name, us, grid, in_specs, out_specs, out_shape, scratch, *args):
    return pl.pallas_call(
        kernel,
        grid_spec=pltpu.PrefetchScalarGridSpec(
            num_scalar_prefetch=1,
            grid=grid,
            in_specs=in_specs,
            out_specs=out_specs,
            scratch_shapes=scratch,
        ),
        out_shape=out_shape,
        compiler_params=params(),
        cost_estimate=cost(us),
        name=name,
    )(*args)


def shape(dims, kind):
    return jax.ShapeDtypeStruct(dims, kind)


def token_block(rows, width, f):
    return pl.BlockSpec((1, rows, width), lambda *a: (f(*a), 0, 0))


VMEM = pl.BlockSpec(memory_space=pltpu.VMEM)


def call_once(kernel, name, us, limit, in_specs, out_specs, out_shape, scratch, *args):
    return pl.pallas_call(
        kernel,
        in_specs=in_specs,
        out_specs=out_specs,
        out_shape=out_shape,
        scratch_shapes=scratch,
        compiler_params=pltpu.CompilerParams(vmem_limit_bytes=limit << 20),
        cost_estimate=cost(us),
        name=name,
    )(*args)


def forward_call(s, nz, info, x6, got, x6_o, got_o, *weight_in):
    rows, width = x6.shape[1:]
    wide, slots = width // 2, 4 * rows
    o_shape = (1, 2, rows, wide)
    outs = [shape((width, 3 * wide), BF16)] if s == 0 else []
    outs += [
        shape((1, slots, 3 * wide), BF16),
        shape(o_shape, BF16),
        shape(o_shape, BF16),
        shape((1, 8, slots), F32),
    ]
    return call_once(
        partial(attend_forward, s, nz), "attend_forward", 2, 58,
        [SMEM] + [ANY] * 4 + [VMEM] * len(weight_in),
        [VMEM] * (len(outs) - 4) + [ANY] * 3 + [VMEM], outs,
        [
            pltpu.VMEM((slots, wide), BF16),
            pltpu.VMEM((slots, 128), F32),
            pltpu.VMEM((4, rows, width), BF16),
            pltpu.VMEM((1, slots, 3 * wide), BF16),
            pltpu.VMEM((2,) + o_shape, BF16),
            pltpu.SemaphoreType.DMA((7,)),
        ],
        info, x6, got, x6_o, got_o, *weight_in)


def backward_call(s, last, info, x6, got, x6_o, got_o, *ins):
    rows, width = x6.shape[1:]
    wide, slots = width // 2, 4 * rows
    r1 = width // 32
    grad_in = len(ins) > 7
    g_out = [shape((width, 3 * wide), F32)]
    if last:
        nz = 4
        g_out = [shape((2, nz, 2 * r1, 3 * wide), F32), shape((2, nz, 2 * r1, 3 * wide), BF16)]
    outs = g_out + [shape((1, 2, rows, width), BF16)] * 2
    return call_once(
        partial(attend_backward, s, grad_in, last), "attend_backward", 1, 32 if grad_in else 58,
        [SMEM] + [ANY] * (4 + len(ins)), [ANY] * len(outs), outs,
        ([pltpu.VMEM(v.shape, v.dtype) for v in g_out] if last else []) + [
            pltpu.VMEM((slots, wide), BF16),
            pltpu.VMEM((8, slots), F32),
            pltpu.VMEM((slots, wide), BF16),
            pltpu.VMEM((slots, wide), F32),
            pltpu.VMEM((slots, wide), F32),
            pltpu.VMEM((4, rows, width), BF16),
            pltpu.VMEM((width, 3 * wide), BF16),
            pltpu.VMEM((1, slots, 3 * wide), BF16),
            pltpu.VMEM((1, 8, slots), F32),
            pltpu.VMEM((2, 2, rows, wide), BF16),
            pltpu.VMEM((2, 2, rows, wide), BF16),
            pltpu.VMEM((width, 3 * wide), F32),
            pltpu.VMEM((2, rows, width), BF16),
            pltpu.VMEM((2, rows, width), BF16),
            pltpu.SemaphoreType.DMA((19,)),
        ],
        info, x6, got, x6_o, got_o, *ins)


def feed_call(info, alphas, x6, got, c6, c_got, *rest):
    seqs, rows, width = got.shape
    wide = width // 2
    rails = rest[2 * seqs :]
    nz, blob_rows = rails[0].shape[:2]
    devices = nz * 8
    r1 = width // devices
    hidden = ((blob_rows - 16) // r1 - 1) // 2 * width
    act = pl.BlockSpec((1, 2, rows, wide), lambda t, i: (t, 0, 0, 0))
    pair = pl.BlockSpec((1, 2, rows, width), lambda t, i: (t, 0, 0, 0))
    by_seq = token_block(rows, width, lambda t, i: t)
    by_own = token_block(rows, width, lambda t, i: i[OWN + t])
    outs = [
        shape((seqs, rows, width), BF16),
        shape((seqs, rows, width), BF16),
        shape((seqs, 2, rows, width), F32),
        shape((seqs, 2, rows, wide), BF16),
        shape((seqs, 2, rows, wide), BF16),
        shape((2, 2, 2, nz, blob_rows // 2, width), BF16),
        shape((2, 2, 2, nz, blob_rows // 2, width), BF16),
        shape((8, width), F32),
    ]
    return call(
        partial(feed, nz), "feed", 35, (seqs,),
        [SMEM, by_own, by_seq, by_own, by_seq] + [whole(v.shape) for v in rest],
        [by_seq, by_seq, pair, act, act] + [whole(v.shape) for v in outs[5:]],
        outs,
        [
            pltpu.VMEM((width, width), BF16),
            pltpu.VMEM((width, hidden), BF16),
            pltpu.VMEM((hidden, width), BF16),
            pltpu.VMEM((16, width), F32),
            pltpu.VMEM((width, width), F32),
            pltpu.VMEM((width, hidden), F32),
            pltpu.VMEM((hidden, width), F32),
            pltpu.VMEM((8, hidden), F32),
            pltpu.VMEM((8, width), F32),
            pltpu.VMEM((16, width), F32),
            pltpu.VMEM((2 * rows, hidden), BF16),
            pltpu.VMEM((2 * rows, hidden), F32),
            pltpu.VMEM((2 * rows, width), BF16),
            pltpu.VMEM((2 * rows, width), F32),
            pltpu.VMEM((2 * rows, width), F32),
            pltpu.VMEM((2, 2 * rows, wide), BF16),
        ],
        info, alphas, x6, got, c6, c_got, *rest)


def fast_body(
    tokens,
    cotangent,
    lengths,
    project_matrix,
    output_matrix,
    expand_matrix,
    reduce_matrix,
    biases,
    alphas,
    project_first,
    project_second,
    output_first,
    output_second,
    expand_first,
    expand_second,
    reduce_first,
    reduce_second,
    bias_first,
    bias_second,
    alpha_first,
    alpha_second,
):
    rows, seq_dev, width = tokens.shape
    hidden = expand_matrix.shape[1]
    devices = lax.axis_size(BOTH)
    nz = devices // 8
    seqs = seq_dev // 2
    slots = 4 * rows
    wide = width // 2
    table = routes(nz)

    def move(v, way):
        return lax.ppermute(v, BOTH, table[way])

    def after(v, *deps):
        return lax.optimization_barrier((v,) + deps)[0]

    def at(v, axis, index):
        return lax.dynamic_index_in_dim(v, index, axis, False)

    def add(a, b):
        return a.astype(F32) + b.astype(F32)

    ctx, dp = lax.axis_index("ctx"), lax.axis_index("dp")
    y, c, z, x = ctx // 2, ctx % 2, dp // 2, dp % 2
    me = dp * 4 + ctx

    x6 = jnp.transpose(tokens, (1, 0, 2))
    c6 = jnp.transpose(cotangent, (1, 0, 2))
    r1, r2 = output_matrix.shape[0], reduce_matrix.shape[0]
    groups = hidden // width
    blob_rows = (1 + groups) * r1 + r2 + 16
    bias_rows = jnp.zeros((16 * width,), BF16)
    bias_rows = lax.dynamic_update_slice_in_dim(
        bias_rows, biases.astype(BF16), me * biases.shape[0], 0
    ).reshape(16, width)
    vmem = pl.BlockSpec(memory_space=pltpu.VMEM)
    blob = pl.pallas_call(
        pack,
        in_specs=[vmem] * 4,
        out_specs=vmem,
        out_shape=shape((blob_rows, width), BF16),
        compiler_params=params(),
        cost_estimate=cost(1),
        name="pack",
    )(output_matrix, expand_matrix, reduce_matrix, bias_rows)
    bz1 = move(blob, 1)
    x6_o = move(after(x6, blob), "core")

    place = jnp.stack([c, y, z, x]).astype(jnp.int32)
    info, wq_own, wq_give, x_give, c_give = pl.pallas_call(
        prepare,
        in_specs=[SMEM, SMEM, vmem, ANY, ANY],
        out_specs=[SMEM, vmem, vmem, vmem, vmem],
        out_shape=[
            shape((FOUND + seq_dev,), jnp.int32),
            shape((project_matrix.shape[0], 3 * wide), BF16),
            shape((project_matrix.shape[0], 3 * wide), BF16),
            shape((seqs, rows, width), BF16),
            shape((seqs, rows, width), BF16),
        ],
        scratch_shapes=[pltpu.SemaphoreType.DMA((seq_dev,))],
        compiler_params=params(),
        cost_estimate=cost(2),
        name="prepare",
    )(after(place, blob), lengths, project_matrix, x6, c6)
    wq_got = move(wq_give, "core")
    wq_chip = jnp.where(
        c == 0, jnp.concatenate([wq_own, wq_got], 0), jnp.concatenate([wq_got, wq_own], 0)
    )
    got = move(after(x_give, bz1, x6_o, wq_chip), "y")
    wz = [move(wq_chip, r) for r in range(1, nz)]
    wa = jnp.stack([wq_chip] + wz)
    bz01 = jnp.stack([blob, bz1])
    bz23 = move(after(bz01, *wz), 2)
    wax, way, wad = move(wa, "x"), move(wa, "y"), move(wa, "xy")
    ba = jnp.concatenate([bz01, after(bz23, wax, way, wad)], 0)
    got_o = move(after(got, ba, wa), "core")
    bax, bay = move(ba, "x"), move(ba, "y")

    xs4 = (x6, got, x6_o, got_o)
    kept = []
    wq_full = None
    for s in range(seqs):
        weight_in = (wa, wax, way, wad) if s == 0 else (wq_full,)
        deps = (ba,) if s == 0 else (kept[-1][3], bax, bay) if s == 1 else (kept[-1][3], ba_o, bax_o, bay_o)
        res = forward_call(s, nz, after(info, *deps), *xs4, *weight_in)
        if s == 0:
            wq_full = res[0]
            res = res[1:]
        if s == 0:
            bad = move(after(bay, res[3]), "x")
            c_got = move(after(c_give, bay, res[3]), "y")
            ba_o, bax_o, bay_o = (move(after(v, res[3]), "core") for v in (ba, bax, bay))
        o_give = after(res[2], c_got) if s == seqs - 1 else res[2]
        kept.append(tuple(res) + (move(o_give, "core"),))
    rail = (ba, bax, bay, bad)
    rail_o = (ba_o, bax_o, bay_o, move(after(bad, kept[1][4], kept[2][4]), "core"))

    own_o = [k[1] for k in kept]
    oth_o = [k[4] for k in kept]
    mixed_m, mixed_g, dy, do_keep, do_send, g_send, g_keep, ga = feed_call(
        info, alphas, x6, got, c6, c_got, *own_o, *oth_o, *rail, *rail_o
    )

    do_recv = move(do_send, "core")
    g_recv = move(after(g_send, do_recv), "core")

    def backward(s, last, grad, *deps):
        qkv, ok, osend, lse, _ = kept[s]
        ins = (wq_full, qkv, lse, ok, osend, do_keep, do_recv) + (() if grad is None else (grad,))
        return backward_call(s, last, after(info, *deps) if deps else info, *xs4, *ins)

    keeps, sends, recvs = [None] * seqs, [None] * seqs, [None] * seqs
    grad, keeps[2], sends[2] = backward(2, False, None)
    g_recv_late = after(g_recv, sends[2])
    ga_send = add(g_keep[0, 1], g_recv_late[0, 1]).astype(BF16)
    gb_send = add(g_keep[1, 1], g_recv_late[1, 1]).astype(BF16)
    ra, rb = move(ga_send, "x"), move(gb_send, "y")
    recvs[2] = move(sends[2], "core")
    mixed_r = move(mixed_g, "y")
    grad, keeps[0], sends[0] = backward(0, False, grad, ga_send, gb_send, mixed_r)
    ra, rb = after(ra, sends[0]), after(rb, sends[0])
    fa = g_keep[0, 0], g_recv[0, 0], ra
    fb = g_keep[1, 0], g_recv[1, 0], rb

    def part(three, index):
        return sum(v[index].astype(F32) for v in three)

    ga_send, gb_send = part(fa, 1).astype(BF16), part(fb, 1).astype(BF16)
    ra, rb = move(ga_send, "y"), move(gb_send, "x")
    recvs[0] = move(sends[0], "core")
    qkeep, qsend, keeps[1], sends[1] = backward(1, True, grad, ga_send, gb_send, recvs[2], recvs[0])
    ra, rb = after(ra, sends[1]), after(rb, sends[1])
    qr = move(after(qsend, ra, rb), "x")
    recvs[1] = move(sends[1], "core")
    fv = jnp.concatenate([add(part(fa, 0), ra), add(part(fb, 0), rb)], 1).astype(BF16)
    fgot = [move(fv[r], r) for r in range(1, nz)]
    gq = add(qkeep, qr)
    gq_send = gq[1].astype(BF16)
    qr = move(gq_send, "y")
    back = move(
        after(
            jnp.concatenate([(d[None] + add(k[:, 1], r[:, 1])).astype(BF16) for d, k, r in zip(dy[:, 1], keeps, recvs)], 0),
            gq_send,
        ),
        "y",
    )
    gq = add(gq[0], qr)
    qgot = [move(gq[r].astype(BF16), r) for r in range(1, nz)]
    half = pl.BlockSpec((1, 1, rows, width), lambda *_: (0, 0, 0, 0))
    mine = pl.BlockSpec((seqs, 1, rows, width), lambda *_: (0, 0, 0, 0))
    six = (seq_dev, rows, width)
    mixed6, input6 = call(
        placed, "placed", 1, (1,),
        [whole(mixed_m.shape)] * 2 + [mine] + [half] * 6, [whole(six)] * 2,
        [shape(six, BF16), shape(six, F32)],
        [], info, mixed_m, mixed_r, dy, *keeps, *recvs)
    fin_in = (gq, *qgot, fv, *fgot, ga)
    one = lambda v: whole((1,) + v.shape[1:])
    fin_out = [shape((r1, 3 * wide), F32)] * 2 + [shape((devices, 128), F32), shape((blob_rows, width), F32)]
    q_own, q_give, tiny, blob_sum = call(
        finish, "finish", 1, (1,),
        [one(gq)] + [whole(v.shape) for v in qgot] + [one(fv)] + [whole(v.shape) for v in fgot + [ga]],
        [whole(v.shape) for v in fin_out], fin_out,
        [], after(info, mixed6), *fin_in)
    tiny = lax.all_to_all(tiny.reshape(devices, 1, 128), BOTH, 0, 0).reshape(devices, 128)
    q_got = move(q_give, "core")

    g_bias = lax.dynamic_slice_in_dim(
        blob_sum[blob_rows - 16 :].reshape(-1), me * biases.shape[0], biases.shape[0], 0
    )
    states = (
        project_matrix, project_first, project_second,
        output_matrix, output_first, output_second,
        expand_matrix, expand_first, expand_second,
        reduce_matrix, reduce_first, reduce_second,
        biases[None], bias_first[None], bias_second[None],
        alphas[None], alpha_first[None], alpha_second[None],
    )
    outs = [shape(v.shape, F32) for v in states] + [shape((1, 1), F32)]
    ins = (tiny, q_own, q_got, blob_sum, g_bias[None], *states)
    res = call(
        update, "update", 3, (1,), [whole(v.shape) for v in ins], [whole(v.shape) for v in outs], outs, [],
        info, *ins)
    input6 = pl.pallas_call(
        placed_rest,
        grid_spec=pltpu.PrefetchScalarGridSpec(
            num_scalar_prefetch=1,
            grid=(seqs,),
            in_specs=[token_block(rows, width, lambda t, i: t), ANY],
            out_specs=token_block(rows, width, lambda t, i: i[OTHER + t]),
        ),
        out_shape=shape(six, F32),
        input_output_aliases={2: 0},
        cost_estimate=cost(1),
        name="placed_rest",
    )(info, back, input6)
    mixed = jnp.transpose(mixed6, (1, 0, 2))
    input_grad = jnp.transpose(input6, (1, 0, 2))
    results = list(res[:12]) + [v[0] for v in res[12:18]]
    return (mixed, input_grad, *results, res[18][0, 0])


def solution(mesh):
    ctx, dp = mesh.shape["ctx"], mesh.shape["dp"]
    row = P(BOTH, None)
    flat = P(BOTH)
    token = P("ctx", "dp", None)
    body = fast_body if (ctx == 4 and dp == 8) else generic_body
    return jax.shard_map(
        body,
        mesh=mesh,
        in_specs=(token, token, P("dp"), row, row, row, row, flat, P())
        + (row,) * 8
        + (flat, flat, P(), P()),
        out_specs=(token, token) + (row,) * 12 + (flat,) * 3 + (P(),) * 4,
        check_vma=False,
    )
```

```python
from functools import partial

import jax
import jax.numpy as jnp
from jax import lax
from jax.experimental import pallas as pl
from jax.experimental.pallas import tpu as pltpu
from jax.sharding import PartitionSpec as P

HEADS = 8
HEAD = 64
STEP = 10


clip_bound = 1.0
beta_one = 0.9
beta_two = 0.999
adam_eps = 1e-08
matrix_rate = 0.05
alpha_rate = 0.2
decay_rate = 0.1

BOTH = ("dp", "ctx")
F32 = jnp.float32
BF16 = jnp.bfloat16
VMEM_LIMIT = 56 * 1024 * 1024


def adamw(weight, first, second, grad, rate, decay):
    first = beta_one * first + (1.0 - beta_one) * grad
    second = beta_two * second + (1.0 - beta_two) * grad * grad
    mhat = first / (1.0 - beta_one**STEP)
    vhat = second / (1.0 - beta_two**STEP)
    weight = weight - rate * (mhat / (jnp.sqrt(vhat) + adam_eps) + decay * weight)
    return (first, second, weight)


def dot_nn(a, b):
    return lax.dot_general(a, b, (((1,), (0,)), ((), ())), preferred_element_type=F32)


def dot_nt(a, b):
    return lax.dot_general(a, b, (((1,), (1,)), ((), ())), preferred_element_type=F32)


def dot_tn(a, b):
    return lax.dot_general(a, b, (((0,), (0,)), ((), ())), preferred_element_type=F32)


CORE, CHIP_Y, CHIP_Z, CHIP_X, LENS, OWN, OTHER, INFO = 0, 1, 2, 3, 4, 7, 10, 13


def block_places(info, rows):
    core, y = info[CORE], info[CHIP_Y]
    return [
        pl.multiple_of(b * rows, rows)
        for b in (
            2 * y + core,
            2 * (1 - y) + core,
            2 * y + 1 - core,
            2 * (1 - y) + 1 - core,
        )
    ]


def chip_index(info, r, fx, fy):
    z = info[CHIP_Z] ^ r
    x = info[CHIP_X] ^ fx
    y = info[CHIP_Y] ^ fy
    return (z * 2 + x) * 2 + y


PIECES = 4


def gathered_pieces(nz):
    places = ((0, 0), (1, 0), (0, 1), (1, 1))
    return [(i, r, r, fx, fy) for i, (fx, fy) in enumerate(places) for r in range(nz)]


def sequence_copies(s, info, four, x_s, sems):
    own = info[OWN + s]
    at = (own, s, own, s)
    return [pltpu.make_async_copy(v.at[i], x_s.at[b], sems.at[b]) for b, (v, i) in enumerate(zip(four, at))]


def attend_forward(seqs, nz, info, *refs):
    refs = list(refs)
    four = [refs.pop(0) for _ in range(4)]
    x_s, qkv_s, oo_s, o_s, st_s, w_s, sems = refs[-7:]
    refs = refs[:-7]
    assemble = 0 in seqs
    copies = [sequence_copies(s, info, four, x_s.at[i], sems.at[i]) for i, s in enumerate(seqs)]
    pieces = [refs.pop(0) for _ in range(PIECES if assemble else 1)]
    wq_out = refs.pop(0) if assemble else None
    qkv_out, ok_out, os_out, lse_out, lse_s = refs
    for copy in copies[0]:
        copy.start()
    outs = []

    def put(i, src, dst):
        outs.append(pltpu.make_async_copy(src, dst, sems.at[i, 4 + len(outs) % 5]))
        outs[-1].start()

    if assemble:
        rows = pieces[0].shape[1]
        for which, at, r, fx, fy in gathered_pieces(nz):
            place = pl.multiple_of(chip_index(info, r, fx, fy) * rows, rows)
            w_s[pl.ds(place, rows), :] = pieces[which][at]
    else:
        weight = pltpu.make_async_copy(pieces[0], w_s, sems.at[0, 9])
        weight.start()
        weight.wait()
    for more in copies[1:]:
        for copy in more:
            copy.start()
    rows = x_s.shape[2]
    places = block_places(info, rows)
    lane = lax.broadcasted_iota(jnp.int32, (rows, 128), 1)
    low_lane = lane < HEAD
    row_i = lax.broadcasted_iota(jnp.int32, (rows, rows), 0)
    col_i = lax.broadcasted_iota(jnp.int32, (rows, rows), 1)

    def one(i, length, qb, n):
        wide = 256
        span = slice(qb * rows, (qb + 1) * rows)
        base = (n - 1) * rows
        ok = (base + col_i) < length
        if n == qb + 1:
            ok = ok & (col_i <= row_i)
        scores, values = [], []
        for pair in range(2):
            at = pair * 128
            q = qkv_s[i, span, at : at + 128]
            k = qkv_s[i, 0 : n * rows, wide + at : wide + at + 128]
            v = qkv_s[i, 0 : n * rows, 2 * wide + at : 2 * wide + at + 128]
            values.append(jnp.concatenate([v, jnp.ones_like(v)], axis=1))
            for h in range(2):
                mine = low_lane if h == 0 else jnp.logical_not(low_lane)
                qm = jnp.where(mine, q * jnp.asarray(HEAD**-0.5, BF16), jnp.zeros_like(q))
                scores.append(dot_nt(qm, k))
        stats = jnp.zeros((rows, 128), F32)
        res = []
        for head, sc in enumerate(scores):
            last = jnp.where(ok, sc[:, base:], -1e30)
            sc = jnp.concatenate([sc[:, :base], last], axis=1) if n > 1 else last
            top = jnp.max(sc, axis=1, keepdims=True)
            e = jnp.exp(sc - top).astype(BF16)
            ob = dot_nn(e, values[head // 2])
            den = ob[:, 128:]
            res.append(ob[:, :128] / den)
            stats = jnp.where(lane == head, top + jnp.log(den), stats)
        st_s[span, :] = stats
        for pair in range(2):
            o_s[span, pair * 128 : pair * 128 + 128] = jnp.where(
                low_lane, res[2 * pair], res[2 * pair + 1]
            ).astype(BF16)

    for i, s in enumerate(seqs):
        length = info[LENS + s]
        w = w_s[...]
        for b, place in enumerate(places):
            copies[i][b].wait()
            qkv_s[i, pl.ds(place, rows), :] = dot_nn(x_s[i, b], w).astype(BF16)
        put(i, qkv_s.at[i], qkv_out.at[i])
        if assemble:
            put(i, w_s, wq_out)
        blocks = (length + rows - 1) // rows
        for qb in range(qkv_s.shape[1] // rows):
            for n in range(1, qb + 2):
                cond = (blocks == n) if n < qb + 1 else (blocks >= n)

                @pl.when(cond)
                def _(i=i, length=length, qb=qb, n=n):
                    one(i, length, qb, n)

        for b in range(4):
            oo_s[i, b // 2, b % 2] = o_s[pl.ds(places[b], rows), :]
        put(i, oo_s.at[i, 1], os_out.at[i])
        put(i, oo_s.at[i, 0], ok_out.at[i])
        lse_s[i] = jnp.transpose(st_s[...])[:8]
        put(i, lse_s.at[i], lse_out.at[i])
    for copy in outs:
        copy.wait()


def attend_backward(s, grad_in, last_one, info, *refs):
    refs = list(refs)
    four = [refs.pop(0) for _ in range(4)]
    wq_ref, qkv_in, lse_in, ok_in, os_in, dk_in, dr_in = (refs.pop(0) for _ in range(7))
    g_in = refs.pop(0) if grad_in else None
    at = 0 if s == 0 else s - 1
    scratch = refs[-15:]
    (do_s, r_s, dq_s, dk_s, dv_s, x_s, w_s, qkv_ref, lse_ref, o_in, d_in, g_ref, keep_ref, send_ref,
     sems) = scratch
    refs = refs[:-15]
    if last_one:
        qkeep_out, qsend_out, keep_out, send_out, qkeep_ref, qsend_ref = refs
    else:
        g_out, keep_out, send_out = refs
    wanted = [
        (dk_in.at[s], d_in.at[0]),
        (dr_in.at[s], d_in.at[1]),
        (ok_in.at[at], o_in.at[0]),
        (os_in.at[at], o_in.at[1]),
        (lse_in.at[at], lse_ref.at[0]),
        (qkv_in.at[at], qkv_ref.at[0]),
        (wq_ref, w_s),
    ]
    if grad_in:
        wanted.append((g_in, g_ref))
    early = [pltpu.make_async_copy(src, dst, sems.at[4 + i]) for i, (src, dst) in enumerate(wanted)]
    late = sequence_copies(s, info, four, x_s, sems) + early[6:]
    early = early[:6]
    for copy in early:
        copy.start()
    for copy in early:
        copy.wait()
    for copy in late:
        copy.start()
    length = info[LENS + s]
    rows = x_s.shape[1]
    places = block_places(info, rows)
    lane = lax.broadcasted_iota(jnp.int32, (rows, 128), 1)
    low_lane = lane < HEAD
    head_of = lax.broadcasted_iota(jnp.int32, (8, 256), 1) // HEAD
    pick = (head_of == lax.broadcasted_iota(jnp.int32, (8, 256), 0)).astype(BF16)
    for b in range(4):
        do = d_in[b // 2, b % 2]
        o = o_in[b // 2, b % 2]
        do_s[pl.ds(places[b], rows), :] = do
        prod = do.astype(F32) * o.astype(F32)
        high = prod.astype(BF16)
        low = (prod - high.astype(F32)).astype(BF16)
        r_s[:, pl.ds(places[b], rows)] = dot_nt(pick, high) + dot_nt(pick, low)
    dk_s[...] = jnp.zeros_like(dk_s)
    dv_s[...] = jnp.zeros_like(dv_s)
    if not grad_in:
        g_ref[...] = jnp.zeros_like(g_ref)
    key_i = lax.broadcasted_iota(jnp.int32, (rows, rows), 0)
    qry_i = lax.broadcasted_iota(jnp.int32, (rows, rows), 1)
    scale = HEAD**-0.5

    def one_all(qb):
        n = qb + 1
        wide = 256
        span = slice(qb * rows, (qb + 1) * rows)
        ok = (key_i <= qry_i) & ((qb * rows + key_i) < length)
        qms, doms, dqs = [], [], [None] * 4
        for pair in range(2):
            at = pair * 128
            q = qkv_ref[0, span, at : at + 128]
            do = do_s[span, at : at + 128]
            for h in range(2):
                mine = low_lane if h == 0 else jnp.logical_not(low_lane)
                qms.append(jnp.where(mine, q * jnp.asarray(scale, BF16), jnp.zeros_like(q)))
                doms.append(jnp.where(mine, do, jnp.zeros_like(do)))
        for kb in range(n):
            keys = slice(kb * rows, (kb + 1) * rows)
            ks = [qkv_ref[0, keys, wide + 128 * pr : wide + 128 * pr + 128] for pr in range(2)]
            vs = [qkv_ref[0, keys, 2 * wide + 128 * pr : 2 * wide + 128 * pr + 128] for pr in range(2)]
            scs = [dot_nt(ks[h // 2], qms[h]) for h in range(4)]
            dps = [dot_nt(vs[h // 2], doms[h]) for h in range(4)]
            ps, dss = [], []
            for h in range(4):
                p = jnp.exp(scs[h] - lse_ref[0, h : h + 1, span])
                if kb == qb:
                    p = jnp.where(ok, p, 0.0)
                dss.append((p * (dps[h] - r_s[h : h + 1, span])).astype(BF16))
                ps.append(p.astype(BF16))
            for pr in range(2):
                at = slice(128 * pr, 128 * pr + 128)
                dv_s[keys, at] += dot_nn(ps[2 * pr], doms[2 * pr]) + dot_nn(ps[2 * pr + 1], doms[2 * pr + 1])
                dk_s[keys, at] += dot_nn(dss[2 * pr], qms[2 * pr]) + dot_nn(dss[2 * pr + 1], qms[2 * pr + 1])
            for h in range(4):
                dqh = dot_tn(dss[h], ks[h // 2])
                dqs[h] = dqh if dqs[h] is None else dqs[h] + dqh
        for pr in range(2):
            dq_s[span, 128 * pr : 128 * pr + 128] = (
                jnp.where(low_lane, dqs[2 * pr], dqs[2 * pr + 1]) * scale
            ).astype(BF16)

    total = qkv_ref.shape[1] // rows
    for qb in range(total):

        @pl.when(qb * rows < length)
        def _(qb=qb):
            one_all(qb)

    for copy in late:
        copy.wait()
    w = w_s[...]
    outs = []

    def send_out_copy(src, dst):
        outs.append(pltpu.make_async_copy(src, dst, sems.at[13 + len(outs)]))
        outs[-1].start()

    for b in (2, 3, 0, 1):
        place = places[b]
        here = pl.ds(place, rows)

        @pl.when(place < length)
        def _(b=b, here=here):
            d = jnp.concatenate(
                [dq_s[here, :], dk_s[here, :].astype(BF16), dv_s[here, :].astype(BF16)], axis=1
            )
            g_ref[...] += dot_tn(x_s[b], d)
            dx = dot_nt(d, w)
            if b < 2:
                keep_ref[b] = dx.astype(BF16)
            else:
                send_ref[b - 2] = dx.astype(BF16)

        @pl.when(place >= length)
        def _(b=b):
            if b < 2:
                keep_ref[b] = jnp.zeros_like(keep_ref[b])
            else:
                send_ref[b - 2] = jnp.zeros_like(send_ref[b - 2])

        if b == 3:
            send_out_copy(send_ref, send_out.at[0])
        if b == 0:
            send_out_copy(keep_ref.at[0], keep_out.at[0, 0])
    if last_one:
        nz = qkeep_ref.shape[1]
        part = g_ref.shape[0] // (nz * 4)
        for out, dst, fx in ((qsend_ref, qsend_out, 1), (qkeep_ref, qkeep_out, 0)):
            for r in range(nz):
                for fy in range(2):
                    at = pl.multiple_of(chip_index(info, r, fx, fy) * part, part)
                    out[fy, r] = g_ref[pl.ds(at, part), :].astype(out.dtype)
            send_out_copy(out, dst)
    else:
        send_out_copy(g_ref, g_out)
    send_out_copy(keep_ref.at[1], keep_out.at[0, 1])
    for copy in outs:
        copy.wait()


def feed(nz, info, alphas, *refs):
    refs = list(refs)
    xm, xg, cm, cg = (refs.pop(0) for _ in range(4))
    own_o = [refs.pop(0) for _ in range(2)]
    oth_o = [refs.pop(0) for _ in range(2)]
    rails = [[refs.pop(0) for _ in range(PIECES)] for _ in range(2)]
    (mixm, mixg, dy_ref, dkeep, dsend, gsend, gkeep, ga_ref,
     wo_s, w1_s, w2_s, b_s, go_s, g1_s, g2_s, gb1_s, gb2_s, ga_s,
     h_s, gp_s, yb_s, br_s, f_s, oo_s) = refs
    step = s = pl.program_id(0)
    core = info[CORE]
    chips = nz * 4
    width = wo_s.shape[1]
    groups = w1_s.shape[1] // width
    r1 = wo_s.shape[0] // (2 * chips)
    r2 = w2_s.shape[0] // (2 * chips)

    @pl.when(step == 0)
    def _():
        bias = None
        for rail in range(2):
            for which, at, r, fx, fy in gathered_pieces(nz):
                d = chip_index(info, r, fx, fy) * 2 + (core ^ rail)
                piece = rails[rail][which]
                small = pl.ds(pl.multiple_of(d * r1, r1), r1)
                wo_s[small, :] = piece[at, 0:r1]
                for j in range(groups):
                    w1_s[small, j * width : (j + 1) * width] = piece[at, (1 + j) * r1 : (2 + j) * r1]
                first = (1 + groups) * r1
                w2_s[pl.ds(pl.multiple_of(d * r2, r2), r2), :] = piece[at, first : first + r2]
                part = piece[at, first + r2 : first + r2 + 16].astype(F32)
                bias = part if bias is None else bias + part
        b_s[...] = bias
        for ref in (go_s, g1_s, g2_s, gb1_s, gb2_s, ga_s):
            ref[...] = jnp.zeros_like(ref)

    rows = xm.shape[1]
    both = 2 * rows
    y_here = info[CHIP_Y]
    length = info[LENS + s]
    begins = [(2 * y_here + core) * rows, (2 * (1 - y_here) + core) * rows]

    def pick3(three):
        return jnp.where(s == 0, three[0][0], jnp.where(s == 1, three[1][0], three[1][1])).reshape(both, -1)

    here = pl.ds(pl.multiple_of(core * 256, 256), 256)
    there = pl.ds(pl.multiple_of((1 - core) * 256, 256), 256)
    a0, a1 = alphas[0], alphas[1]
    oo_s[0] = pick3(own_o)
    oo_s[1] = pick3(oth_o)
    x = jnp.concatenate([xm[0], xg[0]], axis=0).astype(F32)
    branch = dot_nn(oo_s[0], wo_s[here, :]) + dot_nn(oo_s[1], wo_s[there, :])
    y = x + a0 * branch
    br_s[...] = branch
    yb = y.astype(BF16)
    yb_s[...] = yb
    f = None
    for j in range(groups):
        cols = slice(j * width, (j + 1) * width)
        pre = dot_nn(yb, w1_s[:, cols]) + b_s[j : j + 1, :]
        cdf = 0.5 + 0.5 * lax.erf(pre * (0.5**0.5))
        h = (pre * cdf).astype(BF16)
        h_s[:, cols] = h
        gp_s[:, cols] = cdf + pre * (jnp.exp(-0.5 * pre * pre) * 0.3989422804014327)
        part = dot_nn(h, w2_s[cols, :])
        f = part if f is None else f + part
    f = f + b_s[groups : groups + 1, :]
    f_s[...] = f
    mixed = (y + a1 * f).astype(BF16)
    mixm[0] = mixed[:rows]
    mixg[0] = mixed[rows:]

    def back(at, count, cot, begin_rows):
        span = pl.ds(at, count)
        g = jnp.where(begin_rows < length, cot.astype(F32), 0.0)
        df = (a1 * g).astype(BF16)
        gb2_s[...] += jnp.sum(df.astype(F32).reshape(count // 8, 8, width), axis=0)
        yb = yb_s[span, :]
        dy = g
        for j in range(groups):
            cols = slice(j * width, (j + 1) * width)
            dh = dot_nt(df, w2_s[cols, :])
            dpre = (dh * gp_s[span, cols]).astype(BF16)
            gb1_s[:, cols] += jnp.sum(dpre.astype(F32).reshape(count // 8, 8, width), axis=0)
            g2_s[cols, :] += dot_tn(h_s[span, cols], df)
            g1_s[:, cols] += dot_tn(yb, dpre)
            dy = dy + dot_nt(dpre, w1_s[:, cols])
        ga_s[0:8, :] += jnp.sum((br_s[span, :] * dy).reshape(count // 8, 8, width), axis=0)
        ga_s[8:16, :] += jnp.sum((f_s[span, :] * g).reshape(count // 8, 8, width), axis=0)
        db = (a0 * dy).astype(BF16)
        go_s[here, :] += dot_tn(oo_s[0, span, :], db)
        go_s[there, :] += dot_tn(oo_s[1, span, :], db)
        return dy, dot_nt(db, wo_s[here, :]).astype(BF16), dot_nt(db, wo_s[there, :]).astype(BF16)

    late = jnp.maximum(begins[0], begins[1])
    early = jnp.minimum(begins[0], begins[1])
    row = lax.broadcasted_iota(jnp.int32, (rows, width), 0)

    @pl.when(late < length)
    def _():
        where = jnp.concatenate([begins[0] + row, begins[1] + row], axis=0)
        dy, keep, send = back(0, both, jnp.concatenate([cm[0], cg[0]], axis=0), where)
        dy_ref[0] = dy.reshape(2, rows, width)
        dkeep[0] = keep.reshape(2, rows, -1)
        dsend[0] = send.reshape(2, rows, -1)

    @pl.when(late >= length)
    def _():
        dkeep[...] = jnp.zeros_like(dkeep)
        dsend[...] = jnp.zeros_like(dsend)
        dy_ref[...] = jnp.zeros_like(dy_ref)

        @pl.when(early < length)
        def _():
            half = pl.multiple_of(y_here * rows, rows)
            cot = jnp.where(y_here == 0, cm[0], cg[0])
            dy, keep, send = back(half, rows, cot, early + row)
            dy_ref[0, y_here] = dy
            dkeep[0, y_here] = keep
            dsend[0, y_here] = send

    @pl.when(step == pl.num_programs(0) - 1)
    def _():
        gb = jnp.concatenate(
            [jnp.sum(gb1_s[:, j * width : (j + 1) * width], axis=0, keepdims=True) for j in range(groups)]
            + [jnp.sum(gb2_s[...], axis=0, keepdims=True), jnp.zeros((16 - groups - 1, width), F32)],
            axis=0,
        ).astype(BF16)
        for out, whose in ((gkeep, core), (gsend, 1 - core)):
            for r in range(nz):
                for fx in range(2):
                    for fy in range(2):
                        d = chip_index(info, r, fx, fy) * 2 + whose
                        small = pl.ds(pl.multiple_of(d * r1, r1), r1)
                        out[0, fx, fy, r, 0:r1] = go_s[small, :].astype(BF16)
                        for j in range(groups):
                            out[0, fx, fy, r, (1 + j) * r1 : (2 + j) * r1] = g1_s[
                                small, j * width : (j + 1) * width
                            ].astype(BF16)
                        out[1, fy, fx, r, 0:r2] = g2_s[
                            pl.ds(pl.multiple_of(d * r2, r2), r2), :
                        ].astype(BF16)
                        out[1, fy, fx, r, r2 : r2 + 16] = gb
        ga_ref[0:1, :] = jnp.sum(ga_s[0:8, :], axis=0, keepdims=True)
        ga_ref[1:2, :] = jnp.sum(ga_s[8:16, :], axis=0, keepdims=True)


def prepare(place, lengths, wq, x_ref, info, w_own, w_give, xg_ref, sems):
    six = lengths.shape[0]
    seqs = six // 2
    y = place[1]
    ranks = []
    for i in range(six):
        rank = jnp.int32(0)
        for j in range(six):
            if j != i:
                longer = lengths[j] >= lengths[i] if j < i else lengths[j] > lengths[i]
                rank = rank + longer.astype(jnp.int32)
        ranks.append(rank)
    order = [0] + list(range(3, six, 2)) + [1] + list(range(2, six, 2))
    ids = []
    for r in order:
        ids.append(sum(jnp.where(ranks[i] == r, i, 0) for i in range(six)))
    own = [jnp.where(y == 0, ids[s], ids[seqs + s]) for s in range(seqs)]
    other = [jnp.where(y == 0, ids[seqs + s], ids[s]) for s in range(seqs)]
    copies = [pltpu.make_async_copy(x_ref.at[other[s]], xg_ref.at[s], sems.at[s]) for s in range(seqs)]
    for copy in copies:
        copy.start()
    for i in range(4):
        info[i] = place[i]
    for s in range(seqs):
        info[LENS + s] = lengths[own[s]]
        info[OWN + s] = own[s]
        info[OTHER + s] = other[s]
    wide = wq.shape[1] // 6
    core = place[0]
    for j in range(3):
        left = wq[:, 2 * j * wide : (2 * j + 1) * wide]
        right = wq[:, (2 * j + 1) * wide : (2 * j + 2) * wide]
        cols = slice(j * wide, (j + 1) * wide)
        w_own[:, cols] = jnp.where(core == 0, left, right).astype(BF16)
        w_give[:, cols] = jnp.where(core == 0, right, left).astype(BF16)
    for copy in copies:
        copy.wait()


def give(info, c_ref, cg_ref):
    cg_ref[...] = c_ref[...]


def pack(wo, w1, w2, bias, out):
    rows, width = wo.shape
    groups = w1.shape[1] // width
    out[0:rows] = wo[...].astype(BF16)
    for j in range(groups):
        out[(1 + j) * rows : (2 + j) * rows] = w1[:, j * width : (j + 1) * width].astype(BF16)
    first = (1 + groups) * rows
    out[first : first + w2.shape[0]] = w2[...].astype(BF16)
    out[first + w2.shape[0] :] = bias[...]


def finish(info, gq, r1, r2, r3, fv, f1, f2, f3, ga, q_own, q_give, tiny, blob):
    total = gq[0]
    for r in (r1, r2, r3):
        total = total + r[...].astype(F32)
    rows = q_own.shape[0]
    core = info[CORE]
    tiny_rows = tiny.shape[0]
    sums = jnp.sum(total * total)
    blob[...] = fv[0].astype(F32) + f1[...].astype(F32) + f2[...].astype(F32) + f3[...].astype(F32)
    main = blob.shape[0] - 16
    own = blob[0:main, :]
    sums = sums + jnp.sum(own * own)
    me = ((info[CHIP_Z] * 2 + info[CHIP_X]) * 2 + info[CHIP_Y]) * 2 + core
    bias = blob[main:, :]
    width = bias.shape[1]
    count = 5 * width // tiny_rows
    flat = lax.broadcasted_iota(jnp.int32, bias.shape, 0) * width + lax.broadcasted_iota(
        jnp.int32, bias.shape, 1
    )
    ours = (flat >= me * count) & (flat < (me + 1) * count)
    sums = sums + jnp.sum(jnp.where(ours, bias * bias, 0.0))
    low, high = total[:rows], total[rows:]
    q_own[...] = jnp.where(core == 0, low, high)
    q_give[...] = jnp.where(core == 0, high, low)
    lane = lax.broadcasted_iota(jnp.int32, tiny.shape, 1)
    a0, a1 = jnp.sum(ga[0:1, :]), jnp.sum(ga[1:2, :])
    tiny[...] = jnp.where(lane == 0, sums, jnp.where(lane == 1, a0, jnp.where(lane == 2, a1, 0.0)))


def placed(info, mixm, mixr, mixed):
    for s in range(mixm.shape[0]):
        mixed[info[OWN + s]] = mixm[s]
        mixed[info[OTHER + s]] = mixr[s]


def placed_own(info, dy, k0, k1, k2, r0, r1, r2, grad):
    step = pl.program_id(0)
    for s, (k, r) in enumerate(((k0, r0), (k1, r1), (k2, r2))):

        @pl.when(step == s)
        def _(k=k, r=r):
            grad[0] = dy[0, 0] + (k[0, 0].astype(F32) + r[0, 0].astype(F32))


def placed_rest(info, back, grad_in, grad, wide_s, sems):
    copies = []
    for s in range(back.shape[0]):
        wide_s[s] = back[s].astype(F32)
        copies.append(pltpu.make_async_copy(wide_s.at[s], grad.at[info[OTHER + s]], sems.at[s]))
        copies[-1].start()
    for copy in copies:
        copy.wait()


def update(info, tiny, q_own, q_got, blob, g_bias, *refs):
    ins, outs = refs[:18], refs[18:]
    squares = jnp.sum(tiny[:, 0:1])
    a0, a1 = jnp.sum(tiny[:, 1:2]), jnp.sum(tiny[:, 2:3])
    norm = jnp.sqrt(jnp.zeros((1, 1), F32) + (squares + a0 * a0 + a1 * a1))
    factor = jnp.minimum(1.0, clip_bound / (norm + 1e-06))
    outs[18][...] = norm
    rows = q_own.shape[0]
    wide = q_own.shape[1] // 3

    def put(i, place, grad, rate, decay):
        if grad.ndim == 1:
            f = jnp.zeros(grad.shape, F32) + factor[0, 0]
        else:
            f = factor
        res = adamw(ins[3 * i][place], ins[3 * i + 1][place], ins[3 * i + 2][place], f * grad, rate, decay)
        for j in range(3):
            outs[3 * i + j][place] = res[j]

    core = info[CORE]
    for j in range(3):
        left = q_own[:, j * wide : (j + 1) * wide]
        right = q_got[:, j * wide : (j + 1) * wide]
        both = (jnp.where(core == 0, left, right), jnp.where(core == 0, right, left))
        for k in range(2):
            at = (2 * j + k) * wide
            put(0, (slice(None), slice(at, at + wide)), both[k], matrix_rate, decay_rate)
    width = blob.shape[1]
    groups = ins[6].shape[1] // width
    put(1, (slice(None), slice(None)), blob[0:rows, :], matrix_rate, decay_rate)
    for j in range(groups):
        put(2, (slice(None), slice(j * width, (j + 1) * width)), blob[(1 + j) * rows : (2 + j) * rows, :],
            matrix_rate, decay_rate)
    first = (1 + groups) * rows
    put(3, (slice(None), slice(None)), blob[first : first + ins[9].shape[0], :], matrix_rate, decay_rate)
    put(4, (slice(None), slice(None)), g_bias[...], matrix_rate, 0.0)
    lane = lax.broadcasted_iota(jnp.int32, (1, 2), 1)
    put(5, (slice(None), slice(None)), jnp.where(lane == 0, a0, a1), alpha_rate, 0.0)


def whole(shape):
    return pl.BlockSpec(shape, lambda *_: (0,) * len(shape))


SMEM = pl.BlockSpec(memory_space=pltpu.SMEM)
ANY = pl.BlockSpec(memory_space=pl.ANY)


def routes(nz):
    def perm(to):
        out = []
        for z in range(nz):
            for x in range(2):
                for y in range(2):
                    for c in range(2):
                        z2, x2, y2, c2 = to(z, x, y, c)
                        out.append((((z * 2 + x) * 4 + y * 2 + c), ((z2 * 2 + x2) * 4 + y2 * 2 + c2)))
        return out

    table = {
        "core": perm(lambda z, x, y, c: (z, x, y, 1 - c)),
        "y": perm(lambda z, x, y, c: (z, x, 1 - y, c)),
        "x": perm(lambda z, x, y, c: (z, 1 - x, y, c)),
        "xy": perm(lambda z, x, y, c: (z, 1 - x, 1 - y, c)),
    }
    for r in range(1, nz):
        table[r] = perm(lambda z, x, y, c, r=r: (z ^ r, x, y, c))
    return table


def generic_body(
    tokens,
    cotangent,
    lengths,
    project_matrix,
    output_matrix,
    expand_matrix,
    reduce_matrix,
    biases,
    alphas,
    project_first,
    project_second,
    output_first,
    output_second,
    expand_first,
    expand_second,
    reduce_first,
    reduce_second,
    bias_first,
    bias_second,
    alpha_first,
    alpha_second,
):
    slot_dev, seq_dev, width = tokens.shape
    ctx_index = lax.axis_index("ctx")
    qpos = ctx_index * slot_dev + jnp.arange(slot_dev, dtype=jnp.int32)
    gathered = (
        lax.all_gather(project_matrix.astype(jnp.bfloat16), ("dp", "ctx"), axis=0, tiled=True),
        lax.all_gather(output_matrix.astype(jnp.bfloat16), ("dp", "ctx"), axis=0, tiled=True),
        lax.all_gather(expand_matrix.astype(jnp.bfloat16), ("dp", "ctx"), axis=0, tiled=True),
        lax.all_gather(reduce_matrix.astype(jnp.bfloat16), ("dp", "ctx"), axis=0, tiled=True),
        lax.all_gather(biases.astype(jnp.bfloat16), ("dp", "ctx"), axis=0, tiled=True),
    )
    w_project, w_output, w_expand, w_reduce, bias_all = gathered
    hidden_width = w_expand.shape[1]
    scale = HEAD ** (-0.5)
    flat = tokens.reshape(-1, width)
    query_key_value = jnp.dot(flat, w_project, preferred_element_type=jnp.float32).astype(
        jnp.bfloat16
    )
    query_key_value = query_key_value.reshape(slot_dev, seq_dev, 3 * width)
    query = query_key_value[..., :width].reshape(slot_dev, seq_dev, HEADS, HEAD)
    kv_all = lax.all_gather(query_key_value[..., width:], "ctx", axis=0, tiled=True)
    length = kv_all.shape[0]
    keys = kv_all[..., :width].reshape(length, seq_dev, HEADS, HEAD)
    values = kv_all[..., width:].reshape(length, seq_dev, HEADS, HEAD)
    scores = jnp.einsum("qshe,kshe->shqk", query, keys, preferred_element_type=jnp.float32) * scale
    kpos = jnp.arange(length, dtype=jnp.int32)
    allowed = (kpos[None, None, :] <= qpos[None, :, None]) & (
        kpos[None, None, :] < lengths[:, None, None]
    )
    masked = jnp.where(allowed[:, None], scores, -1e30)
    top = jnp.max(masked, axis=-1, keepdims=True)
    expo = jnp.exp(masked - top)
    prob = expo / jnp.sum(expo, axis=-1, keepdims=True)
    prob_low = prob.astype(jnp.bfloat16)
    attended_rows = jnp.einsum(
        "shqk,kshe->qshe", prob_low, values, preferred_element_type=jnp.float32
    )
    attended_rows = attended_rows.astype(jnp.bfloat16).reshape(slot_dev * seq_dev, width)
    branch_output = jnp.dot(attended_rows, w_output, preferred_element_type=jnp.float32)
    residual_stream = flat.astype(jnp.float32) + alphas[0] * branch_output
    resid_low = residual_stream.astype(jnp.bfloat16)
    bias_float = bias_all.astype(jnp.float32)
    before_activation = (
        jnp.dot(resid_low, w_expand, preferred_element_type=jnp.float32) + bias_float[:hidden_width]
    )
    activate = partial(jax.nn.gelu, approximate=False)
    hidden_rows = activate(before_activation).astype(jnp.bfloat16)
    feed_output = (
        jnp.dot(hidden_rows, w_reduce, preferred_element_type=jnp.float32)
        + bias_float[hidden_width:]
    )
    mixed = (residual_stream + alphas[1] * feed_output).astype(jnp.bfloat16).reshape(tokens.shape)
    valid = (qpos[:, None] < lengths[None, :]).astype(jnp.float32).reshape(-1, 1)
    pull = cotangent.reshape(-1, width).astype(jnp.float32) * valid
    d_ffout = (alphas[1] * pull).astype(jnp.bfloat16)
    g_reduce = jnp.dot(hidden_rows.T, d_ffout, preferred_element_type=jnp.float32)
    g_second_bias = jnp.sum(d_ffout.astype(jnp.float32), axis=0)
    d_hidden = jnp.dot(d_ffout, w_reduce.T, preferred_element_type=jnp.float32)
    d_pre = jax.vjp(activate, before_activation)[1](d_hidden)[0].astype(jnp.bfloat16)
    g_expand = jnp.dot(resid_low.T, d_pre, preferred_element_type=jnp.float32)
    g_first_bias = jnp.sum(d_pre.astype(jnp.float32), axis=0)
    d_resid = pull + jnp.dot(d_pre, w_expand.T, preferred_element_type=jnp.float32)
    g_alpha = jnp.stack([jnp.sum(branch_output * d_resid), jnp.sum(feed_output * pull)])
    d_branch = (alphas[0] * d_resid).astype(jnp.bfloat16)
    g_output = jnp.dot(attended_rows.T, d_branch, preferred_element_type=jnp.float32)
    d_att = jnp.dot(d_branch, w_output.T, preferred_element_type=jnp.float32).astype(jnp.bfloat16)
    d_att = d_att.reshape(slot_dev, seq_dev, HEADS, HEAD)
    d_prob = jnp.einsum("qshe,kshe->shqk", d_att, values, preferred_element_type=jnp.float32)
    d_scores = (prob * (d_prob - jnp.sum(prob * d_prob, axis=-1, keepdims=True))).astype(
        jnp.bfloat16
    )
    d_query = (
        jnp.einsum("shqk,kshe->qshe", d_scores, keys, preferred_element_type=jnp.float32) * scale
    )
    count = lax.axis_size("ctx") * slot_dev
    g_keys = (
        jnp.einsum("shqk,qshe->kshe", d_scores, query, preferred_element_type=jnp.float32) * scale
    )
    g_values = jnp.einsum("shqk,qshe->kshe", prob_low, d_att, preferred_element_type=jnp.float32)
    d_kv = lax.psum_scatter(
        jnp.concatenate(
            [g_keys.reshape(count, seq_dev, width), g_values.reshape(count, seq_dev, width)],
            axis=-1,
        ).astype(jnp.bfloat16),
        "ctx",
        scatter_dimension=0,
        tiled=True,
    ).astype(jnp.float32)
    d_qkv = jnp.concatenate([d_query.reshape(slot_dev, seq_dev, width), d_kv], axis=-1)
    d_qkv = d_qkv.astype(jnp.bfloat16).reshape(-1, 3 * width)
    g_project = jnp.dot(flat.T, d_qkv, preferred_element_type=jnp.float32)
    input_grad = (
        d_resid + jnp.dot(d_qkv, w_project.T, preferred_element_type=jnp.float32)
    ).reshape(tokens.shape)
    g_bias = jnp.concatenate([g_first_bias, g_second_bias])
    devices = lax.axis_size(("dp", "ctx"))
    device_index = lax.axis_index(("dp", "ctx"))
    summed = lax.psum((g_project, g_output, g_expand, g_reduce, g_bias, g_alpha), ("dp", "ctx"))
    squares = jnp.float32(0.0)
    for grad in summed:
        squares = squares + jnp.sum(grad * grad)
    owned = []
    for grad in summed[:5]:
        rows = grad.shape[0] // devices
        owned.append(lax.dynamic_slice_in_dim(grad, device_index * rows, rows, 0))
    alpha_sum = summed[5]
    grad_norm = jnp.sqrt(squares)
    factor = jnp.minimum(1.0, clip_bound / (grad_norm + 1e-06))
    weights = (project_matrix, output_matrix, expand_matrix, reduce_matrix, biases, alphas)
    states = (
        (project_first, project_second),
        (output_first, output_second),
        (expand_first, expand_second),
        (reduce_first, reduce_second),
        (bias_first, bias_second),
        (alpha_first, alpha_second),
    )
    grads = (owned[0], owned[1], owned[2], owned[3], owned[4], alpha_sum)
    rates = (matrix_rate, matrix_rate, matrix_rate, matrix_rate, matrix_rate, alpha_rate)
    decays = (decay_rate, decay_rate, decay_rate, decay_rate, 0.0, 0.0)
    results = []
    for weight, (first, second), grad, rate, decay in zip(weights, states, grads, rates, decays):
        results.extend(adamw(weight, first, second, factor * grad, rate, decay))
    return (
        mixed,
        input_grad,
        results[0],
        results[1],
        results[2],
        results[3],
        results[4],
        results[5],
        results[6],
        results[7],
        results[8],
        results[9],
        results[10],
        results[11],
        results[12],
        results[13],
        results[14],
        results[15],
        results[16],
        results[17],
        grad_norm,
    )


def cost(us):
    return pl.CostEstimate(flops=int(us * 1.1e9), transcendentals=0, bytes_accessed=1 << 20)


def params():
    return pltpu.CompilerParams(vmem_limit_bytes=VMEM_LIMIT)


def call(kernel, name, us, grid, in_specs, out_specs, out_shape, scratch, *args, aliases={}):
    return pl.pallas_call(
        kernel,
        grid_spec=pltpu.PrefetchScalarGridSpec(
            num_scalar_prefetch=1,
            grid=grid,
            in_specs=in_specs,
            out_specs=out_specs,
            scratch_shapes=scratch,
        ),
        out_shape=out_shape,
        input_output_aliases=aliases,
        compiler_params=params(),
        cost_estimate=cost(us),
        name=name,
    )(*args)


def shape(dims, kind):
    return jax.ShapeDtypeStruct(dims, kind)


def token_block(rows, width, f):
    return pl.BlockSpec((1, rows, width), lambda *a: (f(*a), 0, 0))


VMEM = pl.BlockSpec(memory_space=pltpu.VMEM)


def call_once(kernel, name, us, limit, in_specs, out_specs, out_shape, scratch, *args):
    return pl.pallas_call(
        kernel,
        in_specs=in_specs,
        out_specs=out_specs,
        out_shape=out_shape,
        scratch_shapes=scratch,
        compiler_params=pltpu.CompilerParams(vmem_limit_bytes=limit << 20),
        cost_estimate=cost(us),
        name=name,
    )(*args)


def forward_call(seqs, nz, info, x6, got, x6_o, got_o, *weight_in):
    rows, width = x6.shape[1:]
    wide, slots = width // 2, 4 * rows
    n = len(seqs)
    outs = [shape((width, 3 * wide), BF16)] if 0 in seqs else []
    outs += [
        shape((n, slots, 3 * wide), BF16),
        shape((n, 2, rows, wide), BF16),
        shape((n, 2, rows, wide), BF16),
        shape((n, 8, slots), F32),
    ]
    return call_once(
        partial(attend_forward, seqs, nz), "attend_forward", 2 * n, 58,
        [SMEM] + [ANY] * 4 + ([VMEM] * PIECES if 0 in seqs else [ANY]), [ANY] * len(outs), outs,
        [
            pltpu.VMEM((n, 8, slots), F32),
            pltpu.VMEM((n, 4, rows, width), BF16),
            pltpu.VMEM((n, slots, 3 * wide), BF16),
            pltpu.VMEM((n, 2, 2, rows, wide), BF16),
            pltpu.VMEM((slots, wide), BF16),
            pltpu.VMEM((slots, 128), F32),
            pltpu.VMEM((width, 3 * wide), BF16),
            pltpu.SemaphoreType.DMA((n, 10)),
        ],
        info, x6, got, x6_o, got_o, *weight_in)


def backward_call(s, last, info, x6, got, x6_o, got_o, *ins):
    rows, width = x6.shape[1:]
    wide, slots = width // 2, 4 * rows
    r1 = width // 32
    grad_in = len(ins) > 7
    g_out = [shape((width, 3 * wide), F32)]
    if last:
        nz = 4
        g_out = [shape((2, nz, 2 * r1, 3 * wide), F32), shape((2, nz, 2 * r1, 3 * wide), BF16)]
    outs = g_out + [shape((1, 2, rows, width), BF16)] * 2
    return call_once(
        partial(attend_backward, s, grad_in, last), "attend_backward", 1, 32 if grad_in else 58,
        [SMEM] + [ANY] * (4 + len(ins)), [ANY] * len(outs), outs,
        ([pltpu.VMEM(v.shape, v.dtype) for v in g_out] if last else []) + [
            pltpu.VMEM((slots, wide), BF16),
            pltpu.VMEM((8, slots), F32),
            pltpu.VMEM((slots, wide), BF16),
            pltpu.VMEM((slots, wide), F32),
            pltpu.VMEM((slots, wide), F32),
            pltpu.VMEM((4, rows, width), BF16),
            pltpu.VMEM((width, 3 * wide), BF16),
            pltpu.VMEM((1, slots, 3 * wide), BF16),
            pltpu.VMEM((1, 8, slots), F32),
            pltpu.VMEM((2, 2, rows, wide), BF16),
            pltpu.VMEM((2, 2, rows, wide), BF16),
            pltpu.VMEM((width, 3 * wide), F32),
            pltpu.VMEM((2, rows, width), BF16),
            pltpu.VMEM((2, rows, width), BF16),
            pltpu.SemaphoreType.DMA((19,)),
        ],
        info, x6, got, x6_o, got_o, *ins)


def feed_call(info, alphas, x6, got, c6, c_got, *rest):
    seqs, rows, width = got.shape
    wide = width // 2
    rails = rest[4:]
    nz, blob_rows = rails[0].shape[:2]
    devices = nz * 8
    r1 = width // devices
    hidden = ((blob_rows - 16) // r1 - 1) // 2 * width
    act = pl.BlockSpec((1, 2, rows, wide), lambda t, i: (t, 0, 0, 0))
    pair = pl.BlockSpec((1, 2, rows, width), lambda t, i: (t, 0, 0, 0))
    by_seq = token_block(rows, width, lambda t, i: t)
    by_own = token_block(rows, width, lambda t, i: i[OWN + t])
    outs = [
        shape((seqs, rows, width), BF16),
        shape((seqs, rows, width), BF16),
        shape((seqs, 2, rows, width), F32),
        shape((seqs, 2, rows, wide), BF16),
        shape((seqs, 2, rows, wide), BF16),
        shape((2, 2, 2, nz, blob_rows // 2, width), BF16),
        shape((2, 2, 2, nz, blob_rows // 2, width), BF16),
        shape((8, width), F32),
    ]
    return call(
        partial(feed, nz), "feed", 35, (seqs,),
        [SMEM, by_own, by_seq, by_own, by_seq] + [whole(v.shape) for v in rest],
        [by_seq, by_seq, pair, act, act] + [whole(v.shape) for v in outs[5:]],
        outs,
        [
            pltpu.VMEM((width, width), BF16),
            pltpu.VMEM((width, hidden), BF16),
            pltpu.VMEM((hidden, width), BF16),
            pltpu.VMEM((16, width), F32),
            pltpu.VMEM((width, width), F32),
            pltpu.VMEM((width, hidden), F32),
            pltpu.VMEM((hidden, width), F32),
            pltpu.VMEM((8, hidden), F32),
            pltpu.VMEM((8, width), F32),
            pltpu.VMEM((16, width), F32),
            pltpu.VMEM((2 * rows, hidden), BF16),
            pltpu.VMEM((2 * rows, hidden), F32),
            pltpu.VMEM((2 * rows, width), BF16),
            pltpu.VMEM((2 * rows, width), F32),
            pltpu.VMEM((2 * rows, width), F32),
            pltpu.VMEM((2, 2 * rows, wide), BF16),
        ],
        info, alphas, x6, got, c6, c_got, *rest)


def fast_body(
    tokens,
    cotangent,
    lengths,
    project_matrix,
    output_matrix,
    expand_matrix,
    reduce_matrix,
    biases,
    alphas,
    project_first,
    project_second,
    output_first,
    output_second,
    expand_first,
    expand_second,
    reduce_first,
    reduce_second,
    bias_first,
    bias_second,
    alpha_first,
    alpha_second,
):
    rows, seq_dev, width = tokens.shape
    hidden = expand_matrix.shape[1]
    devices = lax.axis_size(BOTH)
    nz = devices // 8
    seqs = seq_dev // 2
    slots = 4 * rows
    wide = width // 2
    table = routes(nz)

    def move(v, way):
        return lax.ppermute(v, BOTH, table[way])

    def after(v, *deps):
        return lax.optimization_barrier((v,) + deps)[0]

    def at(v, axis, index):
        return lax.dynamic_index_in_dim(v, index, axis, False)

    def add(a, b):
        return a.astype(F32) + b.astype(F32)

    ctx, dp = lax.axis_index("ctx"), lax.axis_index("dp")
    y, c, z, x = ctx // 2, ctx % 2, dp // 2, dp % 2
    me = dp * 4 + ctx

    x6 = jnp.transpose(tokens, (1, 0, 2))
    c6 = jnp.transpose(cotangent, (1, 0, 2))
    place = jnp.stack([c, y, z, x]).astype(jnp.int32)
    vmem = pl.BlockSpec(memory_space=pltpu.VMEM)
    info, wq_own, wq_give, x_give = pl.pallas_call(
        prepare,
        in_specs=[SMEM, SMEM, vmem, ANY],
        out_specs=[SMEM, vmem, vmem, vmem],
        out_shape=[
            shape((INFO,), jnp.int32),
            shape((project_matrix.shape[0], 3 * wide), BF16),
            shape((project_matrix.shape[0], 3 * wide), BF16),
            shape((seqs, rows, width), BF16),
        ],
        scratch_shapes=[pltpu.SemaphoreType.DMA((seqs,))],
        compiler_params=params(),
        cost_estimate=cost(2),
        name="prepare",
    )(place, lengths, project_matrix, x6)
    got = move(x_give, "y")
    wq_got = move(wq_give, "core")
    wq_chip = jnp.where(
        c == 0, jnp.concatenate([wq_own, wq_got], 0), jnp.concatenate([wq_got, wq_own], 0)
    )
    r1, r2 = output_matrix.shape[0], reduce_matrix.shape[0]
    groups = hidden // width
    blob_rows = (1 + groups) * r1 + r2 + 16
    bias_rows = jnp.zeros((16 * width,), BF16)
    bias_rows = lax.dynamic_update_slice_in_dim(
        bias_rows, biases.astype(BF16), me * biases.shape[0], 0
    ).reshape(16, width)
    blob = pl.pallas_call(
        pack,
        in_specs=[vmem] * 4,
        out_specs=vmem,
        out_shape=shape((blob_rows, width), BF16),
        compiler_params=params(),
        cost_estimate=cost(1),
        name="pack",
    )(output_matrix, expand_matrix, reduce_matrix, after(bias_rows, wq_give))
    bz1 = move(blob, 1)
    x6_o = move(after(x6, wq_chip), "core")
    c_give = call(
        give, "give", 1, (seqs,), [token_block(rows, width, lambda t, i: i[OTHER + t])],
        token_block(rows, width, lambda t, i: t), shape((seqs, rows, width), BF16),
        [], after(info, blob), c6)
    wz = [move(wq_chip, r) for r in range(1, nz)]
    wa = jnp.stack([wq_chip] + wz)
    bz01 = jnp.stack([blob, bz1])
    bz23 = move(after(bz01, *wz), 2)
    wax, way, wad = move(after(wa, got, c_give), "x"), move(wa, "y"), move(wa, "xy")
    ba = jnp.concatenate([bz01, after(bz23, wax, way, wad)], 0)
    got_o = move(after(got, ba, wa), "core")
    bax, bay = move(ba, "x"), move(ba, "y")

    xs4 = (x6, got, x6_o, got_o)
    wq_full, *first = forward_call((0,), nz, after(info, ba, c_give), *xs4, wa, wax, way, wad)
    lse = first[3]
    bad = move(after(bay, lse), "x")
    c_got = move(after(c_give, bay, lse), "y")
    ba_o, bax_o, bay_o = (move(after(v, lse), "core") for v in (ba, bax, bay))
    o_first = move(first[2], "core")
    others = forward_call(tuple(range(1, seqs)), nz, after(info, bax, bay), *xs4, wq_full)
    o_others = move(after(others[2], c_got, ba_o, bax_o, bay_o, o_first), "core")
    kept = [first] + [others] * (seqs - 1)
    rail = (ba, bax, bay, bad)
    rail_o = (ba_o, bax_o, bay_o, move(after(bad, o_others), "core"))

    own_o = (first[1], others[1])
    oth_o = (o_first, o_others)
    mixed_m, mixed_g, dy, do_keep, do_send, g_send, g_keep, ga = feed_call(
        info, alphas, x6, got, c6, c_got, *own_o, *oth_o, *rail, *rail_o
    )

    do_recv = move(do_send, "core")
    g_recv = move(after(g_send, do_recv), "core")

    def backward(s, last, grad, *deps):
        qkv, ok, osend, lse = kept[s]
        ins = (wq_full, qkv, lse, ok, osend, do_keep, do_recv) + (() if grad is None else (grad,))
        return backward_call(s, last, after(info, *deps) if deps else info, *xs4, *ins)

    keeps, sends, recvs = [None] * seqs, [None] * seqs, [None] * seqs
    grad, keeps[2], sends[2] = backward(2, False, None)
    g_recv_late = after(g_recv, sends[2])
    ga_send = add(g_keep[0, 1], g_recv_late[0, 1]).astype(BF16)
    gb_send = add(g_keep[1, 1], g_recv_late[1, 1]).astype(BF16)
    ra, rb = move(ga_send, "x"), move(gb_send, "y")
    recvs[2] = move(sends[2], "core")
    mixed_r = move(mixed_g, "y")
    grad, keeps[0], sends[0] = backward(0, False, grad, ga_send, gb_send, mixed_r)
    ra, rb = after(ra, sends[0]), after(rb, sends[0])
    fa = g_keep[0, 0], g_recv[0, 0], ra
    fb = g_keep[1, 0], g_recv[1, 0], rb

    def part(three, index):
        return sum(v[index].astype(F32) for v in three)

    ga_send, gb_send = part(fa, 1).astype(BF16), part(fb, 1).astype(BF16)
    ra, rb = move(ga_send, "y"), move(gb_send, "x")
    recvs[0] = move(sends[0], "core")
    qkeep, qsend, keeps[1], sends[1] = backward(1, True, grad, ga_send, gb_send, recvs[2], recvs[0])
    ra, rb = after(ra, sends[1]), after(rb, sends[1])
    qr = move(after(qsend, ra, rb), "x")
    recvs[1] = move(sends[1], "core")
    fv = jnp.concatenate([add(part(fa, 0), ra), add(part(fb, 0), rb)], 1).astype(BF16)
    fgot = [move(fv[r], r) for r in range(1, nz)]
    half = pl.BlockSpec((1, 1, rows, width), lambda *_: (0, 0, 0, 0))
    six = (seq_dev, rows, width)
    mixed6 = call(
        placed, "placed", 1, (1,), [whole(mixed_m.shape)] * 2, whole(six), shape(six, BF16), [],
        after(info, fv), mixed_m, mixed_r)
    gq = add(qkeep, qr)
    gq_send = gq[1].astype(BF16)
    qr = move(after(gq_send, mixed6), "y")
    back = move(
        after(
            jnp.concatenate([(d[None] + add(k[:, 1], r[:, 1])).astype(BF16) for d, k, r in zip(dy[:, 1], keeps, recvs)], 0),
            gq_send,
        ),
        "y",
    )
    input6 = call(
        placed_own, "placed_own", 1, (seqs,),
        [pl.BlockSpec((1, 1, rows, width), lambda t, i: (t, 0, 0, 0))] + [half] * 6,
        token_block(rows, width, lambda t, i: i[OWN + t]), shape(six, F32), [],
        after(info, gq_send), dy, *keeps, *recvs)
    gq = add(gq[0], qr)
    gq = after(gq, input6)
    qgot = [move(gq[r].astype(BF16), r) for r in range(1, nz)]
    fin_in = (gq, *qgot, fv, *fgot, ga)
    one = lambda v: whole((1,) + v.shape[1:])
    fin_out = [shape((r1, 3 * wide), F32)] * 2 + [shape((devices, 128), F32), shape((blob_rows, width), F32)]
    q_own, q_give, tiny, blob_sum = call(
        finish, "finish", 1, (1,),
        [one(gq)] + [whole(v.shape) for v in qgot] + [one(fv)] + [whole(v.shape) for v in fgot + [ga]],
        [whole(v.shape) for v in fin_out], fin_out,
        [], info, *fin_in)
    tiny = lax.all_to_all(tiny.reshape(devices, 1, 128), BOTH, 0, 0).reshape(devices, 128)
    q_got = move(q_give, "core")

    input6 = call(
        placed_rest, "placed_rest", 1, (1,), [whole(back.shape), ANY], ANY, shape(six, F32),
        [pltpu.VMEM(back.shape, F32), pltpu.SemaphoreType.DMA((seqs,))], info, back, input6,
        aliases={2: 0})
    g_bias = lax.dynamic_slice_in_dim(
        blob_sum[blob_rows - 16 :].reshape(-1), me * biases.shape[0], biases.shape[0], 0
    )
    states = (
        project_matrix, project_first, project_second,
        output_matrix, output_first, output_second,
        expand_matrix, expand_first, expand_second,
        reduce_matrix, reduce_first, reduce_second,
        biases[None], bias_first[None], bias_second[None],
        alphas[None], alpha_first[None], alpha_second[None],
    )
    outs = [shape(v.shape, F32) for v in states] + [shape((1, 1), F32)]
    ins = (tiny, q_own, q_got, blob_sum, g_bias[None], *states)
    res = call(
        update, "update", 3, (1,), [whole(v.shape) for v in ins], [whole(v.shape) for v in outs], outs, [],
        after(info, input6), *ins)
    mixed = jnp.transpose(mixed6, (1, 0, 2))
    input_grad = jnp.transpose(input6, (1, 0, 2))
    results = list(res[:12]) + [v[0] for v in res[12:18]]
    return (mixed, input_grad, *results, res[18][0, 0])


def solution(mesh):
    ctx, dp = mesh.shape["ctx"], mesh.shape["dp"]
    row = P(BOTH, None)
    flat = P(BOTH)
    token = P("ctx", "dp", None)
    body = fast_body if (ctx == 4 and dp == 8) else generic_body
    return jax.shard_map(
        body,
        mesh=mesh,
        in_specs=(token, token, P("dp"), row, row, row, row, flat, P())
        + (row,) * 8
        + (flat, flat, P(), P()),
        out_specs=(token, token) + (row,) * 12 + (flat,) * 3 + (P(),) * 4,
        check_vma=False,
    )
```

```python
from functools import partial

import jax
import jax.numpy as jnp
from jax import lax
from jax.experimental import pallas as pl
from jax.experimental.pallas import tpu as pltpu
from jax.sharding import PartitionSpec as P

HEADS = 8
HEAD = 64
STEP = 10


clip_bound = 1.0
beta_one = 0.9
beta_two = 0.999
adam_eps = 1e-08
matrix_rate = 0.05
alpha_rate = 0.2
decay_rate = 0.1

BOTH = ("dp", "ctx")
F32 = jnp.float32
BF16 = jnp.bfloat16
VMEM_LIMIT = 56 * 1024 * 1024


def adamw(weight, first, second, grad, rate, decay):
    first = beta_one * first + (1.0 - beta_one) * grad
    second = beta_two * second + (1.0 - beta_two) * grad * grad
    mhat = first / (1.0 - beta_one**STEP)
    vhat = second / (1.0 - beta_two**STEP)
    weight = weight - rate * (mhat / (jnp.sqrt(vhat) + adam_eps) + decay * weight)
    return (first, second, weight)


def dot_nn(a, b):
    return lax.dot_general(a, b, (((1,), (0,)), ((), ())), preferred_element_type=F32)


def dot_nt(a, b):
    return lax.dot_general(a, b, (((1,), (1,)), ((), ())), preferred_element_type=F32)


def dot_tn(a, b):
    return lax.dot_general(a, b, (((0,), (0,)), ((), ())), preferred_element_type=F32)


CORE, CHIP_Y, CHIP_Z, CHIP_X, LENS, OWN, OTHER, INFO = 0, 1, 2, 3, 4, 7, 10, 13


def block_places(info, rows):
    core, y = info[CORE], info[CHIP_Y]
    return [
        pl.multiple_of(b * rows, rows)
        for b in (
            2 * y + core,
            2 * (1 - y) + core,
            2 * y + 1 - core,
            2 * (1 - y) + 1 - core,
        )
    ]


def chip_index(info, r, fx, fy):
    z = info[CHIP_Z] ^ r
    x = info[CHIP_X] ^ fx
    y = info[CHIP_Y] ^ fy
    return (z * 2 + x) * 2 + y


PIECES = 4


def gathered_pieces(nz):
    places = ((0, 0), (1, 0), (0, 1), (1, 1))
    return [(i, r, r, fx, fy) for i, (fx, fy) in enumerate(places) for r in range(nz)]


def sequence_copies(s, info, four, x_s, sems):
    own = info[OWN + s]
    at = (own, s, own, s)
    return [pltpu.make_async_copy(v.at[i], x_s.at[b], sems.at[b]) for b, (v, i) in enumerate(zip(four, at))]


def attend_forward(seqs, nz, info, *refs):
    refs = list(refs)
    four = [refs.pop(0) for _ in range(4)]
    x_s, qkv_s, oo_s, o_s, st_s, w_s, sems = refs[-7:]
    refs = refs[:-7]
    assemble = 0 in seqs
    copies = [sequence_copies(s, info, four, x_s.at[i], sems.at[i]) for i, s in enumerate(seqs)]
    pieces = [refs.pop(0) for _ in range(PIECES if assemble else 1)]
    wq_out = refs.pop(0) if assemble else None
    qkv_out, ok_out, os_out, lse_out, lse_s = refs
    for copy in copies[0]:
        copy.start()

    if assemble:
        rows = pieces[0].shape[1]
        for which, at, r, fx, fy in gathered_pieces(nz):
            place = pl.multiple_of(chip_index(info, r, fx, fy) * rows, rows)
            w_s[pl.ds(place, rows), :] = pieces[which][at]
    else:
        weight = pltpu.make_async_copy(pieces[0], w_s, sems.at[0, 9])
        weight.start()
        weight.wait()
    for more in copies[1:]:
        for copy in more:
            copy.start()
    rows = x_s.shape[2]
    places = block_places(info, rows)
    lane = lax.broadcasted_iota(jnp.int32, (rows, 128), 1)
    low_lane = lane < HEAD
    row_i = lax.broadcasted_iota(jnp.int32, (rows, rows), 0)
    col_i = lax.broadcasted_iota(jnp.int32, (rows, rows), 1)

    def one(i, length, qb, n):
        wide = 256
        span = slice(qb * rows, (qb + 1) * rows)
        base = (n - 1) * rows
        ok = (base + col_i) < length
        if n == qb + 1:
            ok = ok & (col_i <= row_i)
        scores, values = [], []
        for pair in range(2):
            at = pair * 128
            q = qkv_s[i, span, at : at + 128]
            k = qkv_s[i, 0 : n * rows, wide + at : wide + at + 128]
            v = qkv_s[i, 0 : n * rows, 2 * wide + at : 2 * wide + at + 128]
            values.append(jnp.concatenate([v, jnp.ones_like(v)], axis=1))
            for h in range(2):
                mine = low_lane if h == 0 else jnp.logical_not(low_lane)
                qm = jnp.where(mine, q * jnp.asarray(HEAD**-0.5, BF16), jnp.zeros_like(q))
                scores.append(dot_nt(qm, k))
        stats = jnp.zeros((rows, 128), F32)
        res = []
        for head, sc in enumerate(scores):
            last = jnp.where(ok, sc[:, base:], -1e30)
            sc = jnp.concatenate([sc[:, :base], last], axis=1) if n > 1 else last
            top = jnp.max(sc, axis=1, keepdims=True)
            e = jnp.exp(sc - top).astype(BF16)
            ob = dot_nn(e, values[head // 2])
            den = ob[:, 128:]
            res.append(ob[:, :128] / den)
            stats = jnp.where(lane == head, top + jnp.log(den), stats)
        st_s[span, :] = stats
        for pair in range(2):
            o_s[span, pair * 128 : pair * 128 + 128] = jnp.where(
                low_lane, res[2 * pair], res[2 * pair + 1]
            ).astype(BF16)

    def results(i):
        pairs = [
            (qkv_s.at[i], qkv_out.at[i]),
            (oo_s.at[i, 1], os_out.at[i]),
            (oo_s.at[i, 0], ok_out.at[i]),
            (lse_s.at[i], lse_out.at[i]),
        ]
        return [pltpu.make_async_copy(src, dst, sems.at[i, 4 + k]) for k, (src, dst) in enumerate(pairs)]

    def sequence(i, s):
        length = info[LENS + s]
        outs = results(i)
        waits = sequence_copies(s, info, four, x_s.at[i], sems.at[i])
        w = w_s[...]
        for b, place in enumerate(places):
            waits[b].wait()
            qkv_s[i, pl.ds(place, rows), :] = dot_nn(x_s[i, b], w).astype(BF16)
        outs[0].start()
        blocks = (length + rows - 1) // rows
        for qb in range(qkv_s.shape[1] // rows):
            for n in range(1, qb + 2):
                cond = (blocks == n) if n < qb + 1 else (blocks >= n)

                @pl.when(cond)
                def _(qb=qb, n=n):
                    one(i, length, qb, n)

        for b in range(4):
            oo_s[i, b // 2, b % 2] = o_s[pl.ds(places[b], rows), :]
        outs[1].start()
        outs[2].start()
        lse_s[i] = jnp.transpose(st_s[...])[:8]
        outs[3].start()

    if assemble:
        weight = pltpu.make_async_copy(w_s, wq_out, sems.at[0, 9])
        weight.start()
    if len(seqs) == 1:
        sequence(0, seqs[0])
    else:
        lax.fori_loop(0, len(seqs), lambda i, carry: (sequence(i, seqs[0] + i), carry)[1], 0)
    for i in range(len(seqs)):
        for copy in results(i):
            copy.wait()
    if assemble:
        weight.wait()


def attend_backward(s, grad_in, last_one, info, *refs):
    refs = list(refs)
    four = [refs.pop(0) for _ in range(4)]
    wq_ref, qkv_in, lse_in, ok_in, os_in, dk_in, dr_in = (refs.pop(0) for _ in range(7))
    g_in = refs.pop(0) if grad_in else None
    at = 0 if s == 0 else s - 1
    scratch = refs[-15:]
    (do_s, r_s, dq_s, dk_s, dv_s, x_s, w_s, qkv_ref, lse_ref, o_in, d_in, g_ref, keep_ref, send_ref,
     sems) = scratch
    refs = refs[:-15]
    if last_one:
        qkeep_out, qsend_out, keep_out, send_out, qkeep_ref, qsend_ref = refs
    else:
        g_out, keep_out, send_out = refs
    wanted = [
        (dk_in.at[s], d_in.at[0]),
        (dr_in.at[s], d_in.at[1]),
        (ok_in.at[at], o_in.at[0]),
        (os_in.at[at], o_in.at[1]),
        (lse_in.at[at], lse_ref.at[0]),
        (qkv_in.at[at], qkv_ref.at[0]),
        (wq_ref, w_s),
    ]
    if grad_in:
        wanted.append((g_in, g_ref))
    early = [pltpu.make_async_copy(src, dst, sems.at[4 + i]) for i, (src, dst) in enumerate(wanted)]
    late = sequence_copies(s, info, four, x_s, sems) + early[6:]
    early = early[:6]
    for copy in early + late:
        copy.start()
    for copy in early[:4]:
        copy.wait()
    length = info[LENS + s]
    rows = x_s.shape[1]
    places = block_places(info, rows)
    lane = lax.broadcasted_iota(jnp.int32, (rows, 128), 1)
    low_lane = lane < HEAD
    head_of = lax.broadcasted_iota(jnp.int32, (8, 256), 1) // HEAD
    pick = (head_of == lax.broadcasted_iota(jnp.int32, (8, 256), 0)).astype(BF16)
    for b in range(4):
        do = d_in[b // 2, b % 2]
        o = o_in[b // 2, b % 2]
        do_s[pl.ds(places[b], rows), :] = do
        prod = do.astype(F32) * o.astype(F32)
        high = prod.astype(BF16)
        low = (prod - high.astype(F32)).astype(BF16)
        r_s[:, pl.ds(places[b], rows)] = dot_nt(pick, high) + dot_nt(pick, low)
    dk_s[...] = jnp.zeros_like(dk_s)
    dv_s[...] = jnp.zeros_like(dv_s)
    if not grad_in:
        g_ref[...] = jnp.zeros_like(g_ref)
    for copy in early[4:]:
        copy.wait()
    key_i = lax.broadcasted_iota(jnp.int32, (rows, rows), 0)
    qry_i = lax.broadcasted_iota(jnp.int32, (rows, rows), 1)
    scale = HEAD**-0.5

    def one_all(qb):
        n = qb + 1
        wide = 256
        span = slice(qb * rows, (qb + 1) * rows)
        ok = (key_i <= qry_i) & ((qb * rows + key_i) < length)
        qms, doms, dqs = [], [], [None] * 4
        for pair in range(2):
            at = pair * 128
            q = qkv_ref[0, span, at : at + 128]
            do = do_s[span, at : at + 128]
            for h in range(2):
                mine = low_lane if h == 0 else jnp.logical_not(low_lane)
                qms.append(jnp.where(mine, q * jnp.asarray(scale, BF16), jnp.zeros_like(q)))
                doms.append(jnp.where(mine, do, jnp.zeros_like(do)))
        for kb in range(n):
            keys = slice(kb * rows, (kb + 1) * rows)
            ks = [qkv_ref[0, keys, wide + 128 * pr : wide + 128 * pr + 128] for pr in range(2)]
            vs = [qkv_ref[0, keys, 2 * wide + 128 * pr : 2 * wide + 128 * pr + 128] for pr in range(2)]
            scs = [dot_nt(ks[h // 2], qms[h]) for h in range(4)]
            dps = [dot_nt(vs[h // 2], doms[h]) for h in range(4)]
            ps, dss = [], []
            for h in range(4):
                p = jnp.exp(scs[h] - lse_ref[0, h : h + 1, span])
                if kb == qb:
                    p = jnp.where(ok, p, 0.0)
                dss.append((p * (dps[h] - r_s[h : h + 1, span])).astype(BF16))
                ps.append(p.astype(BF16))
            for pr in range(2):
                at = slice(128 * pr, 128 * pr + 128)
                dv_s[keys, at] += dot_nn(ps[2 * pr], doms[2 * pr]) + dot_nn(ps[2 * pr + 1], doms[2 * pr + 1])
                dk_s[keys, at] += dot_nn(dss[2 * pr], qms[2 * pr]) + dot_nn(dss[2 * pr + 1], qms[2 * pr + 1])
            for h in range(4):
                dqh = dot_tn(dss[h], ks[h // 2])
                dqs[h] = dqh if dqs[h] is None else dqs[h] + dqh
        for pr in range(2):
            dq_s[span, 128 * pr : 128 * pr + 128] = (
                jnp.where(low_lane, dqs[2 * pr], dqs[2 * pr + 1]) * scale
            ).astype(BF16)

    total = qkv_ref.shape[1] // rows
    for qb in range(total):

        @pl.when(qb * rows < length)
        def _(qb=qb):
            one_all(qb)

    for copy in late:
        copy.wait()
    w = w_s[...]
    outs = []

    def send_out_copy(src, dst):
        outs.append(pltpu.make_async_copy(src, dst, sems.at[13 + len(outs)]))
        outs[-1].start()

    for b in (2, 3, 0, 1):
        place = places[b]
        here = pl.ds(place, rows)

        @pl.when(place < length)
        def _(b=b, here=here):
            d = jnp.concatenate(
                [dq_s[here, :], dk_s[here, :].astype(BF16), dv_s[here, :].astype(BF16)], axis=1
            )
            g_ref[...] += dot_tn(x_s[b], d)
            dx = dot_nt(d, w)
            if b < 2:
                keep_ref[b] = dx.astype(BF16)
            else:
                send_ref[b - 2] = dx.astype(BF16)

        @pl.when(place >= length)
        def _(b=b):
            if b < 2:
                keep_ref[b] = jnp.zeros_like(keep_ref[b])
            else:
                send_ref[b - 2] = jnp.zeros_like(send_ref[b - 2])

        if b == 3:
            send_out_copy(send_ref, send_out.at[0])
        if b == 0:
            send_out_copy(keep_ref.at[0], keep_out.at[0, 0])
    if last_one:
        nz, part, cut = qkeep_ref.shape[2:]
        for out, dst, way in ((qsend_ref, qsend_out, 1), (qkeep_ref, qkeep_out, 0)):
            for r in range(nz):
                for other in range(2):
                    for half, (fx, fy) in enumerate(((way, other), (other, way))):
                        at = pl.multiple_of(chip_index(info, r, fx, fy) * part, part)
                        out[half, other, r] = g_ref[
                            pl.ds(at, part), half * cut : (half + 1) * cut
                        ].astype(out.dtype)
            send_out_copy(out, dst)
    else:
        send_out_copy(g_ref, g_out)
    send_out_copy(keep_ref.at[1], keep_out.at[0, 1])
    for copy in outs:
        copy.wait()


def feed(nz, info, alphas, *refs):
    refs = list(refs)
    xm, xg, cm, cg = (refs.pop(0) for _ in range(4))
    own_o = [refs.pop(0) for _ in range(2)]
    oth_o = [refs.pop(0) for _ in range(2)]
    rails = [[refs.pop(0) for _ in range(PIECES)] for _ in range(2)]
    (mixm, mixg, dy_ref, dkeep, dsend, gsend, gkeep, ga_ref,
     wo_s, w1_s, w2_s, b_s, go_s, g1_s, g2_s, gb1_s, gb2_s, ga_s,
     h_s, gp_s, yb_s, br_s, f_s, oo_s) = refs
    step = s = pl.program_id(0)
    core = info[CORE]
    chips = nz * 4
    width = wo_s.shape[1]
    groups = w1_s.shape[1] // width
    r1 = wo_s.shape[0] // (2 * chips)
    r2 = w2_s.shape[0] // (2 * chips)

    @pl.when(step == 0)
    def _():
        bias = None
        for rail in range(2):
            for which, at, r, fx, fy in gathered_pieces(nz):
                d = chip_index(info, r, fx, fy) * 2 + (core ^ rail)
                piece = rails[rail][which]
                small = pl.ds(pl.multiple_of(d * r1, r1), r1)
                wo_s[small, :] = piece[at, 0:r1]
                for j in range(groups):
                    w1_s[small, j * width : (j + 1) * width] = piece[at, (1 + j) * r1 : (2 + j) * r1]
                first = (1 + groups) * r1
                w2_s[pl.ds(pl.multiple_of(d * r2, r2), r2), :] = piece[at, first : first + r2]
                part = piece[at, first + r2 : first + r2 + 16].astype(F32)
                bias = part if bias is None else bias + part
        b_s[...] = bias
        for ref in (go_s, g1_s, g2_s, gb1_s, gb2_s, ga_s):
            ref[...] = jnp.zeros_like(ref)

    rows = xm.shape[1]
    both = 2 * rows
    y_here = info[CHIP_Y]
    length = info[LENS + s]
    begins = [(2 * y_here + core) * rows, (2 * (1 - y_here) + core) * rows]

    def pick3(three):
        return jnp.where(s == 0, three[0][0], jnp.where(s == 1, three[1][0], three[1][1])).reshape(both, -1)

    here = pl.ds(pl.multiple_of(core * 256, 256), 256)
    there = pl.ds(pl.multiple_of((1 - core) * 256, 256), 256)
    a0, a1 = alphas[0], alphas[1]
    oo_s[0] = pick3(own_o)
    oo_s[1] = pick3(oth_o)
    x = jnp.concatenate([xm[0], xg[0]], axis=0).astype(F32)
    branch = dot_nn(oo_s[0], wo_s[here, :]) + dot_nn(oo_s[1], wo_s[there, :])
    y = x + a0 * branch
    br_s[...] = branch
    yb = y.astype(BF16)
    yb_s[...] = yb
    f = None
    span = 2 * width
    for j in range(groups // 2):
        cols = slice(j * span, (j + 1) * span)
        bias = jnp.concatenate([b_s[2 * j : 2 * j + 1, :], b_s[2 * j + 1 : 2 * j + 2, :]], axis=1)
        pre = dot_nn(yb, w1_s[:, cols]) + bias
        cdf = 0.5 + 0.5 * lax.erf(pre * (0.5**0.5))
        h = (pre * cdf).astype(BF16)
        h_s[:, cols] = h
        gp_s[:, cols] = cdf + pre * (jnp.exp(-0.5 * pre * pre) * 0.3989422804014327)
        part = dot_nn(h, w2_s[cols, :])
        f = part if f is None else f + part
    f = f + b_s[groups : groups + 1, :]
    f_s[...] = f
    mixed = (y + a1 * f).astype(BF16)
    mixm[0] = mixed[:rows]
    mixg[0] = mixed[rows:]

    def back(at, count, cot, begin_rows):
        span = pl.ds(at, count)
        g = jnp.where(begin_rows < length, cot.astype(F32), 0.0)
        df = (a1 * g).astype(BF16)
        gb2_s[...] += jnp.sum(df.astype(F32).reshape(count // 8, 8, width), axis=0)
        yb = yb_s[span, :]
        dy = g
        for j in range(groups):
            cols = slice(j * width, (j + 1) * width)
            dh = dot_nt(df, w2_s[cols, :])
            dpre = (dh * gp_s[span, cols]).astype(BF16)
            gb1_s[:, cols] += jnp.sum(dpre.astype(F32).reshape(count // 8, 8, width), axis=0)
            g2_s[cols, :] += dot_tn(h_s[span, cols], df)
            g1_s[:, cols] += dot_tn(yb, dpre)
            dy = dy + dot_nt(dpre, w1_s[:, cols])
        ga_s[0:8, :] += jnp.sum((br_s[span, :] * dy).reshape(count // 8, 8, width), axis=0)
        ga_s[8:16, :] += jnp.sum((f_s[span, :] * g).reshape(count // 8, 8, width), axis=0)
        db = (a0 * dy).astype(BF16)
        go_s[here, :] += dot_tn(oo_s[0, span, :], db)
        go_s[there, :] += dot_tn(oo_s[1, span, :], db)
        return dy, dot_nt(db, wo_s[here, :]).astype(BF16), dot_nt(db, wo_s[there, :]).astype(BF16)

    late = jnp.maximum(begins[0], begins[1])
    early = jnp.minimum(begins[0], begins[1])
    row = lax.broadcasted_iota(jnp.int32, (rows, width), 0)

    @pl.when(late < length)
    def _():
        where = jnp.concatenate([begins[0] + row, begins[1] + row], axis=0)
        dy, keep, send = back(0, both, jnp.concatenate([cm[0], cg[0]], axis=0), where)
        dy_ref[0] = dy.reshape(2, rows, width)
        dkeep[0] = keep.reshape(2, rows, -1)
        dsend[0] = send.reshape(2, rows, -1)

    @pl.when(late >= length)
    def _():
        dkeep[...] = jnp.zeros_like(dkeep)
        dsend[...] = jnp.zeros_like(dsend)
        dy_ref[...] = jnp.zeros_like(dy_ref)

        @pl.when(early < length)
        def _():
            half = pl.multiple_of(y_here * rows, rows)
            cot = jnp.where(y_here == 0, cm[0], cg[0])
            dy, keep, send = back(half, rows, cot, early + row)
            dy_ref[0, y_here] = dy
            dkeep[0, y_here] = keep
            dsend[0, y_here] = send

    @pl.when(step == pl.num_programs(0) - 1)
    def _():
        gb = jnp.concatenate(
            [jnp.sum(gb1_s[:, j * width : (j + 1) * width], axis=0, keepdims=True) for j in range(groups)]
            + [jnp.sum(gb2_s[...], axis=0, keepdims=True), jnp.zeros((16 - groups - 1, width), F32)],
            axis=0,
        ).astype(BF16)
        for out, whose in ((gkeep, core), (gsend, 1 - core)):
            for r in range(nz):
                for fx in range(2):
                    for fy in range(2):
                        d = chip_index(info, r, fx, fy) * 2 + whose
                        small = pl.ds(pl.multiple_of(d * r1, r1), r1)
                        out[0, fx, fy, r, 0:r1] = go_s[small, :].astype(BF16)
                        for j in range(groups):
                            out[0, fx, fy, r, (1 + j) * r1 : (2 + j) * r1] = g1_s[
                                small, j * width : (j + 1) * width
                            ].astype(BF16)
                        out[1, fy, fx, r, 0:r2] = g2_s[
                            pl.ds(pl.multiple_of(d * r2, r2), r2), :
                        ].astype(BF16)
                        out[1, fy, fx, r, r2 : r2 + 16] = gb
        ga_ref[0:1, :] = jnp.sum(ga_s[0:8, :], axis=0, keepdims=True)
        ga_ref[1:2, :] = jnp.sum(ga_s[8:16, :], axis=0, keepdims=True)


def prepare(place, lengths, wq, x_ref, info, w_own, w_give, xg_ref, sems):
    six = lengths.shape[0]
    seqs = six // 2
    y = place[1]
    ranks = []
    for i in range(six):
        rank = jnp.int32(0)
        for j in range(six):
            if j != i:
                longer = lengths[j] >= lengths[i] if j < i else lengths[j] > lengths[i]
                rank = rank + longer.astype(jnp.int32)
        ranks.append(rank)
    order = [0] + list(range(3, six, 2)) + [1] + list(range(2, six, 2))
    ids = []
    for r in order:
        ids.append(sum(jnp.where(ranks[i] == r, i, 0) for i in range(six)))
    own = [jnp.where(y == 0, ids[s], ids[seqs + s]) for s in range(seqs)]
    other = [jnp.where(y == 0, ids[seqs + s], ids[s]) for s in range(seqs)]
    copies = [pltpu.make_async_copy(x_ref.at[other[s]], xg_ref.at[s], sems.at[s]) for s in range(seqs)]
    for copy in copies:
        copy.start()
    for i in range(4):
        info[i] = place[i]
    for s in range(seqs):
        info[LENS + s] = lengths[own[s]]
        info[OWN + s] = own[s]
        info[OTHER + s] = other[s]
    wide = wq.shape[1] // 6
    core = place[0]
    for j in range(3):
        left = wq[:, 2 * j * wide : (2 * j + 1) * wide]
        right = wq[:, (2 * j + 1) * wide : (2 * j + 2) * wide]
        cols = slice(j * wide, (j + 1) * wide)
        w_own[:, cols] = jnp.where(core == 0, left, right).astype(BF16)
        w_give[:, cols] = jnp.where(core == 0, right, left).astype(BF16)
    for copy in copies:
        copy.wait()


def give(info, c_ref, cg_ref):
    cg_ref[...] = c_ref[...]


def pack(wo, w1, w2, bias, out):
    rows, width = wo.shape
    groups = w1.shape[1] // width
    out[0:rows] = wo[...].astype(BF16)
    for j in range(groups):
        out[(1 + j) * rows : (2 + j) * rows] = w1[:, j * width : (j + 1) * width].astype(BF16)
    first = (1 + groups) * rows
    out[first : first + w2.shape[0]] = w2[...].astype(BF16)
    out[first + w2.shape[0] :] = bias[...]


def finish(info, gq, r1, r2, r3, fv, f1, f2, f3, ga, q_own, q_give, tiny, blob):
    total = gq[0]
    for r in (r1, r2, r3):
        total = total + r[...].astype(F32)
    rows = q_own.shape[0]
    core = info[CORE]
    tiny_rows = tiny.shape[0]
    sums = jnp.sum(total * total)
    blob[...] = fv[0].astype(F32) + f1[...].astype(F32) + f2[...].astype(F32) + f3[...].astype(F32)
    main = blob.shape[0] - 16
    own = blob[0:main, :]
    sums = sums + jnp.sum(own * own)
    me = ((info[CHIP_Z] * 2 + info[CHIP_X]) * 2 + info[CHIP_Y]) * 2 + core
    bias = blob[main:, :]
    width = bias.shape[1]
    count = 5 * width // tiny_rows
    flat = lax.broadcasted_iota(jnp.int32, bias.shape, 0) * width + lax.broadcasted_iota(
        jnp.int32, bias.shape, 1
    )
    ours = (flat >= me * count) & (flat < (me + 1) * count)
    sums = sums + jnp.sum(jnp.where(ours, bias * bias, 0.0))
    low, high = total[:rows], total[rows:]
    q_own[...] = jnp.where(core == 0, low, high)
    q_give[...] = jnp.where(core == 0, high, low)
    lane = lax.broadcasted_iota(jnp.int32, tiny.shape, 1)
    a0, a1 = jnp.sum(ga[0:1, :]), jnp.sum(ga[1:2, :])
    tiny[...] = jnp.where(lane == 0, sums, jnp.where(lane == 1, a0, jnp.where(lane == 2, a1, 0.0)))


def placed(info, mixm, mixr, mixed):
    for s in range(mixm.shape[0]):
        mixed[info[OWN + s]] = mixm[s]
        mixed[info[OTHER + s]] = mixr[s]


def placed_own(info, dy, k0, k1, k2, r0, r1, r2, grad):
    step = pl.program_id(0)
    for s, (k, r) in enumerate(((k0, r0), (k1, r1), (k2, r2))):

        @pl.when(step == s)
        def _(k=k, r=r):
            grad[0] = dy[0, 0] + (k[0, 0].astype(F32) + r[0, 0].astype(F32))


def placed_rest(info, early, late, grad_in, grad, wide_s, sems):
    copies = []
    for i, (ref, at, s) in enumerate(((early, 0, 2), (early, 1, 0), (late, 0, 1))):
        wide_s[i] = ref[at].astype(F32)
        copies.append(pltpu.make_async_copy(wide_s.at[i], grad.at[info[OTHER + s]], sems.at[i]))
        copies[-1].start()
    for copy in copies:
        copy.wait()


def update(info, tiny, q_own, q_got, blob, g_bias, *refs):
    ins, outs = refs[:18], refs[18:]
    squares = jnp.sum(tiny[:, 0:1])
    a0, a1 = jnp.sum(tiny[:, 1:2]), jnp.sum(tiny[:, 2:3])
    norm = jnp.sqrt(jnp.zeros((1, 1), F32) + (squares + a0 * a0 + a1 * a1))
    factor = jnp.minimum(1.0, clip_bound / (norm + 1e-06))
    outs[18][...] = norm
    rows = q_own.shape[0]
    wide = q_own.shape[1] // 3

    def put(i, place, grad, rate, decay):
        if grad.ndim == 1:
            f = jnp.zeros(grad.shape, F32) + factor[0, 0]
        else:
            f = factor
        res = adamw(ins[3 * i][place], ins[3 * i + 1][place], ins[3 * i + 2][place], f * grad, rate, decay)
        for j in range(3):
            outs[3 * i + j][place] = res[j]

    core = info[CORE]
    for j in range(3):
        left = q_own[:, j * wide : (j + 1) * wide]
        right = q_got[:, j * wide : (j + 1) * wide]
        both = (jnp.where(core == 0, left, right), jnp.where(core == 0, right, left))
        for k in range(2):
            at = (2 * j + k) * wide
            put(0, (slice(None), slice(at, at + wide)), both[k], matrix_rate, decay_rate)
    width = blob.shape[1]
    groups = ins[6].shape[1] // width
    put(1, (slice(None), slice(None)), blob[0:rows, :], matrix_rate, decay_rate)
    for j in range(groups):
        put(2, (slice(None), slice(j * width, (j + 1) * width)), blob[(1 + j) * rows : (2 + j) * rows, :],
            matrix_rate, decay_rate)
    first = (1 + groups) * rows
    put(3, (slice(None), slice(None)), blob[first : first + ins[9].shape[0], :], matrix_rate, decay_rate)
    put(4, (slice(None), slice(None)), g_bias[...], matrix_rate, 0.0)
    lane = lax.broadcasted_iota(jnp.int32, (1, 2), 1)
    put(5, (slice(None), slice(None)), jnp.where(lane == 0, a0, a1), alpha_rate, 0.0)


def whole(shape):
    return pl.BlockSpec(shape, lambda *_: (0,) * len(shape))


SMEM = pl.BlockSpec(memory_space=pltpu.SMEM)
ANY = pl.BlockSpec(memory_space=pl.ANY)


def routes(nz):
    def perm(to):
        out = []
        for z in range(nz):
            for x in range(2):
                for y in range(2):
                    for c in range(2):
                        z2, x2, y2, c2 = to(z, x, y, c)
                        out.append((((z * 2 + x) * 4 + y * 2 + c), ((z2 * 2 + x2) * 4 + y2 * 2 + c2)))
        return out

    table = {
        "core": perm(lambda z, x, y, c: (z, x, y, 1 - c)),
        "y": perm(lambda z, x, y, c: (z, x, 1 - y, c)),
        "x": perm(lambda z, x, y, c: (z, 1 - x, y, c)),
        "xy": perm(lambda z, x, y, c: (z, 1 - x, 1 - y, c)),
    }
    for r in range(1, nz):
        table[r] = perm(lambda z, x, y, c, r=r: (z ^ r, x, y, c))
    return table


def generic_body(
    tokens,
    cotangent,
    lengths,
    project_matrix,
    output_matrix,
    expand_matrix,
    reduce_matrix,
    biases,
    alphas,
    project_first,
    project_second,
    output_first,
    output_second,
    expand_first,
    expand_second,
    reduce_first,
    reduce_second,
    bias_first,
    bias_second,
    alpha_first,
    alpha_second,
):
    slot_dev, seq_dev, width = tokens.shape
    ctx_index = lax.axis_index("ctx")
    qpos = ctx_index * slot_dev + jnp.arange(slot_dev, dtype=jnp.int32)
    gathered = (
        lax.all_gather(project_matrix.astype(jnp.bfloat16), ("dp", "ctx"), axis=0, tiled=True),
        lax.all_gather(output_matrix.astype(jnp.bfloat16), ("dp", "ctx"), axis=0, tiled=True),
        lax.all_gather(expand_matrix.astype(jnp.bfloat16), ("dp", "ctx"), axis=0, tiled=True),
        lax.all_gather(reduce_matrix.astype(jnp.bfloat16), ("dp", "ctx"), axis=0, tiled=True),
        lax.all_gather(biases.astype(jnp.bfloat16), ("dp", "ctx"), axis=0, tiled=True),
    )
    w_project, w_output, w_expand, w_reduce, bias_all = gathered
    hidden_width = w_expand.shape[1]
    scale = HEAD ** (-0.5)
    flat = tokens.reshape(-1, width)
    query_key_value = jnp.dot(flat, w_project, preferred_element_type=jnp.float32).astype(
        jnp.bfloat16
    )
    query_key_value = query_key_value.reshape(slot_dev, seq_dev, 3 * width)
    query = query_key_value[..., :width].reshape(slot_dev, seq_dev, HEADS, HEAD)
    kv_all = lax.all_gather(query_key_value[..., width:], "ctx", axis=0, tiled=True)
    length = kv_all.shape[0]
    keys = kv_all[..., :width].reshape(length, seq_dev, HEADS, HEAD)
    values = kv_all[..., width:].reshape(length, seq_dev, HEADS, HEAD)
    scores = jnp.einsum("qshe,kshe->shqk", query, keys, preferred_element_type=jnp.float32) * scale
    kpos = jnp.arange(length, dtype=jnp.int32)
    allowed = (kpos[None, None, :] <= qpos[None, :, None]) & (
        kpos[None, None, :] < lengths[:, None, None]
    )
    masked = jnp.where(allowed[:, None], scores, -1e30)
    top = jnp.max(masked, axis=-1, keepdims=True)
    expo = jnp.exp(masked - top)
    prob = expo / jnp.sum(expo, axis=-1, keepdims=True)
    prob_low = prob.astype(jnp.bfloat16)
    attended_rows = jnp.einsum(
        "shqk,kshe->qshe", prob_low, values, preferred_element_type=jnp.float32
    )
    attended_rows = attended_rows.astype(jnp.bfloat16).reshape(slot_dev * seq_dev, width)
    branch_output = jnp.dot(attended_rows, w_output, preferred_element_type=jnp.float32)
    residual_stream = flat.astype(jnp.float32) + alphas[0] * branch_output
    resid_low = residual_stream.astype(jnp.bfloat16)
    bias_float = bias_all.astype(jnp.float32)
    before_activation = (
        jnp.dot(resid_low, w_expand, preferred_element_type=jnp.float32) + bias_float[:hidden_width]
    )
    activate = partial(jax.nn.gelu, approximate=False)
    hidden_rows = activate(before_activation).astype(jnp.bfloat16)
    feed_output = (
        jnp.dot(hidden_rows, w_reduce, preferred_element_type=jnp.float32)
        + bias_float[hidden_width:]
    )
    mixed = (residual_stream + alphas[1] * feed_output).astype(jnp.bfloat16).reshape(tokens.shape)
    valid = (qpos[:, None] < lengths[None, :]).astype(jnp.float32).reshape(-1, 1)
    pull = cotangent.reshape(-1, width).astype(jnp.float32) * valid
    d_ffout = (alphas[1] * pull).astype(jnp.bfloat16)
    g_reduce = jnp.dot(hidden_rows.T, d_ffout, preferred_element_type=jnp.float32)
    g_second_bias = jnp.sum(d_ffout.astype(jnp.float32), axis=0)
    d_hidden = jnp.dot(d_ffout, w_reduce.T, preferred_element_type=jnp.float32)
    d_pre = jax.vjp(activate, before_activation)[1](d_hidden)[0].astype(jnp.bfloat16)
    g_expand = jnp.dot(resid_low.T, d_pre, preferred_element_type=jnp.float32)
    g_first_bias = jnp.sum(d_pre.astype(jnp.float32), axis=0)
    d_resid = pull + jnp.dot(d_pre, w_expand.T, preferred_element_type=jnp.float32)
    g_alpha = jnp.stack([jnp.sum(branch_output * d_resid), jnp.sum(feed_output * pull)])
    d_branch = (alphas[0] * d_resid).astype(jnp.bfloat16)
    g_output = jnp.dot(attended_rows.T, d_branch, preferred_element_type=jnp.float32)
    d_att = jnp.dot(d_branch, w_output.T, preferred_element_type=jnp.float32).astype(jnp.bfloat16)
    d_att = d_att.reshape(slot_dev, seq_dev, HEADS, HEAD)
    d_prob = jnp.einsum("qshe,kshe->shqk", d_att, values, preferred_element_type=jnp.float32)
    d_scores = (prob * (d_prob - jnp.sum(prob * d_prob, axis=-1, keepdims=True))).astype(
        jnp.bfloat16
    )
    d_query = (
        jnp.einsum("shqk,kshe->qshe", d_scores, keys, preferred_element_type=jnp.float32) * scale
    )
    count = lax.axis_size("ctx") * slot_dev
    g_keys = (
        jnp.einsum("shqk,qshe->kshe", d_scores, query, preferred_element_type=jnp.float32) * scale
    )
    g_values = jnp.einsum("shqk,qshe->kshe", prob_low, d_att, preferred_element_type=jnp.float32)
    d_kv = lax.psum_scatter(
        jnp.concatenate(
            [g_keys.reshape(count, seq_dev, width), g_values.reshape(count, seq_dev, width)],
            axis=-1,
        ).astype(jnp.bfloat16),
        "ctx",
        scatter_dimension=0,
        tiled=True,
    ).astype(jnp.float32)
    d_qkv = jnp.concatenate([d_query.reshape(slot_dev, seq_dev, width), d_kv], axis=-1)
    d_qkv = d_qkv.astype(jnp.bfloat16).reshape(-1, 3 * width)
    g_project = jnp.dot(flat.T, d_qkv, preferred_element_type=jnp.float32)
    input_grad = (
        d_resid + jnp.dot(d_qkv, w_project.T, preferred_element_type=jnp.float32)
    ).reshape(tokens.shape)
    g_bias = jnp.concatenate([g_first_bias, g_second_bias])
    devices = lax.axis_size(("dp", "ctx"))
    device_index = lax.axis_index(("dp", "ctx"))
    summed = lax.psum((g_project, g_output, g_expand, g_reduce, g_bias, g_alpha), ("dp", "ctx"))
    squares = jnp.float32(0.0)
    for grad in summed:
        squares = squares + jnp.sum(grad * grad)
    owned = []
    for grad in summed[:5]:
        rows = grad.shape[0] // devices
        owned.append(lax.dynamic_slice_in_dim(grad, device_index * rows, rows, 0))
    alpha_sum = summed[5]
    grad_norm = jnp.sqrt(squares)
    factor = jnp.minimum(1.0, clip_bound / (grad_norm + 1e-06))
    weights = (project_matrix, output_matrix, expand_matrix, reduce_matrix, biases, alphas)
    states = (
        (project_first, project_second),
        (output_first, output_second),
        (expand_first, expand_second),
        (reduce_first, reduce_second),
        (bias_first, bias_second),
        (alpha_first, alpha_second),
    )
    grads = (owned[0], owned[1], owned[2], owned[3], owned[4], alpha_sum)
    rates = (matrix_rate, matrix_rate, matrix_rate, matrix_rate, matrix_rate, alpha_rate)
    decays = (decay_rate, decay_rate, decay_rate, decay_rate, 0.0, 0.0)
    results = []
    for weight, (first, second), grad, rate, decay in zip(weights, states, grads, rates, decays):
        results.extend(adamw(weight, first, second, factor * grad, rate, decay))
    return (
        mixed,
        input_grad,
        results[0],
        results[1],
        results[2],
        results[3],
        results[4],
        results[5],
        results[6],
        results[7],
        results[8],
        results[9],
        results[10],
        results[11],
        results[12],
        results[13],
        results[14],
        results[15],
        results[16],
        results[17],
        grad_norm,
    )


def cost(us):
    return pl.CostEstimate(flops=int(us * 1.1e9), transcendentals=0, bytes_accessed=1 << 20)


def params():
    return pltpu.CompilerParams(vmem_limit_bytes=VMEM_LIMIT)


def call(kernel, name, us, grid, in_specs, out_specs, out_shape, scratch, *args, aliases={}, limit=24):
    return pl.pallas_call(
        kernel,
        grid_spec=pltpu.PrefetchScalarGridSpec(
            num_scalar_prefetch=1,
            grid=grid,
            in_specs=in_specs,
            out_specs=out_specs,
            scratch_shapes=scratch,
        ),
        out_shape=out_shape,
        input_output_aliases=aliases,
        compiler_params=pltpu.CompilerParams(vmem_limit_bytes=limit << 20),
        cost_estimate=cost(us),
        name=name,
    )(*args)


def shape(dims, kind):
    return jax.ShapeDtypeStruct(dims, kind)


def token_block(rows, width, f):
    return pl.BlockSpec((1, rows, width), lambda *a: (f(*a), 0, 0))


VMEM = pl.BlockSpec(memory_space=pltpu.VMEM)


def call_once(kernel, name, us, limit, in_specs, out_specs, out_shape, scratch, *args):
    return pl.pallas_call(
        kernel,
        in_specs=in_specs,
        out_specs=out_specs,
        out_shape=out_shape,
        scratch_shapes=scratch,
        compiler_params=pltpu.CompilerParams(vmem_limit_bytes=limit << 20),
        cost_estimate=cost(us),
        name=name,
    )(*args)


def forward_call(seqs, nz, info, x6, got, x6_o, got_o, *weight_in):
    rows, width = x6.shape[1:]
    wide, slots = width // 2, 4 * rows
    n = len(seqs)
    outs = [shape((width, 3 * wide), BF16)] if 0 in seqs else []
    outs += [
        shape((n, slots, 3 * wide), BF16),
        shape((n, 2, rows, wide), BF16),
        shape((n, 2, rows, wide), BF16),
        shape((n, 8, slots), F32),
    ]
    return call_once(
        partial(attend_forward, seqs, nz), "attend_forward", 2 * n, 58,
        [SMEM] + [ANY] * 4 + ([VMEM] * PIECES if 0 in seqs else [ANY]), [ANY] * len(outs), outs,
        [
            pltpu.VMEM((n, 8, slots), F32),
            pltpu.VMEM((n, 4, rows, width), BF16),
            pltpu.VMEM((n, slots, 3 * wide), BF16),
            pltpu.VMEM((n, 2, 2, rows, wide), BF16),
            pltpu.VMEM((slots, wide), BF16),
            pltpu.VMEM((slots, 128), F32),
            pltpu.VMEM((width, 3 * wide), BF16),
            pltpu.SemaphoreType.DMA((n, 10)),
        ],
        info, x6, got, x6_o, got_o, *weight_in)


def backward_call(s, last, info, x6, got, x6_o, got_o, *ins):
    rows, width = x6.shape[1:]
    wide, slots = width // 2, 4 * rows
    r1 = width // 32
    grad_in = len(ins) > 7
    g_out = [shape((width, 3 * wide), F32)]
    if last:
        nz = 4
        halves = (2, 2, nz, 2 * r1, 3 * wide // 2)
        g_out = [shape(halves, F32), shape(halves, BF16)]
    outs = g_out + [shape((1, 2, rows, width), BF16)] * 2
    return call_once(
        partial(attend_backward, s, grad_in, last), "attend_backward", 1, 32 if grad_in else 58,
        [SMEM] + [ANY] * (4 + len(ins)), [ANY] * len(outs), outs,
        ([pltpu.VMEM(v.shape, v.dtype) for v in g_out] if last else []) + [
            pltpu.VMEM((slots, wide), BF16),
            pltpu.VMEM((8, slots), F32),
            pltpu.VMEM((slots, wide), BF16),
            pltpu.VMEM((slots, wide), F32),
            pltpu.VMEM((slots, wide), F32),
            pltpu.VMEM((4, rows, width), BF16),
            pltpu.VMEM((width, 3 * wide), BF16),
            pltpu.VMEM((1, slots, 3 * wide), BF16),
            pltpu.VMEM((1, 8, slots), F32),
            pltpu.VMEM((2, 2, rows, wide), BF16),
            pltpu.VMEM((2, 2, rows, wide), BF16),
            pltpu.VMEM((width, 3 * wide), F32),
            pltpu.VMEM((2, rows, width), BF16),
            pltpu.VMEM((2, rows, width), BF16),
            pltpu.SemaphoreType.DMA((19,)),
        ],
        info, x6, got, x6_o, got_o, *ins)


def feed_call(info, alphas, x6, got, c6, c_got, *rest):
    seqs, rows, width = got.shape
    wide = width // 2
    rails = rest[4:]
    nz, blob_rows = rails[0].shape[:2]
    devices = nz * 8
    r1 = width // devices
    hidden = ((blob_rows - 16) // r1 - 1) // 2 * width
    act = pl.BlockSpec((1, 2, rows, wide), lambda t, i: (t, 0, 0, 0))
    pair = pl.BlockSpec((1, 2, rows, width), lambda t, i: (t, 0, 0, 0))
    by_seq = token_block(rows, width, lambda t, i: t)
    by_own = token_block(rows, width, lambda t, i: i[OWN + t])
    outs = [
        shape((seqs, rows, width), BF16),
        shape((seqs, rows, width), BF16),
        shape((seqs, 2, rows, width), F32),
        shape((seqs, 2, rows, wide), BF16),
        shape((seqs, 2, rows, wide), BF16),
        shape((2, 2, 2, nz, blob_rows // 2, width), BF16),
        shape((2, 2, 2, nz, blob_rows // 2, width), BF16),
        shape((8, width), F32),
    ]
    return call(
        partial(feed, nz), "feed", 35, (seqs,),
        [SMEM, by_own, by_seq, by_own, by_seq] + [whole(v.shape) for v in rest],
        [by_seq, by_seq, pair, act, act] + [whole(v.shape) for v in outs[5:]],
        outs,
        [
            pltpu.VMEM((width, width), BF16),
            pltpu.VMEM((width, hidden), BF16),
            pltpu.VMEM((hidden, width), BF16),
            pltpu.VMEM((16, width), F32),
            pltpu.VMEM((width, width), F32),
            pltpu.VMEM((width, hidden), F32),
            pltpu.VMEM((hidden, width), F32),
            pltpu.VMEM((8, hidden), F32),
            pltpu.VMEM((8, width), F32),
            pltpu.VMEM((16, width), F32),
            pltpu.VMEM((2 * rows, hidden), BF16),
            pltpu.VMEM((2 * rows, hidden), F32),
            pltpu.VMEM((2 * rows, width), BF16),
            pltpu.VMEM((2 * rows, width), F32),
            pltpu.VMEM((2 * rows, width), F32),
            pltpu.VMEM((2, 2 * rows, wide), BF16),
        ],
        info, alphas, x6, got, c6, c_got, *rest, limit=VMEM_LIMIT >> 20)


def fast_body(
    tokens,
    cotangent,
    lengths,
    project_matrix,
    output_matrix,
    expand_matrix,
    reduce_matrix,
    biases,
    alphas,
    project_first,
    project_second,
    output_first,
    output_second,
    expand_first,
    expand_second,
    reduce_first,
    reduce_second,
    bias_first,
    bias_second,
    alpha_first,
    alpha_second,
):
    rows, seq_dev, width = tokens.shape
    hidden = expand_matrix.shape[1]
    devices = lax.axis_size(BOTH)
    nz = devices // 8
    seqs = seq_dev // 2
    slots = 4 * rows
    wide = width // 2
    table = routes(nz)

    def move(v, way):
        return lax.ppermute(v, BOTH, table[way])

    def after(v, *deps):
        return lax.optimization_barrier((v,) + deps)[0]

    def at(v, axis, index):
        return lax.dynamic_index_in_dim(v, index, axis, False)

    def add(a, b):
        return a.astype(F32) + b.astype(F32)

    ctx, dp = lax.axis_index("ctx"), lax.axis_index("dp")
    y, c, z, x = ctx // 2, ctx % 2, dp // 2, dp % 2
    me = dp * 4 + ctx

    x6 = jnp.transpose(tokens, (1, 0, 2))
    c6 = jnp.transpose(cotangent, (1, 0, 2))
    place = jnp.stack([c, y, z, x]).astype(jnp.int32)
    vmem = pl.BlockSpec(memory_space=pltpu.VMEM)
    info, wq_own, wq_give, x_give = pl.pallas_call(
        prepare,
        in_specs=[SMEM, SMEM, vmem, ANY],
        out_specs=[SMEM, vmem, vmem, vmem],
        out_shape=[
            shape((INFO,), jnp.int32),
            shape((project_matrix.shape[0], 3 * wide), BF16),
            shape((project_matrix.shape[0], 3 * wide), BF16),
            shape((seqs, rows, width), BF16),
        ],
        scratch_shapes=[pltpu.SemaphoreType.DMA((seqs,))],
        compiler_params=params(),
        cost_estimate=cost(2),
        name="prepare",
    )(place, lengths, project_matrix, x6)
    got = move(x_give, "y")
    wq_got = move(wq_give, "core")
    wq_chip = jnp.where(
        c == 0, jnp.concatenate([wq_own, wq_got], 0), jnp.concatenate([wq_got, wq_own], 0)
    )
    r1, r2 = output_matrix.shape[0], reduce_matrix.shape[0]
    groups = hidden // width
    blob_rows = (1 + groups) * r1 + r2 + 16
    bias_rows = jnp.zeros((16 * width,), BF16)
    bias_rows = lax.dynamic_update_slice_in_dim(
        bias_rows, biases.astype(BF16), me * biases.shape[0], 0
    ).reshape(16, width)
    blob = pl.pallas_call(
        pack,
        in_specs=[vmem] * 4,
        out_specs=vmem,
        out_shape=shape((blob_rows, width), BF16),
        compiler_params=params(),
        cost_estimate=cost(1),
        name="pack",
    )(output_matrix, expand_matrix, reduce_matrix, after(bias_rows, wq_give))
    bz1 = move(blob, 1)
    x6_o = move(after(x6, wq_chip), "core")
    c_give = call(
        give, "give", 1, (seqs,), [token_block(rows, width, lambda t, i: i[OTHER + t])],
        token_block(rows, width, lambda t, i: t), shape((seqs, rows, width), BF16),
        [], after(info, blob), c6)
    wz = [move(wq_chip, r) for r in range(1, nz)]
    wa = jnp.stack([wq_chip] + wz)
    bz01 = jnp.stack([blob, bz1])
    bz23 = move(after(bz01, *wz), 2)
    wax, way, wad = move(after(wa, got, c_give), "x"), move(wa, "y"), move(wa, "xy")
    ba = jnp.concatenate([bz01, after(bz23, wax, way, wad)], 0)
    got_o = move(after(got, ba, wa), "core")
    bax, bay = move(ba, "x"), move(ba, "y")

    xs4 = (x6, got, x6_o, got_o)
    wq_full, *first = forward_call((0,), nz, after(info, ba, c_give), *xs4, wa, wax, way, wad)
    lse = first[3]
    bad = move(after(bay, lse), "x")
    c_got = move(after(c_give, bay, lse), "y")
    ba_o, bax_o, bay_o = (move(after(v, lse), "core") for v in (ba, bax, bay))
    o_first = move(first[2], "core")
    others = forward_call(tuple(range(1, seqs)), nz, after(info, bax, bay), *xs4, wq_full)
    o_others = move(after(others[2], c_got, ba_o, bax_o, bay_o, o_first), "core")
    kept = [first] + [others] * (seqs - 1)
    rail = (ba, bax, bay, bad)
    rail_o = (ba_o, bax_o, bay_o, move(after(bad, o_others), "core"))

    own_o = (first[1], others[1])
    oth_o = (o_first, o_others)
    mixed_m, mixed_g, dy, do_keep, do_send, g_send, g_keep, ga = feed_call(
        info, alphas, x6, got, c6, c_got, *own_o, *oth_o, *rail, *rail_o
    )

    do_recv = move(do_send, "core")
    g_recv = move(after(g_send, do_recv), "core")

    def backward(s, last, grad, *deps):
        qkv, ok, osend, lse = kept[s]
        ins = (wq_full, qkv, lse, ok, osend, do_keep, do_recv) + (() if grad is None else (grad,))
        return backward_call(s, last, after(info, *deps) if deps else info, *xs4, *ins)

    keeps, sends, recvs = [None] * seqs, [None] * seqs, [None] * seqs
    grad, keeps[2], sends[2] = backward(2, False, None)
    g_recv_late = after(g_recv, sends[2])
    ga_send = add(g_keep[0, 1], g_recv_late[0, 1]).astype(BF16)
    gb_send = add(g_keep[1, 1], g_recv_late[1, 1]).astype(BF16)
    ra, rb = move(ga_send, "x"), move(gb_send, "y")
    recvs[2] = move(sends[2], "core")
    mixed_r = move(mixed_g, "y")
    grad, keeps[0], sends[0] = backward(0, False, grad, ga_send, gb_send, mixed_r)
    ra, rb = after(ra, sends[0]), after(rb, sends[0])
    fa = g_keep[0, 0], g_recv[0, 0], ra
    fb = g_keep[1, 0], g_recv[1, 0], rb

    def part(three, index):
        return sum(v[index].astype(F32) for v in three)

    ga_send, gb_send = part(fa, 1).astype(BF16), part(fb, 1).astype(BF16)
    ra, rb = move(ga_send, "y"), move(gb_send, "x")
    recvs[0] = after(move(sends[0], "core"), ga_send, gb_send)
    recvs[2] = after(recvs[2], ga_send, gb_send)

    def got_grad(s):
        return (dy[s : s + 1, 1] + add(keeps[s][:, 1], recvs[s][:, 1])).astype(BF16)

    back_early = jnp.concatenate([got_grad(2), got_grad(0)], 0)
    qkeep, qsend, keeps[1], sends[1] = backward(1, True, grad, ga_send, gb_send, back_early)
    back_early = move(back_early, "y")
    ra, rb = after(ra, sends[1]), after(rb, sends[1])
    qx, qy = move(after(qsend[0], ra, rb), "x"), move(after(qsend[1], ra, rb), "y")
    recvs[1] = move(sends[1], "core")
    fv = jnp.concatenate([add(part(fa, 0), ra), add(part(fb, 0), rb)], 1).astype(BF16)
    fgot = [move(fv[r], r) for r in range(1, nz)]
    half = pl.BlockSpec((1, 1, rows, width), lambda *_: (0, 0, 0, 0))
    six = (seq_dev, rows, width)
    mixed6 = call(
        placed, "placed", 1, (1,), [whole(mixed_m.shape)] * 2, whole(six), shape(six, BF16), [],
        after(info, fv, back_early), mixed_m, mixed_r)
    qx_send, qy_send = add(qkeep[0, 1], qx[1]).astype(BF16), add(qkeep[1, 1], qy[1]).astype(BF16)
    qx2, qy2 = move(after(qx_send, qy_send, mixed6), "y"), move(after(qy_send, qx_send, mixed6), "x")
    back_late = move(after(got_grad(1), qx2, qy2), "y")
    input6 = call(
        placed_own, "placed_own", 1, (seqs,),
        [pl.BlockSpec((1, 1, rows, width), lambda t, i: (t, 0, 0, 0))] + [half] * 6,
        token_block(rows, width, lambda t, i: i[OWN + t]), shape(six, F32), [],
        after(info, qx_send, qy_send), dy, *keeps, *recvs)
    gq = jnp.concatenate(
        [add(qkeep[0, 0], qx[0]) + qx2.astype(F32), add(qkeep[1, 0], qy[0]) + qy2.astype(F32)], 2
    )
    gq = after(gq, input6)
    qgot = [move(gq[r].astype(BF16), r) for r in range(1, nz)]
    input6 = call(
        placed_rest, "placed_rest", 1, (1,), [whole(back_early.shape), whole(back_late.shape), ANY], ANY,
        shape(six, F32), [pltpu.VMEM((seqs, rows, width), F32), pltpu.SemaphoreType.DMA((seqs,))],
        info, back_early, back_late, input6, aliases={3: 0})
    fin_in = (gq, *qgot, fv, *fgot, ga)
    one = lambda v: whole((1,) + v.shape[1:])
    fin_out = [shape((r1, 3 * wide), F32)] * 2 + [shape((devices, 128), F32), shape((blob_rows, width), F32)]
    q_own, q_give, tiny, blob_sum = call(
        finish, "finish", 1, (1,),
        [one(gq)] + [whole(v.shape) for v in qgot] + [one(fv)] + [whole(v.shape) for v in fgot + [ga]],
        [whole(v.shape) for v in fin_out], fin_out,
        [], info, *fin_in)
    tiny = lax.all_to_all(tiny.reshape(devices, 1, 128), BOTH, 0, 0).reshape(devices, 128)
    q_got = move(q_give, "core")

    g_bias = lax.dynamic_slice_in_dim(
        blob_sum[blob_rows - 16 :].reshape(-1), me * biases.shape[0], biases.shape[0], 0
    )
    states = (
        project_matrix, project_first, project_second,
        output_matrix, output_first, output_second,
        expand_matrix, expand_first, expand_second,
        reduce_matrix, reduce_first, reduce_second,
        biases[None], bias_first[None], bias_second[None],
        alphas[None], alpha_first[None], alpha_second[None],
    )
    outs = [shape(v.shape, F32) for v in states] + [shape((1, 1), F32)]
    ins = (tiny, q_own, q_got, blob_sum, g_bias[None], *states)
    res = call(
        update, "update", 3, (1,), [whole(v.shape) for v in ins], [whole(v.shape) for v in outs], outs, [],
        after(info, input6), *ins)
    mixed = jnp.transpose(mixed6, (1, 0, 2))
    input_grad = jnp.transpose(input6, (1, 0, 2))
    results = list(res[:12]) + [v[0] for v in res[12:18]]
    return (mixed, input_grad, *results, res[18][0, 0])


def solution(mesh):
    ctx, dp = mesh.shape["ctx"], mesh.shape["dp"]
    row = P(BOTH, None)
    flat = P(BOTH)
    token = P("ctx", "dp", None)
    body = fast_body if (ctx == 4 and dp == 8) else generic_body
    return jax.shard_map(
        body,
        mesh=mesh,
        in_specs=(token, token, P("dp"), row, row, row, row, flat, P())
        + (row,) * 8
        + (flat, flat, P(), P()),
        out_specs=(token, token) + (row,) * 12 + (flat,) * 3 + (P(),) * 4,
        check_vma=False,
    )
```
